256 devices in a mesh: blk: 128 (over x, z_lo, y, core), row: 2 (over z_hi).
Axes of the slice: x: 4, y: 4, z: 8 (z_hi: 2, z_lo: 4; z = z_hi * 4 + z_lo), core: 2. Of those that a mesh axis runs over, the one named last changes fastest.
Arguments:
- row_feats: bfloat16 [3072, 2048], P('row'), may hold values from -9 to 9
- col_feats: bfloat16 [65536, 2048], P('blk'), may hold values from -9 to 9
- offsets: int32 [3, 4], replicated, may hold values from 0 to 255
Outputs:
- energy: float32 [2, 3072, 32768], P(None, 'row', 'blk')
- norms: float32 [3, 2, 32768], P(None, None, 'blk')
The draws below stay inside these ranges and needn't reach their ends.
All inputs are finite; a program needn't handle non-finite values.
Results may differ from the reference program's by a relative error of at most 0.0003.
Values sent between devices are 32-bit elements; how exact they have to be, the bound alone decides.
No kernel may reach another device: no remote copies, remote signals or barrier semaphores. Data moves between devices by JAX's collectives and lax.ppermute only.
A program may use at most 64 MiB of HBM per device.

```python
import math
import jax
import jax.numpy as jnp
from jax import lax

F = 2048
B = 256
ROUNDS = 3
INNER = 4
NPOS = 128
COLS = 65536
ROWS = 3072


def shared_signs(key):
    count = min(64, F // 2)
    signs = 2.0 * jax.random.bernoulli(key, 0.5, (count,)).astype(jnp.float32) - 1.0
    return jnp.concatenate([signs, jnp.zeros((F - count,), jnp.float32)])


def base_noise(key, shape):
    return jnp.clip(jax.random.normal(key, shape, jnp.float32), -6.0, 6.0)


def draw_row_feats(key, part):
    signs = shared_signs(key)
    key = jax.random.fold_in(key, 11)
    count = min(64, F // 2)
    amplitude = math.sqrt(3.2 * math.sqrt(F) / count)
    noise = base_noise(key, (ROWS, F))
    place = (jnp.arange(ROWS, dtype=jnp.float32) + 0.5) / ROWS
    phase = jnp.cos(math.pi * place)
    values = noise + amplitude * phase[:, None] * signs[None, :]
    return values.astype(jnp.bfloat16)


def draw_col_feats(key, part):
    signs = shared_signs(key)
    key = jax.random.fold_in(key, 23)
    noise_key, phase_key = jax.random.split(key)
    count = min(64, F // 2)
    amplitude = math.sqrt(3.2 * math.sqrt(F) / count)
    noise = base_noise(noise_key, (COLS, F))
    phase = jax.random.uniform(phase_key, (COLS,), jnp.float32, -1.0, 1.0)
    values = noise + amplitude * phase[:, None] * signs[None, :]
    return values.astype(jnp.bfloat16)


def place_ends(entries, own_key, smallest, high):
    longest = entries.shape.index(max(entries.shape))
    spots = []
    for shift in (0, 1):
        where = [jax.random.randint(jax.random.fold_in(own_key, axis), (), 0, length) for axis, length in enumerate(entries.shape)]
        where[longest] = (where[longest] + shift) % entries.shape[longest]
        spots.append(tuple(where))
    return entries.at[spots[0]].set(smallest).at[spots[1]].set(high)


def setup_inputs(seed: int = 0) -> dict:
    splits = jax.random.split(jax.random.key(seed), 4)
    return {
        "row_feats": draw_row_feats(jax.random.fold_in(splits[3], 71), 0),
        "col_feats": draw_col_feats(jax.random.fold_in(splits[3], 71), 0),
        "offsets": place_ends(jax.random.randint(splits[2], (ROUNDS, INNER), 0, B), jax.random.fold_in(splits[2], 1), 0, B - 1).astype(jnp.int32),
    }


def rotation_terms(gram):
    upper_sq, lower_sq, mixed = (gram[0], gram[1], gram[2])
    theta = 0.5 * jnp.arctan2(2.0 * mixed, upper_sq - lower_sq)
    cosine = jnp.cos(theta)
    sine_part = jnp.sin(theta)
    cross_term = 2.0 * cosine * sine_part * mixed
    new_upper = cosine * cosine * upper_sq + cross_term + sine_part * sine_part * lower_sq
    new_lower = sine_part * sine_part * upper_sq - cross_term + cosine * cosine * lower_sq
    return (cosine, sine_part, new_upper, new_lower)

def reference(row_feats, col_feats, offsets):
    rows_wide = row_feats.astype(jnp.float32)
    cols_wide = col_feats.astype(jnp.float32)
    row_norm = lax.optimization_barrier(jnp.sum(rows_wide * rows_wide, axis=1))
    col_norm = lax.optimization_barrier(jnp.sum(cols_wide * cols_wide, axis=1))
    cross = jnp.dot(row_feats, col_feats.T, preferred_element_type=jnp.float32)
    kernel = jnp.exp(-(0.25 / math.sqrt(F)) * (row_norm[:, None] + col_norm[None, :] - 2.0 * cross - 2.0 * F))
    blocks = kernel.reshape(ROWS, NPOS, 2, B)
    upper = jnp.transpose(blocks[:, :, 0, :], (1, 0, 2))
    lower = jnp.transpose(blocks[:, :, 1, :], (1, 0, 2))
    records = []
    for round_index in range(ROUNDS):
        for inner_index in range(INNER):
            offset = offsets[round_index, inner_index]
            lower_view = jnp.roll(lower, -offset, axis=2)
            gram = jnp.stack([lax.optimization_barrier(jnp.sum(upper * upper, axis=1)), lax.optimization_barrier(jnp.sum(lower_view * lower_view, axis=1)), lax.optimization_barrier(jnp.sum(upper * lower_view, axis=1))])
            cosine, sine_part, unused_a, unused_b = rotation_terms(gram)
            cosine = cosine[:, None, :]
            sine_part = sine_part[:, None, :]
            upper, lower_view = (cosine * upper + sine_part * lower_view, cosine * lower_view - sine_part * upper)
            lower = jnp.roll(lower_view, offset, axis=2)
        upper_mean = lax.optimization_barrier(jnp.sum(upper * upper, axis=1)).reshape(NPOS * B) / ROWS
        lower_mean = lax.optimization_barrier(jnp.sum(lower * lower, axis=1)).reshape(NPOS * B) / ROWS
        records.append(jnp.stack([upper_mean, lower_mean]))
        new_upper = jnp.concatenate([upper[:1], lower[:1], upper[1:-1]], axis=0)
        new_lower = jnp.concatenate([lower[1:], upper[-1:]], axis=0)
        upper, lower = (new_upper, new_lower)
    upper_flat = jnp.transpose(upper, (1, 0, 2)).reshape(ROWS, NPOS * B)
    lower_flat = jnp.transpose(lower, (1, 0, 2)).reshape(ROWS, NPOS * B)
    energy = jnp.stack([upper_flat * upper_flat, lower_flat * lower_flat])
    return (energy, jnp.stack(records))
```

```python
import functools
import math

import jax
import jax.numpy as jnp
from jax import lax
from jax.experimental import pallas as pl
from jax.experimental.pallas import tpu as pltpu
from jax.sharding import PartitionSpec as P

F32 = jnp.float32
BF16 = jnp.bfloat16
W = 256
LAGS = 96
VMEM_LIMIT = 48 * 1024 * 1024


def group_rows(m):
    return (16 * m, 16) if m < 4 else (64 + 8 * (m - 4), 8)


def lag_targets(o):
    t, s = [0], [0]
    first, second = [0], [1]
    rows = {}
    for step in range(4):
        count = 1 << step
        for m in range(count):
            start, _ = group_rows(m)
            place = {3: 0, 2: 8, 1: 12, 0: 14}[step]
            for n in range(count):
                lag = (o[step] + s[n] - t[m]) & (W - 1)
                rows[start + place + n] = lag + W * second[n]
        if step < 3:
            t, s = t + [x + o[step] for x in s], s + [x - o[step] for x in t]
            first, second = first + second, second + first
    rows[15] = 0
    rows[16 + 14] = W
    return rows, t, first


def split(x):
    hi = x.astype(BF16)
    return hi, (x - hi.astype(F32)).astype(BF16)


TN = (((0,), (0,)), ((), ()))
NT = (((1,), (1,)), ((), ()))


def skew(x):
    row = lax.broadcasted_iota(jnp.int32, (W, W), 0)
    for bit in (1, 2, 4):
        x = jnp.where((row & bit) != 0, pltpu.roll(x, W - bit, 1), x)
    tiles = [pltpu.roll(x[8 * t : 8 * t + 8], (W - 8 * t) % W, 1) for t in range(W // 8)]
    return jnp.concatenate(tiles, axis=0)


def build_onehot(o, table_ref):
    rows, bases, first = lag_targets(o)
    table_ref[...] = jnp.full((LAGS, 128), -1, jnp.int32)
    for r, target in rows.items():
        table_ref[r : r + 1, :] = jnp.full((1, 128), target, jnp.int32)
    return bases, first


def lag_products(gram_ref, o, table_ref, out_ref):
    bases, first = build_onehot(o, table_ref)
    table = table_ref[...]
    table = jnp.concatenate([table] * 4, axis=1)
    onehot = (table == lax.broadcasted_iota(jnp.int32, (LAGS, 2 * W), 1)).astype(F32).astype(BF16)
    diags = {}
    for kind in (0, 1):
        sheets = []
        for side in (0, 1):
            block = gram_ref[kind * W : (kind + 1) * W, side * W : (side + 1) * W]
            sheets.append(skew(block))
        sheet = jnp.concatenate(sheets, axis=1)
        hi, lo = split(sheet)
        lowest = (sheet - hi.astype(F32) - lo.astype(F32)).astype(BF16)
        total = None
        for part in (lowest, lo, hi):
            term = lax.dot_general(onehot, part, NT, preferred_element_type=F32)
            total = term if total is None else total + term
        diags[kind] = total
    for m in range(8):
        start, count = group_rows(m)
        tile = diags[first[m]][start : start + count]
        base = bases[m]
        if m > 0:
            tile = pltpu.roll(tile, (-base) & (W - 1), 1)
        out_ref[start : start + count, :] = tile


def gram_step(a, b, gram_ref):
    both = jnp.concatenate([a, b], axis=1)
    hi, lo = split(both)
    g = lax.dot_general(hi, lo, TN, preferred_element_type=F32)
    g += lax.dot_general(lo, hi, TN, preferred_element_type=F32)
    g += lax.dot_general(hi, hi, TN, preferred_element_type=F32)
    gram_ref[...] += g


def angle(g, upper_sq, lower_sq):
    twice = 2.0 * g
    diff = upper_sq - lower_sq
    scale = jnp.maximum(jnp.abs(twice), jnp.abs(diff))
    live = scale > 0.0
    safe = jnp.where(live, scale, 1.0)
    x = jnp.where(live, diff / safe, 1.0)
    y = jnp.where(live, twice / safe, 0.0)
    r = jnp.sqrt(x * x + y * y)
    big = jnp.sqrt(0.5 * (1.0 + jnp.abs(x) / r))
    small = 0.5 * jnp.abs(y) / (r * big)
    wide = x < 0.0
    c = jnp.where(wide, small, big)
    s = jnp.where(wide, big, small)
    s = jnp.where(y < 0.0, -s, s)
    cross = twice * c * s
    return c, s, c * c * upper_sq + cross + s * s * lower_sq, s * s * upper_sq - cross + c * c * lower_sq


def angles(lags, o, coef_ref):
    row = lax.broadcasted_iota(jnp.int32, (8, W), 0)
    a = jnp.ones((8, W), F32)
    b = jnp.ones((8, W), F32)
    upper_sq = lags[15:16]
    lower_sq = lags[30:31]
    tiles = [lags[16 * m + 8 : 16 * m + 16] for m in range(4)]
    last = [lags[group_rows(m)[0] : group_rows(m)[0] + 8] for m in range(8)]
    for step in range(4):
        count = 1 << step
        if step == 3:
            parts, place = last, 0
        else:
            parts, place = tiles[:count], (6, 4, 0)[step]
        acc = None
        for m in range(count):
            term = a[m : m + 1] * parts[m]
            acc = term if acc is None else acc + term
        view = pltpu.roll(b, place, 0) if place else b
        acc = jnp.where((row >= place) & (row < place + count), acc * view, 0.0)
        g = jnp.sum(acc, axis=0, keepdims=True)
        c, s, upper_sq, lower_sq = angle(g, upper_sq, lower_sq)
        coef_ref[step : step + 1, :] = c
        coef_ref[4 + step : 5 + step, :] = s
        if step < 3:
            shift_a, shift_b = pltpu.roll(a, count, 0), pltpu.roll(b, count, 0)
            a, b = jnp.where(row < count, c * a, s * shift_b), jnp.where(row < count, c * b, -s * shift_a)
            turn = (o[step] - o[step + 1]) & (W - 1)
            b = pltpu.roll(b, turn, 1)
            lower_sq = pltpu.roll(jnp.broadcast_to(lower_sq, (8, W)), turn, 1)[0:1]
    coef_ref[8:9, :] = upper_sq
    coef_ref[9:10, :] = pltpu.roll(jnp.broadcast_to(lower_sq, (8, W)), o[3] & (W - 1), 1)[0:1]


def rotate(upper, lower, coef, o):
    lower = pltpu.roll(lower, (-o[0]) & (W - 1), 1)
    for step in range(4):
        c, s = coef[step : step + 1], coef[4 + step : 5 + step]
        upper, lower = c * upper + s * lower, c * lower - s * upper
        turn = (o[step] - o[step + 1]) if step < 3 else o[3]
        lower = pltpu.roll(lower, turn & (W - 1), 1)
    return upper, lower


def spec_rows(r):
    return pl.BlockSpec((r, W), lambda i: (i, 0))


def spec_whole(shape):
    return pl.BlockSpec(shape, lambda i: (0,) * len(shape))


SMEM = pl.BlockSpec(memory_space=pltpu.SMEM)


def tile_rows(rows, most=512):
    r = most
    while rows % r:
        r //= 2
    return r


def block(rows):
    return jax.ShapeDtypeStruct((rows, W), F32)


LAG_SHAPE = jax.ShapeDtypeStruct((LAGS, W), F32)
COEF_SHAPE = jax.ShapeDtypeStruct((16, W), F32)
GRAM_SCRATCH = [pltpu.VMEM((2 * W, 2 * W), F32), pltpu.VMEM((LAGS, 128), jnp.int32)]


def call(kernel, name, grid, in_specs, out_specs, out_shape, scratch=(), flops=0, moved=0):
    return pl.pallas_call(
        kernel,
        name=name,
        grid=(grid,),
        in_specs=in_specs,
        out_specs=out_specs,
        out_shape=out_shape,
        scratch_shapes=list(scratch),
        compiler_params=pltpu.CompilerParams(vmem_limit_bytes=VMEM_LIMIT),
        cost_estimate=pl.CostEstimate(flops=flops, bytes_accessed=moved, transcendentals=0),
    )


def offsets_of(o_ref, round_index):
    return [o_ref[round_index, j] for j in range(4)]


def pick(flag, a, b):
    return jnp.where(flag, a, b), jnp.where(flag, b, a)


def first_kernel(o_ref, rows_ref, cols_ref, upper_ref, lower_ref, lag_ref, gram_ref, table_ref, norm_ref):
    i = pl.program_id(0)
    count, feat = cols_ref.shape

    @pl.when(i == 0)
    def _():
        gram_ref[...] = jnp.zeros_like(gram_ref)
        ones = jnp.ones((8, feat), BF16)
        for k in range(0, count, 128):
            wide = cols_ref[k : k + 128].astype(F32)
            hi, lo = split(wide * wide)
            norm_ref[:, k : k + 128] = lax.dot_general(
                ones, lo, NT, preferred_element_type=F32
            ) + lax.dot_general(ones, hi, NT, preferred_element_type=F32)

    rows = rows_ref[...]
    wide = rows.astype(F32)
    row_norm = jnp.sum(wide * wide, axis=1, keepdims=True)
    cross = lax.dot_general(rows, cols_ref[...], NT, preferred_element_type=F32)
    kernel = jnp.exp(
        -(0.25 / math.sqrt(feat)) * (row_norm + norm_ref[0:1] - 2.0 * cross - 2.0 * feat)
    )
    upper, lower = kernel[:, :W], kernel[:, W:]
    upper_ref[...] = upper
    lower_ref[...] = lower
    gram_step(upper, lower, gram_ref)

    @pl.when(i == pl.num_programs(0) - 1)
    def _():
        lag_products(gram_ref, offsets_of(o_ref, 0), table_ref, lag_ref)


def first(offsets, row_feats, col_feats):
    rows, feat = row_feats.shape
    r = tile_rows(rows)
    return call(
        first_kernel,
        "first",
        rows // r,
        [SMEM, pl.BlockSpec((r, feat), lambda i: (i, 0)), spec_whole(col_feats.shape)],
        (spec_rows(r), spec_rows(r), spec_whole((LAGS, W))),
        (block(rows), block(rows), LAG_SHAPE),
        GRAM_SCRATCH + [pltpu.VMEM((8, 2 * W), F32)],
    )(offsets, row_feats, col_feats)


def turn_kernel(round_index, o_ref, p_ref, mine_ref, other_ref, a_ref, b_ref, first_ref, second_ref, coef_ref):
    p = p_ref[0]
    core = p & 1
    o = offsets_of(o_ref, round_index)

    @pl.when(pl.program_id(0) == 0)
    def _():
        angles(mine_ref[...] + other_ref[...], o, coef_ref)

    a, b = a_ref[...], b_ref[...]
    if round_index == 0:
        upper, lower = a, b
        keep = (core == 1) | (p == 0)
    else:
        upper, lower = pick(core == 0, a, b)
        keep = (core == 0) & (p != 0)
    upper, lower = rotate(upper, lower, coef_ref[...], o)
    first_ref[...], second_ref[...] = pick(keep, upper, lower)


def turn(round_index, offsets, p, mine, other, a, b):
    rows = a.shape[0]
    r = tile_rows(rows)
    lag = spec_whole((LAGS, W))
    return call(
        functools.partial(turn_kernel, round_index),
        "turn%d" % round_index,
        rows // r,
        [SMEM, SMEM, lag, lag, spec_rows(r), spec_rows(r)],
        (spec_rows(r), spec_rows(r), spec_whole((16, W))),
        (block(rows), block(rows), COEF_SHAPE),
    )(offsets, p, mine, other, a, b)


def pairs_kernel(o_ref, p_ref, a_ref, b_ref, lag_ref, gram_ref, table_ref):
    i = pl.program_id(0)

    @pl.when(i == 0)
    def _():
        gram_ref[...] = jnp.zeros_like(gram_ref)

    upper, lower = pick((p_ref[0] & 1) == 0, a_ref[...], b_ref[...])
    gram_step(upper, lower, gram_ref)

    @pl.when(i == pl.num_programs(0) - 1)
    def _():
        lag_products(gram_ref, offsets_of(o_ref, 1), table_ref, lag_ref)


def pairs(offsets, p, a, b):
    rows = a.shape[0]
    r = tile_rows(rows)
    return call(
        pairs_kernel,
        "pairs",
        rows // r,
        [SMEM, SMEM, spec_rows(r), spec_rows(r)],
        spec_whole((LAGS, W)),
        LAG_SHAPE,
        GRAM_SCRATCH,
    )(offsets, p, a, b)


def side_kernel(last, o_ref, p_ref, coef_ref, sx_ref, ry_ref, z_ref, q_ref, lag_ref, gram_ref, table_ref):
    i = pl.program_id(0)
    p = p_ref[0]
    core = p & 1

    @pl.when(i == 0)
    def _():
        gram_ref[...] = jnp.zeros_like(gram_ref)

    near_end = (p == 1) | (p == last - 1)
    upper, lower = pick((core == 0) != near_end, sx_ref[...], ry_ref[...])
    upper, lower = rotate(upper, lower, coef_ref[...], offsets_of(o_ref, 1))
    q = jnp.where((core == 1) | (p == last - 1), upper, lower)
    q_ref[...] = q
    upper, lower = pick(core == 0, z_ref[...], q)
    gram_step(upper, lower, gram_ref)

    @pl.when(i == pl.num_programs(0) - 1)
    def _():
        lag_products(gram_ref, offsets_of(o_ref, 2), table_ref, lag_ref)


def side(last, offsets, p, coef, sx, ry, z):
    rows = sx.shape[0]
    r = tile_rows(rows)
    return call(
        functools.partial(side_kernel, last),
        "side",
        rows // r,
        [SMEM, SMEM, spec_whole((16, W))] + [spec_rows(r)] * 3,
        (spec_rows(r), spec_whole((LAGS, W))),
        (block(rows), LAG_SHAPE),
        GRAM_SCRATCH,
    )(offsets, p, coef, sx, ry, z)


def solve_kernel(o_ref, mine_ref, other_ref, coef_ref):
    angles(mine_ref[...] + other_ref[...], offsets_of(o_ref, 2), coef_ref)


def solve(offsets, mine, other):
    lag = spec_whole((LAGS, W))
    return call(solve_kernel, "solve", 1, [SMEM, lag, lag], spec_whole((16, W)), COEF_SHAPE)(offsets, mine, other)


def last_kernel(last, o_ref, p_ref, own_ref, got_ref, z_ref, q_ref, r_ref, v_ref, out_ref):
    p = p_ref[0]
    core = p & 1
    o = offsets_of(o_ref, 2)
    upper, lower = pick(core == 0, z_ref[...], q_ref[...])
    upper, lower = rotate(upper, lower, own_ref[...], o)
    own = jnp.where((core == 1) & (p != 1), upper, lower)
    upper, lower = pick((core == 0) != ((p == 0) | (p == last)), r_ref[...], v_ref[...])
    upper, lower = rotate(upper, lower, got_ref[...], o)
    got = jnp.where((core == 0) | (p == last), upper, lower)
    own, got = own * own, got * got
    out_ref[0], out_ref[1] = pick(core == 0, got, own)


def finish(last, offsets, p, own, got, z, q, r_block, v):
    rows = z.shape[0]
    r = tile_rows(rows)
    coef = spec_whole((16, W))
    return call(
        functools.partial(last_kernel, last),
        "finish",
        rows // r,
        [SMEM, SMEM, coef, coef] + [spec_rows(r)] * 4,
        pl.BlockSpec((2, r, W), lambda i: (0, i, 0)),
        jax.ShapeDtypeStruct((2, rows, W), F32),
    )(offsets, p, own, got, z, q, r_block, v)


def body(row_feats, col_feats, offsets):
    n = lax.axis_size("blk")
    chips = n // 2
    p = lax.axis_index("blk").astype(jnp.int32).reshape(1)
    row_total = row_feats.shape[0] * lax.axis_size("row")
    across = [(0, 1), (1, 0)]
    sibling = [(i, i ^ 1) for i in range(n)]
    meet = [(2 * j + 1, 2 * j + 2) for j in range(chips - 1)] + [(2 * j, 2 * j - 1) for j in range(1, chips)]
    meet += [(0, 0), (n - 1, n - 1)]
    lend = [(2 * j, 2 * j + 3) for j in range(chips - 1)] + [(2 * j + 1, 2 * j - 2) for j in range(1, chips)]
    lend += [(1, 1), (n - 2, n - 2)]
    deal = [(2 * j, 2 * j + 2) for j in range(chips - 1)] + [(2 * j + 1, 2 * j - 1) for j in range(1, chips)]
    deal += [(1, 0), (n - 2, n - 1)]
    tell = [(2 * j, 2 * j - 2) for j in range(1, chips)] + [(2 * j + 1, 2 * j + 3) for j in range(chips - 1)]
    tell += [(0, 1), (n - 1, n - 2)]

    upper, lower, lag = first(offsets, row_feats, col_feats)
    lag_other = lax.ppermute(lag, "row", across)
    x, y, coef_a = turn(0, offsets, p, lag, lag_other, upper, lower)
    rx = lax.ppermute(x, "blk", meet)
    sy = lax.ppermute(y, "blk", sibling)
    rx, sy, x, y = lax.optimization_barrier((rx, sy, x, y))
    ry = lax.ppermute(y, "blk", lend)
    sx = lax.ppermute(x, "blk", sibling)
    lag = pairs(offsets, p, rx, sy)
    lag_other = lax.ppermute(lag, "row", across)
    z, v, coef_b = turn(1, offsets, p, lag, lag_other, rx, sy)
    r_block = lax.ppermute(z, "blk", deal)
    coef_side = lax.ppermute(coef_b, "blk", tell)
    q, lag = side(n - 1, offsets, p, coef_side, sx, ry, z)
    lag_other = lax.ppermute(lag, "row", across)
    coef_c = solve(offsets, lag, lag_other)
    coef_got = lax.ppermute(coef_c, "blk", deal)
    coef_norm = lax.ppermute(coef_c, "blk", sibling)
    energy = finish(n - 1, offsets, p, coef_c, coef_got, z, q, r_block, v)
    norms = jnp.stack([coef_a[8:10], coef_b[8:10], coef_norm[8:10]]) / row_total
    return (energy, norms)


def solution(mesh):
    return jax.shard_map(
        body,
        mesh=mesh,
        in_specs=(P("row", None), P("blk", None), P()),
        out_specs=(P(None, "row", "blk"), P(None, None, "blk")),
        check_vma=False,
    )
```

```python
import functools
import math

import jax
import jax.numpy as jnp
from jax import lax
from jax.experimental import pallas as pl
from jax.experimental.pallas import tpu as pltpu
from jax.sharding import PartitionSpec as P

F32 = jnp.float32
BF16 = jnp.bfloat16
W = 256
H = 128
LAGS = 96
VMEM_LIMIT = 24 * 1024 * 1024
FIRST_LIMIT = 50 * 1024 * 1024


def group_rows(m):
    return (16 * m, 16) if m < 4 else (64 + 8 * (m - 4), 8)


def lag_targets(o):
    t, s = [0], [0]
    first, second = [0], [1]
    rows = {}
    for step in range(4):
        count = 1 << step
        for m in range(count):
            start, _ = group_rows(m)
            place = {3: 0, 2: 8, 1: 12, 0: 14}[step]
            for n in range(count):
                lag = (o[step] + s[n] - t[m]) & (W - 1)
                rows[start + place + n] = lag + W * second[n]
        if step < 3:
            t, s = t + [x + o[step] for x in s], s + [x - o[step] for x in t]
            first, second = first + second, second + first
    rows[15] = 0
    rows[16 + 14] = W
    return rows, t, first


def split(x):
    hi = x.astype(BF16)
    return hi, (x - hi.astype(F32)).astype(BF16)


TN = (((0,), (0,)), ((), ()))
NT = (((1,), (1,)), ((), ()))


def skew(x):
    row = lax.broadcasted_iota(jnp.int32, (W, W), 0)
    for bit in (1, 2, 4):
        x = jnp.where((row & bit) != 0, pltpu.roll(x, W - bit, 1), x)
    tiles = [pltpu.roll(x[8 * t : 8 * t + 8], (W - 8 * t) % W, 1) for t in range(W // 8)]
    return jnp.concatenate(tiles, axis=0)


def build_onehot(o, table_ref):
    rows, _, _ = lag_targets(o)
    table_ref[...] = jnp.full((LAGS, 128), -1, jnp.int32)
    for r, target in rows.items():
        table_ref[r : r + 1, :] = jnp.full((1, 128), target, jnp.int32)
    table = jnp.concatenate([table_ref[...]] * 4, axis=1)
    return (table == lax.broadcasted_iota(jnp.int32, (LAGS, 2 * W), 1)).astype(F32).astype(BF16)


def lag_products(gram, o, onehot, out_ref):
    _, bases, first = lag_targets(o)
    diags = {}
    for kind in (0, 1):
        sheets = [skew(gram[kind * W : (kind + 1) * W, side * W : (side + 1) * W]) for side in (0, 1)]
        hi, lo = split(jnp.concatenate(sheets, axis=1))
        diags[kind] = lax.dot_general(onehot, lo, NT, preferred_element_type=F32) + lax.dot_general(
            onehot, hi, NT, preferred_element_type=F32
        )
    for m in range(8):
        start, count = group_rows(m)
        tile = diags[first[m]][start : start + count]
        if m > 0:
            tile = pltpu.roll(tile, (-bases[m]) & (W - 1), 1)
        out_ref[start : start + count, :] = tile


def gram_of(a, b):
    hi, lo = split(jnp.concatenate([a, b], axis=1))
    return (
        lax.dot_general(hi, lo, TN, preferred_element_type=F32)
        + lax.dot_general(lo, hi, TN, preferred_element_type=F32)
        + lax.dot_general(hi, hi, TN, preferred_element_type=F32)
    )


def angle(g, upper_sq, lower_sq):
    twice = 2.0 * g
    diff = upper_sq - lower_sq
    scale = jnp.maximum(jnp.abs(twice), jnp.abs(diff))
    live = scale > 0.0
    safe = jnp.where(live, scale, 1.0)
    x = jnp.where(live, diff / safe, 1.0)
    y = jnp.where(live, twice / safe, 0.0)
    r = jnp.sqrt(x * x + y * y)
    big = jnp.sqrt(0.5 * (1.0 + jnp.abs(x) / r))
    small = 0.5 * jnp.abs(y) / (r * big)
    wide = x < 0.0
    c = jnp.where(wide, small, big)
    s = jnp.where(wide, big, small)
    s = jnp.where(y < 0.0, -s, s)
    cross = twice * c * s
    return c, s, c * c * upper_sq + cross + s * s * lower_sq, s * s * upper_sq - cross + c * c * lower_sq


def angles(lags, o, coef_ref):
    row = lax.broadcasted_iota(jnp.int32, (8, W), 0)
    a = jnp.ones((8, W), F32)
    b = jnp.ones((8, W), F32)
    upper_sq = lags[15:16]
    lower_sq = lags[30:31]
    tiles = [lags[16 * m + 8 : 16 * m + 16] for m in range(4)]
    last = [lags[group_rows(m)[0] : group_rows(m)[0] + 8] for m in range(8)]
    for step in range(4):
        count = 1 << step
        if step == 3:
            parts, place = last, 0
        else:
            parts, place = tiles[:count], (6, 4, 0)[step]
        acc = None
        for m in range(count):
            term = a[m : m + 1] * parts[m]
            acc = term if acc is None else acc + term
        view = pltpu.roll(b, place, 0) if place else b
        acc = jnp.where((row >= place) & (row < place + count), acc * view, 0.0)
        g = jnp.sum(acc, axis=0, keepdims=True)
        c, s, upper_sq, lower_sq = angle(g, upper_sq, lower_sq)
        coef_ref[step : step + 1, :] = c
        coef_ref[4 + step : 5 + step, :] = s
        if step < 3:
            shift_a, shift_b = pltpu.roll(a, count, 0), pltpu.roll(b, count, 0)
            a, b = jnp.where(row < count, c * a, s * shift_b), jnp.where(row < count, c * b, -s * shift_a)
            turn = (o[step] - o[step + 1]) & (W - 1)
            b = pltpu.roll(b, turn, 1)
            lower_sq = pltpu.roll(jnp.broadcast_to(lower_sq, (8, W)), turn, 1)[0:1]
    coef_ref[8:9, :] = upper_sq
    coef_ref[9:10, :] = pltpu.roll(jnp.broadcast_to(lower_sq, (8, W)), o[3] & (W - 1), 1)[0:1]


def halves(x):
    return [x[:, :H], x[:, H:]]


def turn_halves(x, amount):
    short = amount & (H - 1)
    lane = lax.broadcasted_iota(jnp.int32, (1, H), 1)
    cross = (lane < short) != ((amount & H) != 0)
    a, b = pltpu.roll(x[0], short, 1), pltpu.roll(x[1], short, 1)
    return [jnp.where(cross, b, a), jnp.where(cross, a, b)]


def rotate(upper, lower, coef, o):
    upper, lower = list(upper), turn_halves(lower, (-o[0]) & (W - 1))
    for step in range(4):
        for h in (0, 1):
            c = coef[step : step + 1, h * H : (h + 1) * H]
            s = coef[4 + step : 5 + step, h * H : (h + 1) * H]
            upper[h], lower[h] = c * upper[h] + s * lower[h], c * lower[h] - s * upper[h]
        turn = (o[step] - o[step + 1]) if step < 3 else o[3]
        lower = turn_halves(lower, turn & (W - 1))
    return upper, lower


SMEM = pl.BlockSpec(memory_space=pltpu.SMEM)
VMEM = pl.BlockSpec(memory_space=pltpu.VMEM)
ANY = pl.BlockSpec(memory_space=pl.ANY)
LAG_SHAPE = jax.ShapeDtypeStruct((LAGS, W), F32)
COEF_SHAPE = jax.ShapeDtypeStruct((16, W), F32)
ONEHOT_SHAPE = jax.ShapeDtypeStruct((LAGS, 2 * W), BF16)
TABLE = pltpu.VMEM((LAGS, 128), jnp.int32)


def tile_rows(rows, most=512):
    r = most
    while rows % r:
        r //= 2
    return r


def block(rows):
    return jax.ShapeDtypeStruct((rows, W), F32)


def call(kernel, name, in_specs, out_specs, out_shape, scratch=(), us=1, limit=VMEM_LIMIT):
    return pl.pallas_call(
        kernel,
        name=name,
        in_specs=in_specs,
        out_specs=out_specs,
        out_shape=out_shape,
        scratch_shapes=list(scratch),
        compiler_params=pltpu.CompilerParams(vmem_limit_bytes=limit),
        cost_estimate=pl.CostEstimate(flops=us * 10**9, bytes_accessed=us * 3 * 10**6, transcendentals=0),
    )


def offsets_of(o_ref, round_index):
    return [o_ref[round_index, j] for j in range(4)]


def pick(flag, a, b):
    return jnp.where(flag, a, b), jnp.where(flag, b, a)


def pick_halves(flag, a, b):
    pairs = [pick(flag, x, y) for x, y in zip(a, b)]
    return [x for x, _ in pairs], [y for _, y in pairs]


def read(ref, rows):
    return [ref[rows, :H], ref[rows, H:]]


def write(ref, rows, x):
    ref[rows, :H] = x[0]
    ref[rows, H:] = x[1]


def by_tiles(rows, go):
    r = tile_rows(rows)

    @pl.loop(0, rows // r)
    def _(i):
        go(pl.ds(pl.multiple_of(i * r, r), r))


def first_kernel(
    o_hbm, rows_hbm, cols_hbm, upper_ref, lower_ref, lag_ref, rows_ref, cols_ref, table_ref, norm_ref, o_ref, sem
):
    count, feat = cols_ref.shape
    total = rows_ref.shape[0]
    r = tile_rows(total)
    tiles = total // r
    half = count // 2
    fetch_cols = [
        pltpu.make_async_copy(cols_hbm.at[pl.ds(k * half, half)], cols_ref.at[pl.ds(k * half, half)], sem.at[k])
        for k in range(2)
    ]
    fetch_rows = [
        pltpu.make_async_copy(rows_hbm.at[pl.ds(t * r, r)], rows_ref.at[pl.ds(t * r, r)], sem.at[2 + t])
        for t in range(tiles)
    ]
    fetch_o = pltpu.make_async_copy(o_hbm, o_ref, sem.at[15])
    for copy in [fetch_o] + fetch_cols + fetch_rows:
        copy.start()
    fetch_o.wait()
    o = offsets_of(o_ref, 0)
    onehot = build_onehot(o, table_ref)
    for copy in fetch_cols:
        copy.wait()
    for t in range(tiles):
        fetch_rows[t].wait()
        if t == 0:
            for k in range(0, count, H):
                wide = cols_ref[k : k + H].astype(F32)
                sums = jnp.sum(wide * wide, axis=1, keepdims=True)
                norm_ref[:, k : k + H] = jnp.transpose(jnp.broadcast_to(sums, (H, H)))[0:8]
        part = slice(t * r, (t + 1) * r)
        rows = rows_ref[part]
        cross = lax.dot_general(rows, cols_ref[...], NT, preferred_element_type=F32)
        wide = rows.astype(F32)
        row_norm = jnp.sum(wide * wide, axis=1, keepdims=True)
        kernel = jnp.exp(
            -(0.25 / math.sqrt(feat)) * (row_norm + norm_ref[0:1] - 2.0 * cross - 2.0 * feat)
        )
        upper_ref[part] = kernel[:, :W]
        lower_ref[part] = kernel[:, W:]
    lag_products(gram_of(upper_ref[...], lower_ref[...]), o, onehot, lag_ref)


def first(offsets, row_feats, col_feats):
    rows, feat = row_feats.shape
    return call(
        first_kernel,
        "first",
        [ANY, ANY, ANY],
        (VMEM, VMEM, VMEM),
        (block(rows), block(rows), LAG_SHAPE),
        [
            pltpu.VMEM(row_feats.shape, BF16),
            pltpu.VMEM(col_feats.shape, BF16),
            TABLE,
            pltpu.VMEM((8, 2 * W), F32),
            pltpu.SMEM((3, 4), jnp.int32),
            pltpu.SemaphoreType.DMA((16,)),
        ],
        us=10,
        limit=FIRST_LIMIT,
    )(offsets, row_feats, col_feats)


def table_kernel(round_index, o_ref, after_ref, out_ref, table_ref):
    out_ref[...] = build_onehot(offsets_of(o_ref, round_index), table_ref)


def table(round_index, offsets, after):
    return call(
        functools.partial(table_kernel, round_index), "table%d" % round_index, [SMEM, ANY], VMEM, ONEHOT_SHAPE, [TABLE]
    )(offsets, after)


def turn_kernel(round_index, o_ref, p_ref, mine_ref, other_ref, a_ref, b_ref, first_ref, second_ref, coef_ref):
    p = p_ref[0]
    core = p & 1
    o = offsets_of(o_ref, round_index)
    angles(mine_ref[...] + other_ref[...], o, coef_ref)
    coef = coef_ref[...]

    def go(rows):
        upper, lower = read(a_ref, rows), read(b_ref, rows)
        if round_index == 0:
            keep = (core == 1) | (p == 0)
        else:
            upper, lower = pick_halves(core == 0, upper, lower)
            keep = (core == 0) & (p != 0)
        upper, lower = rotate(upper, lower, coef, o)
        upper, lower = pick_halves(keep, upper, lower)
        write(first_ref, rows, upper)
        write(second_ref, rows, lower)

    by_tiles(a_ref.shape[0], go)


def turn(round_index, offsets, p, mine, other, a, b):
    rows = a.shape[0]
    return call(
        functools.partial(turn_kernel, round_index),
        "turn%d" % round_index,
        [SMEM, SMEM] + [VMEM] * 4,
        (VMEM, VMEM, VMEM),
        (block(rows), block(rows), COEF_SHAPE),
        us=40,
    )(offsets, p, mine, other, a, b)


def pairs_kernel(o_ref, p_ref, hot_ref, a_ref, b_ref, lag_ref):
    upper, lower = pick((p_ref[0] & 1) == 0, a_ref[...], b_ref[...])
    lag_products(gram_of(upper, lower), offsets_of(o_ref, 1), hot_ref[...], lag_ref)


def pairs(offsets, p, hot, a, b):
    return call(
        pairs_kernel, "pairs", [SMEM, SMEM] + [VMEM] * 3, VMEM, LAG_SHAPE, us=5
    )(offsets, p, hot, a, b)


def side_kernel(last, o_ref, p_ref, hot_ref, coef_ref, sx_ref, ry_ref, z_ref, q_ref, lag_ref):
    p = p_ref[0]
    core = p & 1
    o = offsets_of(o_ref, 1)
    coef = coef_ref[...]
    near_end = (p == 1) | (p == last - 1)

    def go(rows):
        upper, lower = pick_halves((core == 0) != near_end, read(sx_ref, rows), read(ry_ref, rows))
        upper, lower = rotate(upper, lower, coef, o)
        wanted, _ = pick_halves((core == 1) | (p == last - 1), upper, lower)
        write(q_ref, rows, wanted)

    by_tiles(sx_ref.shape[0], go)
    upper, lower = pick(core == 0, z_ref[...], q_ref[...])
    lag_products(gram_of(upper, lower), offsets_of(o_ref, 2), hot_ref[...], lag_ref)


def side(last, offsets, p, hot, coef, sx, ry, z):
    return call(
        functools.partial(side_kernel, last),
        "side",
        [SMEM, SMEM] + [VMEM] * 5,
        (VMEM, VMEM),
        (block(sx.shape[0]), LAG_SHAPE),
        us=8,
    )(offsets, p, hot, coef, sx, ry, z)


def solve_kernel(o_ref, mine_ref, other_ref, coef_ref):
    angles(mine_ref[...] + other_ref[...], offsets_of(o_ref, 2), coef_ref)


def solve(offsets, mine, other):
    return call(solve_kernel, "solve", [SMEM, VMEM, VMEM], VMEM, COEF_SHAPE)(offsets, mine, other)


def own_kernel(o_ref, p_ref, coef_ref, z_ref, q_ref, out_ref):
    p = p_ref[0]
    core = p & 1
    o = offsets_of(o_ref, 2)
    coef = coef_ref[...]

    def go(rows):
        upper, lower = pick_halves(core == 0, read(z_ref, rows), read(q_ref, rows))
        upper, lower = rotate(upper, lower, coef, o)
        wanted, _ = pick_halves((core == 1) & (p != 1), upper, lower)
        write(out_ref, rows, [x * x for x in wanted])

    by_tiles(z_ref.shape[0], go)


def own(offsets, p, coef, z, q):
    return call(own_kernel, "own", [SMEM, SMEM] + [VMEM] * 3, VMEM, block(z.shape[0]), us=4)(
        offsets, p, coef, z, q
    )


def finish_kernel(
    last, row_total, o_ref, p_ref, coef_ref, a_ref, b_ref, c_ref, own_ref, r_ref, v_ref, out_hbm, norm_ref, e_ref, sem
):
    p = p_ref[0]
    core = p & 1
    o = offsets_of(o_ref, 2)
    keep = pltpu.make_async_copy(own_ref, out_hbm.at[1 - core], sem.at[0])
    keep.start()
    coef = coef_ref[...]
    for k, ref in enumerate((a_ref, b_ref, c_ref)):
        norm_ref[k] = ref[8:10, :] / row_total
    total = r_ref.shape[0]
    r = tile_rows(total)
    sends = []
    for t in range(total // r):
        rows = pl.ds(t * r, r)
        swap = (p == 0) | (p == last)
        upper, lower = pick_halves((core == 0) != swap, read(r_ref, rows), read(v_ref, rows))
        upper, lower = rotate(upper, lower, coef, o)
        wanted, _ = pick_halves((core == 0) | (p == last), upper, lower)
        write(e_ref, rows, [x * x for x in wanted])
        copy = pltpu.make_async_copy(e_ref.at[rows], out_hbm.at[core, rows], sem.at[1 + t])
        copy.start()
        sends.append(copy)
    for copy in [keep] + sends:
        copy.wait()


def finish(last, row_total, offsets, p, coef, coefs, own_block, r_block, v):
    rows = v.shape[0]
    return call(
        functools.partial(finish_kernel, last, row_total),
        "finish",
        [SMEM, SMEM] + [VMEM] * 7,
        (ANY, VMEM),
        (jax.ShapeDtypeStruct((2, rows, W), F32), jax.ShapeDtypeStruct((3, 2, W), F32)),
        [pltpu.VMEM((rows, W), F32), pltpu.SemaphoreType.DMA((16,))],
        us=5,
    )(offsets, p, coef, *coefs, own_block, r_block, v)


def body(row_feats, col_feats, offsets):
    n = lax.axis_size("blk")
    chips = n // 2
    p = lax.axis_index("blk").astype(jnp.int32).reshape(1)
    row_total = row_feats.shape[0] * lax.axis_size("row")
    across = [(0, 1), (1, 0)]
    sibling = [(i, i ^ 1) for i in range(n)]
    meet = [(2 * j + 1, 2 * j + 2) for j in range(chips - 1)] + [(2 * j, 2 * j - 1) for j in range(1, chips)]
    meet += [(0, 0), (n - 1, n - 1)]
    lend = [(2 * j, 2 * j + 3) for j in range(chips - 1)] + [(2 * j + 1, 2 * j - 2) for j in range(1, chips)]
    lend += [(1, 1), (n - 2, n - 2)]
    deal = [(2 * j, 2 * j + 2) for j in range(chips - 1)] + [(2 * j + 1, 2 * j - 1) for j in range(1, chips)]
    deal += [(1, 0), (n - 2, n - 1)]
    tell = [(2 * j, 2 * j - 2) for j in range(1, chips)] + [(2 * j + 1, 2 * j + 3) for j in range(chips - 1)]
    tell += [(0, 1), (n - 1, n - 2)]

    upper, lower, lag = first(offsets, row_feats, col_feats)
    lag_other = lax.ppermute(lag, "row", across)
    hot = table(1, offsets, lag)
    x, y, coef_a = turn(0, offsets, p, lag, lag_other, upper, lower)
    rx = lax.ppermute(x, "blk", meet)
    sy = lax.ppermute(y, "blk", sibling)
    sx = lax.ppermute(x, "blk", sibling)
    lag = pairs(offsets, p, hot, rx, sy)
    lag_other = lax.ppermute(lag, "row", across)
    hot = table(2, offsets, lag)
    y, hot = lax.optimization_barrier((y, hot))
    ry = lax.ppermute(y, "blk", lend)
    z, v, coef_b = turn(1, offsets, p, lag, lag_other, rx, sy)
    coef_side = lax.ppermute(coef_b, "blk", tell)
    z, coef_side = lax.optimization_barrier((z, coef_side))
    r_block = lax.ppermute(z, "blk", deal)
    q, lag = side(n - 1, offsets, p, hot, coef_side, sx, ry, z)
    lag_other = lax.ppermute(lag, "row", across)
    coef_c = solve(offsets, lag, lag_other)
    coef_got = lax.ppermute(coef_c, "blk", deal)
    coef_norm = lax.ppermute(coef_c, "blk", sibling)
    own_block = own(offsets, p, coef_c, z, q)
    return finish(n - 1, row_total, offsets, p, coef_got, (coef_a, coef_b, coef_norm), own_block, r_block, v)


def solution(mesh):
    return jax.shard_map(
        body,
        mesh=mesh,
        in_specs=(P("row", None), P("blk", None), P()),
        out_specs=(P(None, "row", "blk"), P(None, None, "blk")),
        check_vma=False,
    )
```

```python
import functools
import math

import jax
import jax.numpy as jnp
from jax import lax
from jax.experimental import pallas as pl
from jax.experimental.pallas import tpu as pltpu
from jax.sharding import PartitionSpec as P

F32 = jnp.float32
BF16 = jnp.bfloat16
W = 256
H = 128
LAGS = 96
VMEM_LIMIT = 24 * 1024 * 1024
FIRST_LIMIT = 50 * 1024 * 1024


def group_rows(m):
    return (16 * m, 16) if m < 4 else (64 + 8 * (m - 4), 8)


def lag_targets(o):
    t, s = [0], [0]
    first, second = [0], [1]
    rows = {}
    for step in range(4):
        count = 1 << step
        for m in range(count):
            start, _ = group_rows(m)
            place = {3: 0, 2: 8, 1: 12, 0: 14}[step]
            for n in range(count):
                lag = (o[step] + s[n] - t[m]) & (W - 1)
                rows[start + place + n] = lag + W * second[n]
        if step < 3:
            t, s = t + [x + o[step] for x in s], s + [x - o[step] for x in t]
            first, second = first + second, second + first
    rows[15] = 0
    rows[16 + 14] = W
    return rows, t, first


def split(x):
    hi = x.astype(BF16)
    return hi, (x - hi.astype(F32)).astype(BF16)


TN = (((0,), (0,)), ((), ()))
NT = (((1,), (1,)), ((), ()))


def skew(x):
    row = lax.broadcasted_iota(jnp.int32, (W, W), 0)
    for bit in (1, 2, 4):
        x = jnp.where((row & bit) != 0, pltpu.roll(x, W - bit, 1), x)
    tiles = [pltpu.roll(x[8 * t : 8 * t + 8], (W - 8 * t) % W, 1) for t in range(W // 8)]
    return jnp.concatenate(tiles, axis=0)


def build_onehot(o, table_ref):
    rows, _, _ = lag_targets(o)
    table_ref[...] = jnp.full((LAGS, 128), -1, jnp.int32)
    for r, target in rows.items():
        table_ref[r : r + 1, :] = jnp.full((1, 128), target, jnp.int32)
    table = jnp.concatenate([table_ref[...]] * 4, axis=1)
    return (table == lax.broadcasted_iota(jnp.int32, (LAGS, 2 * W), 1)).astype(F32).astype(BF16)


def lag_products(gram, o, onehot, out_ref):
    _, bases, first = lag_targets(o)
    diags = {}
    for kind in (0, 1):
        sheets = [skew(gram[kind * W : (kind + 1) * W, side * W : (side + 1) * W]) for side in (0, 1)]
        hi, lo = split(jnp.concatenate(sheets, axis=1))
        diags[kind] = lax.dot_general(onehot, lo, NT, preferred_element_type=F32) + lax.dot_general(
            onehot, hi, NT, preferred_element_type=F32
        )
    for m in range(8):
        start, count = group_rows(m)
        tile = diags[first[m]][start : start + count]
        if m > 0:
            tile = pltpu.roll(tile, (-bases[m]) & (W - 1), 1)
        out_ref[start : start + count, :] = tile


def gram_of(a, b):
    hi, lo = split(jnp.concatenate([a, b], axis=1))
    return (
        lax.dot_general(hi, lo, TN, preferred_element_type=F32)
        + lax.dot_general(lo, hi, TN, preferred_element_type=F32)
        + lax.dot_general(hi, hi, TN, preferred_element_type=F32)
    )


def angle(g, upper_sq, lower_sq):
    twice = 2.0 * g
    diff = upper_sq - lower_sq
    scale = jnp.maximum(jnp.abs(twice), jnp.abs(diff))
    live = scale > 0.0
    safe = jnp.where(live, scale, 1.0)
    x = jnp.where(live, diff / safe, 1.0)
    y = jnp.where(live, twice / safe, 0.0)
    r = jnp.sqrt(x * x + y * y)
    big = jnp.sqrt(0.5 * (1.0 + jnp.abs(x) / r))
    small = 0.5 * jnp.abs(y) / (r * big)
    wide = x < 0.0
    c = jnp.where(wide, small, big)
    s = jnp.where(wide, big, small)
    s = jnp.where(y < 0.0, -s, s)
    cross = twice * c * s
    return c, s, c * c * upper_sq + cross + s * s * lower_sq, s * s * upper_sq - cross + c * c * lower_sq


def angles(lags, o, coef_ref):
    row = lax.broadcasted_iota(jnp.int32, (8, W), 0)
    a = jnp.ones((8, W), F32)
    b = jnp.ones((8, W), F32)
    upper_sq = lags[15:16]
    lower_sq = lags[30:31]
    tiles = [lags[16 * m + 8 : 16 * m + 16] for m in range(4)]
    last = [lags[group_rows(m)[0] : group_rows(m)[0] + 8] for m in range(8)]
    for step in range(4):
        count = 1 << step
        if step == 3:
            parts, place = last, 0
        else:
            parts, place = tiles[:count], (6, 4, 0)[step]
        acc = None
        for m in range(count):
            term = a[m : m + 1] * parts[m]
            acc = term if acc is None else acc + term
        view = pltpu.roll(b, place, 0) if place else b
        acc = jnp.where((row >= place) & (row < place + count), acc * view, 0.0)
        g = jnp.sum(acc, axis=0, keepdims=True)
        c, s, upper_sq, lower_sq = angle(g, upper_sq, lower_sq)
        coef_ref[step : step + 1, :] = c
        coef_ref[4 + step : 5 + step, :] = s
        if step < 3:
            shift_a, shift_b = pltpu.roll(a, count, 0), pltpu.roll(b, count, 0)
            a, b = jnp.where(row < count, c * a, s * shift_b), jnp.where(row < count, c * b, -s * shift_a)
            turn = (o[step] - o[step + 1]) & (W - 1)
            b = pltpu.roll(b, turn, 1)
            lower_sq = pltpu.roll(jnp.broadcast_to(lower_sq, (8, W)), turn, 1)[0:1]
    coef_ref[8:9, :] = upper_sq
    coef_ref[9:10, :] = pltpu.roll(jnp.broadcast_to(lower_sq, (8, W)), o[3] & (W - 1), 1)[0:1]


def halves(x):
    return [x[:, :H], x[:, H:]]


def turn_halves(x, amount):
    short = amount & (H - 1)
    lane = lax.broadcasted_iota(jnp.int32, (1, H), 1)
    cross = (lane < short) != ((amount & H) != 0)
    a, b = pltpu.roll(x[0], short, 1), pltpu.roll(x[1], short, 1)
    return [jnp.where(cross, b, a), jnp.where(cross, a, b)]


def rotate(upper, lower, coef, o):
    upper, lower = list(upper), turn_halves(lower, (-o[0]) & (W - 1))
    for step in range(4):
        for h in (0, 1):
            c = coef[step : step + 1, h * H : (h + 1) * H]
            s = coef[4 + step : 5 + step, h * H : (h + 1) * H]
            upper[h], lower[h] = c * upper[h] + s * lower[h], c * lower[h] - s * upper[h]
        turn = (o[step] - o[step + 1]) if step < 3 else o[3]
        lower = turn_halves(lower, turn & (W - 1))
    return upper, lower


SMEM = pl.BlockSpec(memory_space=pltpu.SMEM)
VMEM = pl.BlockSpec(memory_space=pltpu.VMEM)
ANY = pl.BlockSpec(memory_space=pl.ANY)
LAG_SHAPE = jax.ShapeDtypeStruct((LAGS, W), F32)
COEF_SHAPE = jax.ShapeDtypeStruct((16, W), F32)
ONEHOT_SHAPE = jax.ShapeDtypeStruct((LAGS, 2 * W), BF16)
TABLE = pltpu.VMEM((LAGS, 128), jnp.int32)


def tile_rows(rows, most=512):
    r = most
    while rows % r:
        r //= 2
    return r


def block(rows):
    return jax.ShapeDtypeStruct((rows, W), F32)


def call(kernel, name, in_specs, out_specs, out_shape, scratch=(), us=1, limit=VMEM_LIMIT):
    return pl.pallas_call(
        kernel,
        name=name,
        in_specs=in_specs,
        out_specs=out_specs,
        out_shape=out_shape,
        scratch_shapes=list(scratch),
        compiler_params=pltpu.CompilerParams(vmem_limit_bytes=limit),
        cost_estimate=pl.CostEstimate(flops=us * 10**9, bytes_accessed=us * 3 * 10**6, transcendentals=0),
    )


def offsets_of(o_ref, round_index):
    return [o_ref[round_index, j] for j in range(4)]


def pick(flag, a, b):
    return jnp.where(flag, a, b), jnp.where(flag, b, a)


def pick_halves(flag, a, b):
    pairs = [pick(flag, x, y) for x, y in zip(a, b)]
    return [x for x, _ in pairs], [y for _, y in pairs]


def read(ref, rows):
    return [ref[rows, :H], ref[rows, H:]]


def write(ref, rows, x):
    ref[rows, :H] = x[0]
    ref[rows, H:] = x[1]


def first_kernel(
    o_hbm, rows_hbm, cols_hbm, upper_ref, lower_ref, lag_ref, rows_ref, cols_ref, table_ref, norm_ref, o_ref, sem
):
    count, feat = cols_ref.shape
    total = rows_ref.shape[0]
    r = tile_rows(total)
    tiles = total // r
    half = count // 2
    fetch_cols = [
        pltpu.make_async_copy(cols_hbm.at[pl.ds(k * half, half)], cols_ref.at[pl.ds(k * half, half)], sem.at[k])
        for k in range(2)
    ]
    fetch_rows = [
        pltpu.make_async_copy(rows_hbm.at[pl.ds(t * r, r)], rows_ref.at[pl.ds(t * r, r)], sem.at[2 + t])
        for t in range(tiles)
    ]
    fetch_o = pltpu.make_async_copy(o_hbm, o_ref, sem.at[15])
    for copy in [fetch_o] + fetch_cols + fetch_rows:
        copy.start()
    fetch_o.wait()
    o = offsets_of(o_ref, 0)
    onehot = build_onehot(o, table_ref)
    for copy in fetch_cols:
        copy.wait()
    for t in range(tiles):
        fetch_rows[t].wait()
        if t == 0:
            for k in range(0, count, H):
                wide = cols_ref[k : k + H].astype(F32)
                sums = jnp.sum(wide * wide, axis=1, keepdims=True)
                norm_ref[:, k : k + H] = jnp.transpose(jnp.broadcast_to(sums, (H, H)))[0:8]
        part = slice(t * r, (t + 1) * r)
        rows = rows_ref[part]
        cross = lax.dot_general(rows, cols_ref[...], NT, preferred_element_type=F32)
        wide = rows.astype(F32)
        row_norm = jnp.sum(wide * wide, axis=1, keepdims=True)
        kernel = jnp.exp(
            -(0.25 / math.sqrt(feat)) * (row_norm + norm_ref[0:1] - 2.0 * cross - 2.0 * feat)
        )
        upper_ref[part] = kernel[:, :W]
        lower_ref[part] = kernel[:, W:]
    lag_products(gram_of(upper_ref[...], lower_ref[...]), o, onehot, lag_ref)


def first(offsets, row_feats, col_feats):
    rows, feat = row_feats.shape
    return call(
        first_kernel,
        "first",
        [ANY, ANY, ANY],
        (VMEM, VMEM, VMEM),
        (block(rows), block(rows), LAG_SHAPE),
        [
            pltpu.VMEM(row_feats.shape, BF16),
            pltpu.VMEM(col_feats.shape, BF16),
            TABLE,
            pltpu.VMEM((8, 2 * W), F32),
            pltpu.SMEM((3, 4), jnp.int32),
            pltpu.SemaphoreType.DMA((16,)),
        ],
        us=10,
        limit=FIRST_LIMIT,
    )(offsets, row_feats, col_feats)


def table_kernel(round_index, o_ref, after_ref, out_ref, table_ref):
    out_ref[...] = build_onehot(offsets_of(o_ref, round_index), table_ref)


def table(round_index, offsets, after):
    return call(
        functools.partial(table_kernel, round_index), "table%d" % round_index, [SMEM, ANY], VMEM, ONEHOT_SHAPE, [TABLE]
    )(offsets, after)


def by_parts(total, go):
    part = total // 2
    r = tile_rows(part, 384)
    for k in range(2):

        @pl.loop(0, part // r)
        def _(i):
            start = pl.multiple_of(i * r, r)
            go(pl.ds(pl.multiple_of(k * part + i * r, r), r), k, pl.ds(start, r))


def turn_first_kernel(o_ref, p_ref, mine_ref, other_ref, a_ref, b_ref, xa, xb, ya, yb, coef_ref):
    p = p_ref[0]
    o = offsets_of(o_ref, 0)
    angles(mine_ref[...] + other_ref[...], o, coef_ref)
    coef = coef_ref[...]
    keep = ((p & 1) == 1) | (p == 0)

    def go(rows, k, rows_part):
        upper, lower = rotate(read(a_ref, rows), read(b_ref, rows), coef, o)
        x, y = pick_halves(keep, upper, lower)
        write((xa, xb)[k], rows_part, x)
        write((ya, yb)[k], rows_part, y)

    by_parts(a_ref.shape[0], go)


def turn_first(offsets, p, mine, other, a, b):
    rows = a.shape[0]
    part = block(rows // 2)
    return call(
        turn_first_kernel,
        "turn0",
        [SMEM, SMEM] + [VMEM] * 4,
        (VMEM,) * 5,
        (part, part, part, part, COEF_SHAPE),
        us=5,
    )(offsets, p, mine, other, a, b)


def pairs_start_kernel(p_ref, a_ref, b_ref, gram_ref):
    upper, lower = pick((p_ref[0] & 1) == 0, a_ref[...], b_ref[...])
    gram_ref[...] = gram_of(upper, lower)


def pairs_start(p, a, b):
    return call(
        pairs_start_kernel, "pairs0", [SMEM, VMEM, VMEM], VMEM, jax.ShapeDtypeStruct((2 * W, 2 * W), F32), us=3
    )(p, a, b)


def pairs_kernel(o_ref, p_ref, hot_ref, gram_ref, a_ref, b_ref, lag_ref):
    upper, lower = pick((p_ref[0] & 1) == 0, a_ref[...], b_ref[...])
    lag_products(gram_ref[...] + gram_of(upper, lower), offsets_of(o_ref, 1), hot_ref[...], lag_ref)


def pairs(offsets, p, hot, gram, a, b):
    return call(
        pairs_kernel, "pairs1", [SMEM, SMEM] + [VMEM] * 4, VMEM, LAG_SHAPE, us=4
    )(offsets, p, hot, gram, a, b)


def turn_second_kernel(o_ref, p_ref, mine_ref, other_ref, rxa, rxb, sya, syb, za, zb, v_ref, coef_ref):
    p = p_ref[0]
    core = p & 1
    o = offsets_of(o_ref, 1)
    angles(mine_ref[...] + other_ref[...], o, coef_ref)
    coef = coef_ref[...]

    def go(rows, k, rows_part):
        upper, lower = pick_halves(core == 0, read((rxa, rxb)[k], rows_part), read((sya, syb)[k], rows_part))
        upper, lower = rotate(upper, lower, coef, o)
        z, v = pick_halves((core == 0) & (p != 0), upper, lower)
        write((za, zb)[k], rows_part, z)
        write(v_ref, rows, v)

    by_parts(v_ref.shape[0], go)


def turn_second(offsets, p, mine, other, rxa, rxb, sya, syb):
    rows = rxa.shape[0] * 2
    part = block(rows // 2)
    return call(
        turn_second_kernel,
        "turn1",
        [SMEM, SMEM] + [VMEM] * 6,
        (VMEM,) * 4,
        (part, part, block(rows), COEF_SHAPE),
        us=40,
    )(offsets, p, mine, other, rxa, rxb, sya, syb)


def side_kernel(last, o_ref, p_ref, hot_ref, coef_ref, sxa, sxb, rya, ryb, za, zb, q_ref, lag_ref):
    p = p_ref[0]
    core = p & 1
    o = offsets_of(o_ref, 1)
    coef = coef_ref[...]
    near_end = (p == 1) | (p == last - 1)
    part = za.shape[0]

    def go(rows, k, rows_part):
        upper, lower = pick_halves(
            (core == 0) != near_end, read((sxa, sxb)[k], rows_part), read((rya, ryb)[k], rows_part)
        )
        upper, lower = rotate(upper, lower, coef, o)
        wanted, _ = pick_halves((core == 1) | (p == last - 1), upper, lower)
        write(q_ref, rows, wanted)

    by_parts(q_ref.shape[0], go)
    z = jnp.concatenate([za[...], zb[...]], axis=0)
    upper, lower = pick(core == 0, z, q_ref[...])
    lag_products(gram_of(upper, lower), offsets_of(o_ref, 2), hot_ref[...], lag_ref)


def side(last, offsets, p, hot, coef, sxa, sxb, rya, ryb, za, zb):
    return call(
        functools.partial(side_kernel, last),
        "side",
        [SMEM, SMEM] + [VMEM] * 8,
        (VMEM, VMEM),
        (block(2 * za.shape[0]), LAG_SHAPE),
        us=8,
    )(offsets, p, hot, coef, sxa, sxb, rya, ryb, za, zb)


def solve_kernel(round_index, o_ref, *refs):
    count = len(refs) // 3
    for k in range(count):
        angles(refs[2 * k][...] + refs[2 * k + 1][...], offsets_of(o_ref, round_index), refs[2 * count + k])


def solve(round_index, offsets, *lags):
    count = len(lags) // 2
    return call(
        functools.partial(solve_kernel, round_index),
        "solve%d" % round_index,
        [SMEM] + [VMEM] * len(lags),
        (VMEM,) * count,
        (COEF_SHAPE,) * count,
        us=2,
    )(offsets, *lags)


def own_kernel(o_ref, p_ref, coef_ref, za, zb, q_ref, out_ref):
    p = p_ref[0]
    core = p & 1
    o = offsets_of(o_ref, 2)
    coef = coef_ref[...]

    def go(rows, k, rows_part):
        upper, lower = pick_halves(core == 0, read((za, zb)[k], rows_part), read(q_ref, rows))
        upper, lower = rotate(upper, lower, coef, o)
        wanted, _ = pick_halves((core == 1) & (p != 1), upper, lower)
        write(out_ref, rows, [x * x for x in wanted])

    by_parts(q_ref.shape[0], go)


def own(offsets, p, coef, za, zb, q):
    return call(own_kernel, "own", [SMEM, SMEM] + [VMEM] * 4, VMEM, block(q.shape[0]), us=40)(
        offsets, p, coef, za, zb, q
    )


def finish_kernel(
    last, row_total, o_ref, p_ref, coef_ref, a_ref, b_ref, c_ref, own_ref, ra, rb, v_ref, out_hbm, norm_ref, e_ref, sem
):
    p = p_ref[0]
    core = p & 1
    o = offsets_of(o_ref, 2)
    keep = pltpu.make_async_copy(own_ref, out_hbm.at[1 - core], sem.at[0])
    keep.start()
    coef = coef_ref[...]
    for k, ref in enumerate((a_ref, b_ref, c_ref)):
        norm_ref[k] = ref[8:10, :] / row_total
    part = ra.shape[0]
    r = tile_rows(part, 384)
    tiles = part // r
    sends = []
    for t in range(2 * tiles):
        rows = pl.ds(t * r, r)
        swap = (p == 0) | (p == last)
        upper, lower = pick_halves((core == 0) != swap, read((ra, rb)[t // tiles], pl.ds(t % tiles * r, r)), read(v_ref, rows))
        upper, lower = rotate(upper, lower, coef, o)
        wanted, _ = pick_halves((core == 0) | (p == last), upper, lower)
        write(e_ref, rows, [x * x for x in wanted])
        copy = pltpu.make_async_copy(e_ref.at[rows], out_hbm.at[core, rows], sem.at[1 + t])
        copy.start()
        sends.append(copy)
    for copy in [keep] + sends:
        copy.wait()


def finish(last, row_total, offsets, p, coef, coefs, own_block, ra, rb, v):
    rows = v.shape[0]
    return call(
        functools.partial(finish_kernel, last, row_total),
        "finish",
        [SMEM, SMEM] + [VMEM] * 8,
        (ANY, VMEM),
        (jax.ShapeDtypeStruct((2, rows, W), F32), jax.ShapeDtypeStruct((3, 2, W), F32)),
        [pltpu.VMEM((rows, W), F32), pltpu.SemaphoreType.DMA((16,))],
        us=5,
    )(offsets, p, coef, *coefs, own_block, ra, rb, v)


def body(row_feats, col_feats, offsets):
    n = lax.axis_size("blk")
    chips = n // 2
    p = lax.axis_index("blk").astype(jnp.int32).reshape(1)
    row_total = row_feats.shape[0] * lax.axis_size("row")
    across = [(0, 1), (1, 0)]
    sibling = [(i, i ^ 1) for i in range(n)]
    meet = [(2 * j + 1, 2 * j + 2) for j in range(chips - 1)] + [(2 * j, 2 * j - 1) for j in range(1, chips)]
    meet += [(0, 0), (n - 1, n - 1)]
    lend = [(2 * j, 2 * j + 3) for j in range(chips - 1)] + [(2 * j + 1, 2 * j - 2) for j in range(1, chips)]
    lend += [(1, 1), (n - 2, n - 2)]
    deal = [(2 * j, 2 * j + 2) for j in range(chips - 1)] + [(2 * j + 1, 2 * j - 1) for j in range(1, chips)]
    deal += [(1, 0), (n - 2, n - 1)]
    tell = [(2 * j, 2 * j - 2) for j in range(1, chips)] + [(2 * j + 1, 2 * j + 3) for j in range(chips - 1)]
    tell += [(0, 1), (n - 1, n - 2)]

    def exchange(lag, perm):
        flipped = [(2 * i + r, 2 * j + 1 - r) for i, j in perm for r in (0, 1)]
        return (
            lax.ppermute(lag, "row", across),
            lax.ppermute(lag, "blk", perm),
            lax.ppermute(lag, ("blk", "row"), flipped),
        )

    upper, lower, lag = first(offsets, row_feats, col_feats)
    lag_other = lax.ppermute(lag, "row", across)
    xa, xb, ya, yb, coef_a = turn_first(offsets, p, lag, lag_other, upper, lower)
    hot = table(1, offsets, coef_a)
    rxa = lax.ppermute(xa, "blk", meet)
    rxb = lax.ppermute(xb, "blk", meet)
    xa, xb, ya, yb, hot = lax.optimization_barrier((xa, xb, ya, yb, hot))
    sya = lax.ppermute(ya, "blk", sibling)
    syb = lax.ppermute(yb, "blk", sibling)
    sxa = lax.ppermute(xa, "blk", sibling)
    sxb = lax.ppermute(xb, "blk", sibling)
    gram = pairs_start(p, rxa, sya)
    ya, gram = lax.optimization_barrier((ya, gram))
    rya = lax.ppermute(ya, "blk", lend)
    lag = pairs(offsets, p, hot, gram, rxb, syb)
    lag_other, lag_told, lag_told_other = exchange(lag, tell)
    hot = table(2, offsets, lag)
    yb, hot = lax.optimization_barrier((yb, hot))
    ryb = lax.ppermute(yb, "blk", lend)
    rxa, rya, sxa, sxb = lax.optimization_barrier((rxa, rya, sxa, sxb))
    za, zb, v, coef_b = turn_second(offsets, p, lag, lag_other, rxa, rxb, sya, syb)
    ra = lax.ppermute(za, "blk", deal)
    lag_told, lag_told_other, coef_b = lax.optimization_barrier((lag_told, lag_told_other, coef_b))
    (coef_side,) = solve(1, offsets, lag_told, lag_told_other)
    q, lag = side(n - 1, offsets, p, hot, coef_side, sxa, sxb, rya, ryb, za, zb)
    lag_other, lag_got, lag_got_other = exchange(lag, deal)
    later, _ = lax.optimization_barrier((zb, lag))
    rb = lax.ppermute(later, "blk", deal)
    coef_c, coef_got = solve(2, offsets, lag, lag_other, lag_got, lag_got_other)
    coef_norm = lax.ppermute(coef_c, "blk", sibling)
    coef_own, ra = lax.optimization_barrier((coef_c, ra))
    own_block = own(offsets, p, coef_own, za, zb, q)
    return finish(n - 1, row_total, offsets, p, coef_got, (coef_a, coef_b, coef_norm), own_block, ra, rb, v)


def solution(mesh):
    return jax.shard_map(
        body,
        mesh=mesh,
        in_specs=(P("row", None), P("blk", None), P()),
        out_specs=(P(None, "row", "blk"), P(None, None, "blk")),
        check_vma=False,
    )
```

```python
import functools
import math

import jax
import jax.numpy as jnp
from jax import lax
from jax.experimental import pallas as pl
from jax.experimental.pallas import tpu as pltpu
from jax.sharding import PartitionSpec as P

F32 = jnp.float32
BF16 = jnp.bfloat16
W = 256
H = 128
LAGS = 96
VMEM_LIMIT = 24 * 1024 * 1024
FIRST_LIMIT = 50 * 1024 * 1024


def group_rows(m):
    return (16 * m, 16) if m < 4 else (64 + 8 * (m - 4), 8)


def lag_targets(o):
    t, s = [0], [0]
    first, second = [0], [1]
    rows = {}
    for step in range(4):
        count = 1 << step
        for m in range(count):
            start, _ = group_rows(m)
            place = {3: 0, 2: 8, 1: 12, 0: 14}[step]
            for n in range(count):
                lag = (o[step] + s[n] - t[m]) & (W - 1)
                rows[start + place + n] = lag + W * second[n]
        if step < 3:
            t, s = t + [x + o[step] for x in s], s + [x - o[step] for x in t]
            first, second = first + second, second + first
    rows[15] = 0
    rows[16 + 14] = W
    return rows, t, first


def split(x):
    hi = x.astype(BF16)
    return hi, (x - hi.astype(F32)).astype(BF16)


TN = (((0,), (0,)), ((), ()))
NT = (((1,), (1,)), ((), ()))


def skew(x):
    row = lax.broadcasted_iota(jnp.int32, (W, W), 0)
    for bit in (1, 2, 4):
        x = jnp.where((row & bit) != 0, pltpu.roll(x, W - bit, 1), x)
    tiles = [pltpu.roll(x[8 * t : 8 * t + 8], (W - 8 * t) % W, 1) for t in range(W // 8)]
    return jnp.concatenate(tiles, axis=0)


def build_onehot(o, table_ref):
    rows, _, _ = lag_targets(o)
    table_ref[...] = jnp.full((LAGS, 128), -1, jnp.int32)
    for r, target in rows.items():
        table_ref[r : r + 1, :] = jnp.full((1, 128), target, jnp.int32)
    table = jnp.concatenate([table_ref[...]] * 4, axis=1)
    return (table == lax.broadcasted_iota(jnp.int32, (LAGS, 2 * W), 1)).astype(F32).astype(BF16)


def lag_products(gram, o, onehot, out_ref):
    _, bases, first = lag_targets(o)
    diags = {}
    for kind in (0, 1):
        sheets = [skew(gram[kind * W : (kind + 1) * W, side * W : (side + 1) * W]) for side in (0, 1)]
        hi, lo = split(jnp.concatenate(sheets, axis=1))
        diags[kind] = lax.dot_general(onehot, lo, NT, preferred_element_type=F32) + lax.dot_general(
            onehot, hi, NT, preferred_element_type=F32
        )
    for m in range(8):
        start, count = group_rows(m)
        tile = diags[first[m]][start : start + count]
        if m > 0:
            tile = pltpu.roll(tile, (-bases[m]) & (W - 1), 1)
        out_ref[start : start + count, :] = tile


def gram_of(a, b):
    hi, lo = split(jnp.concatenate([a, b], axis=1))
    return (
        lax.dot_general(hi, lo, TN, preferred_element_type=F32)
        + lax.dot_general(lo, hi, TN, preferred_element_type=F32)
        + lax.dot_general(hi, hi, TN, preferred_element_type=F32)
    )


def angle(g, upper_sq, lower_sq):
    twice = 2.0 * g
    diff = upper_sq - lower_sq
    scale = jnp.maximum(jnp.abs(twice), jnp.abs(diff))
    live = scale > 0.0
    safe = jnp.where(live, scale, 1.0)
    x = jnp.where(live, diff / safe, 1.0)
    y = jnp.where(live, twice / safe, 0.0)
    r = jnp.sqrt(x * x + y * y)
    big = jnp.sqrt(0.5 * (1.0 + jnp.abs(x) / r))
    small = 0.5 * jnp.abs(y) / (r * big)
    wide = x < 0.0
    c = jnp.where(wide, small, big)
    s = jnp.where(wide, big, small)
    s = jnp.where(y < 0.0, -s, s)
    cross = twice * c * s
    return c, s, c * c * upper_sq + cross + s * s * lower_sq, s * s * upper_sq - cross + c * c * lower_sq


def angles(lags, o, coef_ref):
    row = lax.broadcasted_iota(jnp.int32, (8, W), 0)
    a = jnp.ones((8, W), F32)
    b = jnp.ones((8, W), F32)
    upper_sq = lags[15:16]
    lower_sq = lags[30:31]
    tiles = [lags[16 * m + 8 : 16 * m + 16] for m in range(4)]
    last = [lags[group_rows(m)[0] : group_rows(m)[0] + 8] for m in range(8)]
    for step in range(4):
        count = 1 << step
        if step == 3:
            parts, place = last, 0
        else:
            parts, place = tiles[:count], (6, 4, 0)[step]
        acc = None
        for m in range(count):
            term = a[m : m + 1] * parts[m]
            acc = term if acc is None else acc + term
        view = pltpu.roll(b, place, 0) if place else b
        acc = jnp.where((row >= place) & (row < place + count), acc * view, 0.0)
        g = jnp.sum(acc, axis=0, keepdims=True)
        c, s, upper_sq, lower_sq = angle(g, upper_sq, lower_sq)
        coef_ref[step : step + 1, :] = c
        coef_ref[4 + step : 5 + step, :] = s
        if step < 3:
            shift_a, shift_b = pltpu.roll(a, count, 0), pltpu.roll(b, count, 0)
            a, b = jnp.where(row < count, c * a, s * shift_b), jnp.where(row < count, c * b, -s * shift_a)
            turn = (o[step] - o[step + 1]) & (W - 1)
            b = pltpu.roll(b, turn, 1)
            lower_sq = pltpu.roll(jnp.broadcast_to(lower_sq, (8, W)), turn, 1)[0:1]
    coef_ref[8:9, :] = upper_sq
    coef_ref[9:10, :] = pltpu.roll(jnp.broadcast_to(lower_sq, (8, W)), o[3] & (W - 1), 1)[0:1]


def halves(x):
    return [x[:, :H], x[:, H:]]


def turn_halves(x, amount):
    short = amount & (H - 1)
    lane = lax.broadcasted_iota(jnp.int32, (1, H), 1)
    cross = (lane < short) != ((amount & H) != 0)
    a, b = pltpu.roll(x[0], short, 1), pltpu.roll(x[1], short, 1)
    return [jnp.where(cross, b, a), jnp.where(cross, a, b)]


def rotate(upper, lower, coef, o):
    upper, lower = list(upper), turn_halves(lower, (-o[0]) & (W - 1))
    for step in range(4):
        for h in (0, 1):
            c = coef[step : step + 1, h * H : (h + 1) * H]
            s = coef[4 + step : 5 + step, h * H : (h + 1) * H]
            upper[h], lower[h] = c * upper[h] + s * lower[h], c * lower[h] - s * upper[h]
        turn = (o[step] - o[step + 1]) if step < 3 else o[3]
        lower = turn_halves(lower, turn & (W - 1))
    return upper, lower


SMEM = pl.BlockSpec(memory_space=pltpu.SMEM)
VMEM = pl.BlockSpec(memory_space=pltpu.VMEM)
ANY = pl.BlockSpec(memory_space=pl.ANY)
LAG_SHAPE = jax.ShapeDtypeStruct((LAGS, W), F32)
COEF_SHAPE = jax.ShapeDtypeStruct((16, W), F32)
ONEHOT_SHAPE = jax.ShapeDtypeStruct((LAGS, 2 * W), BF16)
TABLE = pltpu.VMEM((LAGS, 128), jnp.int32)


def tile_rows(rows, most=512):
    r = most
    while rows % r:
        r //= 2
    return r


def block(rows):
    return jax.ShapeDtypeStruct((rows, W), F32)


def call(kernel, name, in_specs, out_specs, out_shape, scratch=(), us=1, limit=VMEM_LIMIT):
    return pl.pallas_call(
        kernel,
        name=name,
        in_specs=in_specs,
        out_specs=out_specs,
        out_shape=out_shape,
        scratch_shapes=list(scratch),
        compiler_params=pltpu.CompilerParams(vmem_limit_bytes=limit),
        cost_estimate=pl.CostEstimate(flops=us * 10**9, bytes_accessed=us * 3 * 10**6, transcendentals=0),
    )


def offsets_of(o_ref, round_index):
    return [o_ref[round_index, j] for j in range(4)]


def pick(flag, a, b):
    return jnp.where(flag, a, b), jnp.where(flag, b, a)


def pick_halves(flag, a, b):
    pairs = [pick(flag, x, y) for x, y in zip(a, b)]
    return [x for x, _ in pairs], [y for _, y in pairs]


def read(ref, rows):
    return [ref[rows, :H], ref[rows, H:]]


def write(ref, rows, x):
    ref[rows, :H] = x[0]
    ref[rows, H:] = x[1]


def first_kernel(
    o_hbm, rows_hbm, cols_hbm, upper_ref, lower_ref, lag_ref, rows_ref, cols_ref, table_ref, norm_ref, o_ref, sem
):
    count, feat = cols_ref.shape
    total = rows_ref.shape[0]
    r = tile_rows(total)
    tiles = total // r
    half = count // 2
    fetch_cols = [
        pltpu.make_async_copy(cols_hbm.at[pl.ds(k * half, half)], cols_ref.at[pl.ds(k * half, half)], sem.at[k])
        for k in range(2)
    ]
    fetch_rows = [
        pltpu.make_async_copy(rows_hbm.at[pl.ds(t * r, r)], rows_ref.at[pl.ds(t * r, r)], sem.at[2 + t])
        for t in range(tiles)
    ]
    fetch_o = pltpu.make_async_copy(o_hbm, o_ref, sem.at[15])
    for copy in [fetch_o] + fetch_cols + fetch_rows:
        copy.start()
    fetch_o.wait()
    o = offsets_of(o_ref, 0)
    onehot = build_onehot(o, table_ref)
    for copy in fetch_cols:
        copy.wait()
    for t in range(tiles):
        fetch_rows[t].wait()
        if t == 0:
            for k in range(0, count, H):
                wide = cols_ref[k : k + H].astype(F32)
                sums = jnp.sum(wide * wide, axis=1, keepdims=True)
                norm_ref[:, k : k + H] = jnp.transpose(jnp.broadcast_to(sums, (H, H)))[0:8]
        part = slice(t * r, (t + 1) * r)
        rows = rows_ref[part]
        cross = lax.dot_general(rows, cols_ref[...], NT, preferred_element_type=F32)
        wide = rows.astype(F32)
        row_norm = jnp.sum(wide * wide, axis=1, keepdims=True)
        kernel = jnp.exp(
            -(0.25 / math.sqrt(feat)) * (row_norm + norm_ref[0:1] - 2.0 * cross - 2.0 * feat)
        )
        upper_ref[part] = kernel[:, :W]
        lower_ref[part] = kernel[:, W:]
    lag_products(gram_of(upper_ref[...], lower_ref[...]), o, onehot, lag_ref)


def first(offsets, row_feats, col_feats):
    rows, feat = row_feats.shape
    return call(
        first_kernel,
        "first",
        [ANY, ANY, ANY],
        (VMEM, VMEM, VMEM),
        (block(rows), block(rows), LAG_SHAPE),
        [
            pltpu.VMEM(row_feats.shape, BF16),
            pltpu.VMEM(col_feats.shape, BF16),
            TABLE,
            pltpu.VMEM((8, 2 * W), F32),
            pltpu.SMEM((3, 4), jnp.int32),
            pltpu.SemaphoreType.DMA((16,)),
        ],
        us=10,
        limit=FIRST_LIMIT,
    )(offsets, row_feats, col_feats)


def tables_kernel(o_ref, after_ref, one_ref, two_ref, table_ref):
    one_ref[...] = build_onehot(offsets_of(o_ref, 1), table_ref)
    two_ref[...] = build_onehot(offsets_of(o_ref, 2), table_ref)


def tables(offsets, after):
    return call(tables_kernel, "tables", [SMEM, ANY], (VMEM, VMEM), (ONEHOT_SHAPE, ONEHOT_SHAPE), [TABLE])(
        offsets, after
    )


def by_parts(total, go):
    part = total // 2
    r = tile_rows(part, 384)
    for k in range(2):

        @pl.loop(0, part // r)
        def _(i):
            start = pl.multiple_of(i * r, r)
            go(pl.ds(pl.multiple_of(k * part + i * r, r), r), k, pl.ds(start, r))


def turn_first_kernel(o_ref, p_ref, mine_ref, other_ref, a_ref, b_ref, xa, xb, x_ref, y_ref, coef_ref):
    p = p_ref[0]
    o = offsets_of(o_ref, 0)
    angles(mine_ref[...] + other_ref[...], o, coef_ref)
    coef = coef_ref[...]
    keep = ((p & 1) == 1) | (p == 0)

    def go(rows, k, rows_part):
        upper, lower = rotate(read(a_ref, rows), read(b_ref, rows), coef, o)
        x, y = pick_halves(keep, upper, lower)
        write((xa, xb)[k], rows_part, x)
        write(x_ref, rows, x)
        write(y_ref, rows, y)

    by_parts(a_ref.shape[0], go)


def turn_first(offsets, p, mine, other, a, b):
    rows = a.shape[0]
    part = block(rows // 2)
    return call(
        turn_first_kernel,
        "turn0",
        [SMEM, SMEM] + [VMEM] * 4,
        (VMEM,) * 5,
        (part, part, block(rows), block(rows), COEF_SHAPE),
        us=5,
    )(offsets, p, mine, other, a, b)


def pairs_start_kernel(p_ref, a_ref, b_ref, gram_ref):
    part = a_ref.shape[0]
    upper, lower = pick((p_ref[0] & 1) == 0, a_ref[...], b_ref[:part])
    gram_ref[...] = gram_of(upper, lower)


def pairs_start(p, a, b):
    return call(
        pairs_start_kernel, "pairs0", [SMEM, VMEM, VMEM], VMEM, jax.ShapeDtypeStruct((2 * W, 2 * W), F32), us=3
    )(p, a, b)


def pairs_kernel(o_ref, p_ref, hot_ref, gram_ref, a_ref, b_ref, lag_ref):
    part = a_ref.shape[0]
    upper, lower = pick((p_ref[0] & 1) == 0, a_ref[...], b_ref[part:])
    lag_products(gram_ref[...] + gram_of(upper, lower), offsets_of(o_ref, 1), hot_ref[...], lag_ref)


def pairs(offsets, p, hot, gram, a, b):
    return call(
        pairs_kernel, "pairs1", [SMEM, SMEM] + [VMEM] * 4, VMEM, LAG_SHAPE, us=20
    )(offsets, p, hot, gram, a, b)


def turn_second_kernel(o_ref, p_ref, coef_ref, rxa, rxb, sy_ref, z_ref, v_ref):
    p = p_ref[0]
    core = p & 1
    o = offsets_of(o_ref, 1)
    coef = coef_ref[...]

    def go(rows, k, rows_part):
        upper, lower = pick_halves(core == 0, read((rxa, rxb)[k], rows_part), read(sy_ref, rows))
        upper, lower = rotate(upper, lower, coef, o)
        z, v = pick_halves((core == 0) & (p != 0), upper, lower)
        write(z_ref, rows, z)
        write(v_ref, rows, v)

    by_parts(v_ref.shape[0], go)


def turn_second(offsets, p, coef, rxa, rxb, sy):
    whole = block(sy.shape[0])
    return call(
        turn_second_kernel, "turn1", [SMEM, SMEM] + [VMEM] * 4, (VMEM, VMEM), (whole, whole), us=8
    )(offsets, p, coef, rxa, rxb, sy)


def by_tiles(rows, go):
    r = tile_rows(rows)

    @pl.loop(0, rows // r)
    def _(i):
        go(pl.ds(pl.multiple_of(i * r, r), r))


def side_kernel(last, o_ref, p_ref, hot_ref, coef_ref, sx_ref, ry_ref, z_ref, q_ref, lag_ref):
    p = p_ref[0]
    core = p & 1
    o = offsets_of(o_ref, 1)
    coef = coef_ref[...]
    near_end = (p == 1) | (p == last - 1)

    def go(rows):
        upper, lower = pick_halves((core == 0) != near_end, read(sx_ref, rows), read(ry_ref, rows))
        upper, lower = rotate(upper, lower, coef, o)
        wanted, _ = pick_halves((core == 1) | (p == last - 1), upper, lower)
        write(q_ref, rows, wanted)

    by_tiles(sx_ref.shape[0], go)
    upper, lower = pick(core == 0, z_ref[...], q_ref[...])
    lag_products(gram_of(upper, lower), offsets_of(o_ref, 2), hot_ref[...], lag_ref)


def side(last, offsets, p, hot, coef, sx, ry, z):
    return call(
        functools.partial(side_kernel, last),
        "side",
        [SMEM, SMEM] + [VMEM] * 5,
        (VMEM, VMEM),
        (block(z.shape[0]), LAG_SHAPE),
        us=8,
    )(offsets, p, hot, coef, sx, ry, z)


def solve_kernel(round_index, o_ref, *refs):
    count = len(refs) // 3
    for k in range(count):
        angles(refs[2 * k][...] + refs[2 * k + 1][...], offsets_of(o_ref, round_index), refs[2 * count + k])


def solve(round_index, offsets, *lags):
    count = len(lags) // 2
    return call(
        functools.partial(solve_kernel, round_index),
        "solve%d" % round_index,
        [SMEM] + [VMEM] * len(lags),
        (VMEM,) * count,
        (COEF_SHAPE,) * count,
        us=2,
    )(offsets, *lags)


def own_kernel(o_ref, p_ref, coef_ref, z_ref, q_ref, out_ref):
    p = p_ref[0]
    core = p & 1
    o = offsets_of(o_ref, 2)
    coef = coef_ref[...]

    def go(rows):
        upper, lower = pick_halves(core == 0, read(z_ref, rows), read(q_ref, rows))
        upper, lower = rotate(upper, lower, coef, o)
        wanted, _ = pick_halves((core == 1) & (p != 1), upper, lower)
        write(out_ref, rows, [x * x for x in wanted])

    by_tiles(z_ref.shape[0], go)


def own(offsets, p, coef, z, q):
    return call(own_kernel, "own", [SMEM, SMEM] + [VMEM] * 3, VMEM, block(z.shape[0]), us=5)(
        offsets, p, coef, z, q
    )


def finish_kernel(
    last, row_total, o_ref, p_ref, coef_ref, a_ref, b_ref, c_ref, own_ref, r_ref, v_ref, out_hbm, norm_ref, e_ref, sem
):
    p = p_ref[0]
    core = p & 1
    o = offsets_of(o_ref, 2)
    keep = pltpu.make_async_copy(own_ref, out_hbm.at[1 - core], sem.at[0])
    keep.start()
    coef = coef_ref[...]
    for k, ref in enumerate((a_ref, b_ref, c_ref)):
        norm_ref[k] = ref[8:10, :] / row_total
    total = r_ref.shape[0]
    r = tile_rows(total)
    sends = []
    for t in range(total // r):
        rows = pl.ds(t * r, r)
        swap = (p == 0) | (p == last)
        upper, lower = pick_halves((core == 0) != swap, read(r_ref, rows), read(v_ref, rows))
        upper, lower = rotate(upper, lower, coef, o)
        wanted, _ = pick_halves((core == 0) | (p == last), upper, lower)
        write(e_ref, rows, [x * x for x in wanted])
        copy = pltpu.make_async_copy(e_ref.at[rows], out_hbm.at[core, rows], sem.at[1 + t])
        copy.start()
        sends.append(copy)
    for copy in [keep] + sends:
        copy.wait()


def finish(last, row_total, offsets, p, coef, coefs, own_block, r_block, v):
    rows = v.shape[0]
    return call(
        functools.partial(finish_kernel, last, row_total),
        "finish",
        [SMEM, SMEM] + [VMEM] * 7,
        (ANY, VMEM),
        (jax.ShapeDtypeStruct((2, rows, W), F32), jax.ShapeDtypeStruct((3, 2, W), F32)),
        [pltpu.VMEM((rows, W), F32), pltpu.SemaphoreType.DMA((16,))],
        us=5,
    )(offsets, p, coef, *coefs, own_block, r_block, v)


def body(row_feats, col_feats, offsets):
    n = lax.axis_size("blk")
    chips = n // 2
    p = lax.axis_index("blk").astype(jnp.int32).reshape(1)
    row_total = row_feats.shape[0] * lax.axis_size("row")
    across = [(0, 1), (1, 0)]
    sibling = [(i, i ^ 1) for i in range(n)]
    meet = [(2 * j + 1, 2 * j + 2) for j in range(chips - 1)] + [(2 * j, 2 * j - 1) for j in range(1, chips)]
    meet += [(0, 0), (n - 1, n - 1)]
    lend = [(2 * j, 2 * j + 3) for j in range(chips - 1)] + [(2 * j + 1, 2 * j - 2) for j in range(1, chips)]
    lend += [(1, 1), (n - 2, n - 2)]
    deal = [(2 * j, 2 * j + 2) for j in range(chips - 1)] + [(2 * j + 1, 2 * j - 1) for j in range(1, chips)]
    deal += [(1, 0), (n - 2, n - 1)]
    tell = [(2 * j, 2 * j - 2) for j in range(1, chips)] + [(2 * j + 1, 2 * j + 3) for j in range(chips - 1)]
    tell += [(0, 1), (n - 1, n - 2)]

    upper, lower, lag = first(offsets, row_feats, col_feats)
    lag_other = lax.ppermute(lag, "row", across)
    xa, xb, x, y, coef_a = turn_first(offsets, p, lag, lag_other, upper, lower)
    rxa = lax.ppermute(xa, "blk", meet)
    rxb = lax.ppermute(xb, "blk", meet)
    sy = lax.ppermute(y, "blk", sibling)
    sx = lax.ppermute(x, "blk", sibling)
    hot, hot_later = tables(offsets, coef_a)
    gram = pairs_start(p, rxa, sy)
    y, gram = lax.optimization_barrier((y, gram))
    ry = lax.ppermute(y, "blk", lend)
    lag = pairs(offsets, p, hot, gram, rxb, sy)
    lag_other = lax.ppermute(lag, "row", across)
    (coef_b,) = solve(1, offsets, lag, lag_other)
    coef_side = lax.ppermute(coef_b, "blk", tell)
    z, v = turn_second(offsets, p, coef_b, rxa, rxb, sy)
    z, coef_side = lax.optimization_barrier((z, coef_side))
    r_block = lax.ppermute(z, "blk", deal)
    q, lag = side(n - 1, offsets, p, hot_later, coef_side, sx, ry, z)
    lag_other = lax.ppermute(lag, "row", across)
    (coef_c,) = solve(2, offsets, lag, lag_other)
    coef_got = lax.ppermute(coef_c, "blk", deal)
    coef_norm = lax.ppermute(coef_c, "blk", sibling)
    own_block = own(offsets, p, coef_c, z, q)
    return finish(n - 1, row_total, offsets, p, coef_got, (coef_a, coef_b, coef_norm), own_block, r_block, v)


def solution(mesh):
    return jax.shard_map(
        body,
        mesh=mesh,
        in_specs=(P("row", None), P("blk", None), P()),
        out_specs=(P(None, "row", "blk"), P(None, None, "blk")),
        check_vma=False,
    )
```

```python
import functools
import math

import jax
import jax.numpy as jnp
from jax import lax
from jax.experimental import pallas as pl
from jax.experimental.pallas import tpu as pltpu
from jax.sharding import PartitionSpec as P

F32 = jnp.float32
BF16 = jnp.bfloat16
W = 256
H = 128
LAGS = 96
VMEM_LIMIT = 24 * 1024 * 1024
FIRST_LIMIT = 50 * 1024 * 1024


def group_rows(m):
    return (16 * m, 16) if m < 4 else (64 + 8 * (m - 4), 8)


def lag_targets(o):
    t, s = [0], [0]
    first, second = [0], [1]
    rows = {}
    for step in range(4):
        count = 1 << step
        for m in range(count):
            start, _ = group_rows(m)
            place = {3: 0, 2: 8, 1: 12, 0: 14}[step]
            for n in range(count):
                lag = (o[step] + s[n] - t[m]) & (W - 1)
                rows[start + place + n] = lag + W * second[n]
        if step < 3:
            t, s = t + [x + o[step] for x in s], s + [x - o[step] for x in t]
            first, second = first + second, second + first
    rows[15] = 0
    rows[16 + 14] = W
    return rows, t, first


def split(x):
    hi = x.astype(BF16)
    return hi, (x - hi.astype(F32)).astype(BF16)


TN = (((0,), (0,)), ((), ()))
NT = (((1,), (1,)), ((), ()))


def skew(x):
    row = lax.broadcasted_iota(jnp.int32, (W, W), 0)
    for bit in (1, 2, 4):
        x = jnp.where((row & bit) != 0, pltpu.roll(x, W - bit, 1), x)
    tiles = [pltpu.roll(x[8 * t : 8 * t + 8], (W - 8 * t) % W, 1) for t in range(W // 8)]
    return jnp.concatenate(tiles, axis=0)


def build_onehot(o, table_ref):
    rows, _, _ = lag_targets(o)
    table_ref[...] = jnp.full((LAGS, 128), -1, jnp.int32)
    for r, target in rows.items():
        table_ref[r : r + 1, :] = jnp.full((1, 128), target, jnp.int32)
    table = jnp.concatenate([table_ref[...]] * 4, axis=1)
    return (table == lax.broadcasted_iota(jnp.int32, (LAGS, 2 * W), 1)).astype(F32).astype(BF16)


def lag_products(gram, o, onehot, out_ref):
    _, bases, first = lag_targets(o)
    diags = {}
    for kind in (0, 1):
        sheets = [skew(gram[kind * W : (kind + 1) * W, side * W : (side + 1) * W]) for side in (0, 1)]
        hi, lo = split(jnp.concatenate(sheets, axis=1))
        diags[kind] = lax.dot_general(onehot, lo, NT, preferred_element_type=F32) + lax.dot_general(
            onehot, hi, NT, preferred_element_type=F32
        )
    for m in range(8):
        start, count = group_rows(m)
        tile = diags[first[m]][start : start + count]
        if m > 0:
            tile = pltpu.roll(tile, (-bases[m]) & (W - 1), 1)
        out_ref[start : start + count, :] = tile


def gram_of(a, b):
    hi, lo = split(jnp.concatenate([a, b], axis=1))
    return (
        lax.dot_general(hi, lo, TN, preferred_element_type=F32)
        + lax.dot_general(lo, hi, TN, preferred_element_type=F32)
        + lax.dot_general(hi, hi, TN, preferred_element_type=F32)
    )


def angle(g, upper_sq, lower_sq):
    twice = 2.0 * g
    diff = upper_sq - lower_sq
    scale = jnp.maximum(jnp.abs(twice), jnp.abs(diff))
    live = scale > 0.0
    safe = jnp.where(live, scale, 1.0)
    x = jnp.where(live, diff / safe, 1.0)
    y = jnp.where(live, twice / safe, 0.0)
    r = jnp.sqrt(x * x + y * y)
    big = jnp.sqrt(0.5 * (1.0 + jnp.abs(x) / r))
    small = 0.5 * jnp.abs(y) / (r * big)
    wide = x < 0.0
    c = jnp.where(wide, small, big)
    s = jnp.where(wide, big, small)
    s = jnp.where(y < 0.0, -s, s)
    cross = twice * c * s
    return c, s, c * c * upper_sq + cross + s * s * lower_sq, s * s * upper_sq - cross + c * c * lower_sq


def angles(lags, o, coef_ref):
    row = lax.broadcasted_iota(jnp.int32, (8, W), 0)
    a = jnp.ones((8, W), F32)
    b = jnp.ones((8, W), F32)
    upper_sq = lags[15:16]
    lower_sq = lags[30:31]
    tiles = [lags[16 * m + 8 : 16 * m + 16] for m in range(4)]
    last = [lags[group_rows(m)[0] : group_rows(m)[0] + 8] for m in range(8)]
    for step in range(4):
        count = 1 << step
        if step == 3:
            parts, place = last, 0
        else:
            parts, place = tiles[:count], (6, 4, 0)[step]
        acc = None
        for m in range(count):
            term = a[m : m + 1] * parts[m]
            acc = term if acc is None else acc + term
        view = pltpu.roll(b, place, 0) if place else b
        acc = jnp.where((row >= place) & (row < place + count), acc * view, 0.0)
        g = jnp.sum(acc, axis=0, keepdims=True)
        c, s, upper_sq, lower_sq = angle(g, upper_sq, lower_sq)
        coef_ref[step : step + 1, :] = c
        coef_ref[4 + step : 5 + step, :] = s
        if step < 3:
            shift_a, shift_b = pltpu.roll(a, count, 0), pltpu.roll(b, count, 0)
            a, b = jnp.where(row < count, c * a, s * shift_b), jnp.where(row < count, c * b, -s * shift_a)
            turn = (o[step] - o[step + 1]) & (W - 1)
            b = pltpu.roll(b, turn, 1)
            lower_sq = pltpu.roll(jnp.broadcast_to(lower_sq, (8, W)), turn, 1)[0:1]
    coef_ref[8:9, :] = upper_sq
    coef_ref[9:10, :] = pltpu.roll(jnp.broadcast_to(lower_sq, (8, W)), o[3] & (W - 1), 1)[0:1]


def halves(x):
    return [x[:, :H], x[:, H:]]


def turn_halves(x, amount):
    short = amount & (H - 1)
    lane = lax.broadcasted_iota(jnp.int32, (1, H), 1)
    cross = (lane < short) != ((amount & H) != 0)
    a, b = pltpu.roll(x[0], short, 1), pltpu.roll(x[1], short, 1)
    return [jnp.where(cross, b, a), jnp.where(cross, a, b)]


def rotate(upper, lower, coef, o):
    upper, lower = list(upper), turn_halves(lower, (-o[0]) & (W - 1))
    for step in range(4):
        for h in (0, 1):
            c = coef[step : step + 1, h * H : (h + 1) * H]
            s = coef[4 + step : 5 + step, h * H : (h + 1) * H]
            upper[h], lower[h] = c * upper[h] + s * lower[h], c * lower[h] - s * upper[h]
        turn = (o[step] - o[step + 1]) if step < 3 else o[3]
        lower = turn_halves(lower, turn & (W - 1))
    return upper, lower


SMEM = pl.BlockSpec(memory_space=pltpu.SMEM)
VMEM = pl.BlockSpec(memory_space=pltpu.VMEM)
ANY = pl.BlockSpec(memory_space=pl.ANY)
LAG_SHAPE = jax.ShapeDtypeStruct((LAGS, W), F32)
COEF_SHAPE = jax.ShapeDtypeStruct((16, W), F32)
ONEHOT_SHAPE = jax.ShapeDtypeStruct((LAGS, 2 * W), BF16)
TABLE = pltpu.VMEM((LAGS, 128), jnp.int32)


def tile_rows(rows, most=512):
    r = most
    while rows % r:
        r //= 2
    return r


def block(rows):
    return jax.ShapeDtypeStruct((rows, W), F32)


def call(kernel, name, in_specs, out_specs, out_shape, scratch=(), us=1, limit=VMEM_LIMIT):
    return pl.pallas_call(
        kernel,
        name=name,
        in_specs=in_specs,
        out_specs=out_specs,
        out_shape=out_shape,
        scratch_shapes=list(scratch),
        compiler_params=pltpu.CompilerParams(vmem_limit_bytes=limit),
        cost_estimate=pl.CostEstimate(flops=us * 10**9, bytes_accessed=us * 3 * 10**6, transcendentals=0),
    )


def offsets_of(o_ref, round_index):
    return [o_ref[round_index, j] for j in range(4)]


def pick(flag, a, b):
    return jnp.where(flag, a, b), jnp.where(flag, b, a)


def pick_halves(flag, a, b):
    pairs = [pick(flag, x, y) for x, y in zip(a, b)]
    return [x for x, _ in pairs], [y for _, y in pairs]


def read(ref, rows):
    return [ref[rows, :H], ref[rows, H:]]


def write(ref, rows, x):
    ref[rows, :H] = x[0]
    ref[rows, H:] = x[1]


def first_kernel(
    o_hbm, rows_hbm, cols_hbm, upper_ref, lower_ref, lag_ref, rows_ref, cols_ref, table_ref, norm_ref, o_ref, sem
):
    count, feat = cols_ref.shape
    total = rows_ref.shape[0]
    r = tile_rows(total)
    tiles = total // r
    half = count // 2
    fetch_cols = [
        pltpu.make_async_copy(cols_hbm.at[pl.ds(k * half, half)], cols_ref.at[pl.ds(k * half, half)], sem.at[k])
        for k in range(2)
    ]
    fetch_rows = [
        pltpu.make_async_copy(rows_hbm.at[pl.ds(t * r, r)], rows_ref.at[pl.ds(t * r, r)], sem.at[2 + t])
        for t in range(tiles)
    ]
    fetch_o = pltpu.make_async_copy(o_hbm, o_ref, sem.at[15])
    for copy in [fetch_o] + fetch_cols + fetch_rows:
        copy.start()
    fetch_o.wait()
    o = offsets_of(o_ref, 0)
    onehot = build_onehot(o, table_ref)
    for copy in fetch_cols:
        copy.wait()
    for t in range(tiles):
        fetch_rows[t].wait()
        if t == 0:
            for k in range(0, count, H):
                wide = cols_ref[k : k + H].astype(F32)
                sums = jnp.sum(wide * wide, axis=1, keepdims=True)
                norm_ref[:, k : k + H] = jnp.transpose(jnp.broadcast_to(sums, (H, H)))[0:8]
        part = slice(t * r, (t + 1) * r)
        rows = rows_ref[part]
        cross = lax.dot_general(rows, cols_ref[...], NT, preferred_element_type=F32)
        wide = rows.astype(F32)
        row_norm = jnp.sum(wide * wide, axis=1, keepdims=True)
        kernel = jnp.exp(
            -(0.25 / math.sqrt(feat)) * (row_norm + norm_ref[0:1] - 2.0 * cross - 2.0 * feat)
        )
        upper_ref[part] = kernel[:, :W]
        lower_ref[part] = kernel[:, W:]
    lag_products(gram_of(upper_ref[...], lower_ref[...]), o, onehot, lag_ref)


def first(offsets, row_feats, col_feats):
    rows, feat = row_feats.shape
    return call(
        first_kernel,
        "first",
        [ANY, ANY, ANY],
        (VMEM, VMEM, VMEM),
        (block(rows), block(rows), LAG_SHAPE),
        [
            pltpu.VMEM(row_feats.shape, BF16),
            pltpu.VMEM(col_feats.shape, BF16),
            TABLE,
            pltpu.VMEM((8, 2 * W), F32),
            pltpu.SMEM((3, 4), jnp.int32),
            pltpu.SemaphoreType.DMA((16,)),
        ],
        us=10,
        limit=FIRST_LIMIT,
    )(offsets, row_feats, col_feats)


def tables_kernel(o_ref, after_ref, one_ref, two_ref, table_ref):
    one_ref[...] = build_onehot(offsets_of(o_ref, 1), table_ref)
    two_ref[...] = build_onehot(offsets_of(o_ref, 2), table_ref)


def tables(offsets, after):
    return call(tables_kernel, "tables", [SMEM, ANY], (VMEM, VMEM), (ONEHOT_SHAPE, ONEHOT_SHAPE), [TABLE])(
        offsets, after
    )


def by_parts(total, go):
    part = total // 2
    r = tile_rows(part, 384)
    for k in range(2):

        @pl.loop(0, part // r)
        def _(i):
            start = pl.multiple_of(i * r, r)
            go(pl.ds(pl.multiple_of(k * part + i * r, r), r), k, pl.ds(start, r))


def turn_first_kernel(o_ref, p_ref, mine_ref, other_ref, a_ref, b_ref, xa, xb, x_ref, y_ref, coef_ref):
    p = p_ref[0]
    o = offsets_of(o_ref, 0)
    angles(mine_ref[...] + other_ref[...], o, coef_ref)
    coef = coef_ref[...]
    keep = ((p & 1) == 1) | (p == 0)

    def go(rows, k, rows_part):
        upper, lower = rotate(read(a_ref, rows), read(b_ref, rows), coef, o)
        x, y = pick_halves(keep, upper, lower)
        write((xa, xb)[k], rows_part, x)
        write(x_ref, rows, x)
        write(y_ref, rows, y)

    by_parts(a_ref.shape[0], go)


def turn_first(offsets, p, mine, other, a, b):
    rows = a.shape[0]
    part = block(rows // 2)
    return call(
        turn_first_kernel,
        "turn0",
        [SMEM, SMEM] + [VMEM] * 4,
        (VMEM,) * 5,
        (part, part, block(rows), block(rows), COEF_SHAPE),
        us=5,
    )(offsets, p, mine, other, a, b)


def pairs_start_kernel(p_ref, a_ref, b_ref, gram_ref):
    part = a_ref.shape[0]
    upper, lower = pick((p_ref[0] & 1) == 0, a_ref[...], b_ref[:part])
    gram_ref[...] = gram_of(upper, lower)


def pairs_start(p, a, b):
    return call(
        pairs_start_kernel, "pairs0", [SMEM, VMEM, VMEM], VMEM, jax.ShapeDtypeStruct((2 * W, 2 * W), F32), us=3
    )(p, a, b)


def pairs_kernel(o_ref, p_ref, hot_ref, gram_ref, a_ref, b_ref, lag_ref):
    part = a_ref.shape[0]
    upper, lower = pick((p_ref[0] & 1) == 0, a_ref[...], b_ref[part:])
    lag_products(gram_ref[...] + gram_of(upper, lower), offsets_of(o_ref, 1), hot_ref[...], lag_ref)


def pairs(offsets, p, hot, gram, a, b):
    return call(
        pairs_kernel, "pairs1", [SMEM, SMEM] + [VMEM] * 4, VMEM, LAG_SHAPE, us=20
    )(offsets, p, hot, gram, a, b)


def turn_second_kernel(o_ref, p_ref, coef_ref, rxa, rxb, sy_ref, z_ref, v_ref):
    p = p_ref[0]
    core = p & 1
    o = offsets_of(o_ref, 1)
    coef = coef_ref[...]

    def go(rows, k, rows_part):
        upper, lower = pick_halves(core == 0, read((rxa, rxb)[k], rows_part), read(sy_ref, rows))
        upper, lower = rotate(upper, lower, coef, o)
        z, v = pick_halves((core == 0) & (p != 0), upper, lower)
        write(z_ref, rows, z)
        write(v_ref, rows, v)

    by_parts(v_ref.shape[0], go)


def turn_second(offsets, p, coef, rxa, rxb, sy):
    whole = block(sy.shape[0])
    return call(
        turn_second_kernel, "turn1", [SMEM, SMEM] + [VMEM] * 4, (VMEM, VMEM), (whole, whole), us=8
    )(offsets, p, coef, rxa, rxb, sy)


def by_tiles(rows, go):
    r = tile_rows(rows)

    @pl.loop(0, rows // r)
    def _(i):
        go(pl.ds(pl.multiple_of(i * r, r), r))


def side_kernel(last, o_ref, p_ref, hot_ref, coef_ref, sx_ref, ry_ref, z_ref, q_ref, lag_ref):
    p = p_ref[0]
    core = p & 1
    o = offsets_of(o_ref, 1)
    coef = coef_ref[...]
    near_end = (p == 1) | (p == last - 1)

    def go(rows):
        upper, lower = pick_halves((core == 0) != near_end, read(sx_ref, rows), read(ry_ref, rows))
        upper, lower = rotate(upper, lower, coef, o)
        wanted, _ = pick_halves((core == 1) | (p == last - 1), upper, lower)
        write(q_ref, rows, wanted)

    by_tiles(sx_ref.shape[0], go)
    upper, lower = pick(core == 0, z_ref[...], q_ref[...])
    lag_products(gram_of(upper, lower), offsets_of(o_ref, 2), hot_ref[...], lag_ref)


def side(last, offsets, p, hot, coef, sx, ry, z):
    return call(
        functools.partial(side_kernel, last),
        "side",
        [SMEM, SMEM] + [VMEM] * 5,
        (VMEM, VMEM),
        (block(z.shape[0]), LAG_SHAPE),
        us=8,
    )(offsets, p, hot, coef, sx, ry, z)


def solve_kernel(round_index, o_ref, mine_ref, direct_ref, relayed_ref, coef_ref):
    lags = mine_ref[...] + direct_ref[...] + relayed_ref[...]
    angles(lags, offsets_of(o_ref, round_index), coef_ref)


def solve(round_index, offsets, mine, direct, relayed):
    return call(
        functools.partial(solve_kernel, round_index),
        "solve%d" % round_index,
        [SMEM] + [VMEM] * 3,
        VMEM,
        COEF_SHAPE,
        us=2,
    )(offsets, mine, direct, relayed)


def own_kernel(o_ref, p_ref, coef_ref, z_ref, q_ref, out_ref):
    p = p_ref[0]
    core = p & 1
    o = offsets_of(o_ref, 2)
    coef = coef_ref[...]

    def go(rows):
        upper, lower = pick_halves(core == 0, read(z_ref, rows), read(q_ref, rows))
        upper, lower = rotate(upper, lower, coef, o)
        wanted, _ = pick_halves((core == 1) & (p != 1), upper, lower)
        write(out_ref, rows, [x * x for x in wanted])

    by_tiles(z_ref.shape[0], go)


def own(offsets, p, coef, z, q):
    return call(own_kernel, "own", [SMEM, SMEM] + [VMEM] * 3, VMEM, block(z.shape[0]), us=5)(
        offsets, p, coef, z, q
    )


def finish_kernel(
    last, row_total, o_ref, p_ref, coef_ref, a_ref, b_ref, c_ref, own_ref, r_ref, v_ref, out_hbm, norm_ref, e_ref, sem
):
    p = p_ref[0]
    core = p & 1
    o = offsets_of(o_ref, 2)
    keep = pltpu.make_async_copy(own_ref, out_hbm.at[1 - core], sem.at[0])
    keep.start()
    coef = coef_ref[...]
    for k, ref in enumerate((a_ref, b_ref, c_ref)):
        norm_ref[k] = ref[8:10, :] / row_total
    total = r_ref.shape[0]
    r = tile_rows(total)
    sends = []
    for t in range(total // r):
        rows = pl.ds(t * r, r)
        swap = (p == 0) | (p == last)
        upper, lower = pick_halves((core == 0) != swap, read(r_ref, rows), read(v_ref, rows))
        upper, lower = rotate(upper, lower, coef, o)
        wanted, _ = pick_halves((core == 0) | (p == last), upper, lower)
        write(e_ref, rows, [x * x for x in wanted])
        copy = pltpu.make_async_copy(e_ref.at[rows], out_hbm.at[core, rows], sem.at[1 + t])
        copy.start()
        sends.append(copy)
    for copy in [keep] + sends:
        copy.wait()


def finish(last, row_total, offsets, p, coef, coefs, own_block, r_block, v):
    rows = v.shape[0]
    return call(
        functools.partial(finish_kernel, last, row_total),
        "finish",
        [SMEM, SMEM] + [VMEM] * 7,
        (ANY, VMEM),
        (jax.ShapeDtypeStruct((2, rows, W), F32), jax.ShapeDtypeStruct((3, 2, W), F32)),
        [pltpu.VMEM((rows, W), F32), pltpu.SemaphoreType.DMA((16,))],
        us=5,
    )(offsets, p, coef, *coefs, own_block, r_block, v)


def body(row_feats, col_feats, offsets):
    n = lax.axis_size("blk")
    chips = n // 2
    p = lax.axis_index("blk").astype(jnp.int32).reshape(1)
    row_total = row_feats.shape[0] * lax.axis_size("row")
    across = [(0, 1), (1, 0)]
    sibling = [(i, i ^ 1) for i in range(n)]
    meet = [(2 * j + 1, 2 * j + 2) for j in range(chips - 1)] + [(2 * j, 2 * j - 1) for j in range(1, chips)]
    meet += [(0, 0), (n - 1, n - 1)]
    lend = [(2 * j, 2 * j + 3) for j in range(chips - 1)] + [(2 * j + 1, 2 * j - 2) for j in range(1, chips)]
    lend += [(1, 1), (n - 2, n - 2)]
    deal = [(2 * j, 2 * j + 2) for j in range(chips - 1)] + [(2 * j + 1, 2 * j - 1) for j in range(1, chips)]
    deal += [(1, 0), (n - 2, n - 1)]
    tell = [(2 * j, 2 * j - 2) for j in range(1, chips)] + [(2 * j + 1, 2 * j + 3) for j in range(chips - 1)]
    tell += [(0, 1), (n - 1, n - 2)]

    busy = [i for i in range(n) if i % 8 in (1, 6)]
    hand = [(i, i ^ 1) for i in busy]
    free = [(2 * i + r, 2 * i + 1 - r) for i in range(n) if i not in busy for r in (0, 1)]
    relay = [(2 * (i ^ 1) + r, 2 * i + 1 - r) for i in busy for r in (0, 1)]

    def swap(lag):
        handed = lax.ppermute(lag, "blk", hand)
        lag, handed = lax.optimization_barrier((lag, handed))
        return lag, lax.ppermute(lag, ("blk", "row"), free), lax.ppermute(handed, ("blk", "row"), relay)

    upper, lower, lag = first(offsets, row_feats, col_feats)
    lag_other = lax.ppermute(lag, "row", across)
    xa, xb, x, y, coef_a = turn_first(offsets, p, lag, lag_other, upper, lower)
    rxa = lax.ppermute(xa, "blk", meet)
    rxb = lax.ppermute(xb, "blk", meet)
    sy = lax.ppermute(y, "blk", sibling)
    sx = lax.ppermute(x, "blk", sibling)
    hot, hot_later = tables(offsets, coef_a)
    gram = pairs_start(p, rxa, sy)
    y, gram = lax.optimization_barrier((y, gram))
    ry = lax.ppermute(y, "blk", lend)
    lag = pairs(offsets, p, hot, gram, rxb, sy)
    coef_b = solve(1, offsets, *swap(lag))
    coef_side = lax.ppermute(coef_b, "blk", tell)
    z, v = turn_second(offsets, p, coef_b, rxa, rxb, sy)
    z, coef_side = lax.optimization_barrier((z, coef_side))
    r_block = lax.ppermute(z, "blk", deal)
    q, lag = side(n - 1, offsets, p, hot_later, coef_side, sx, ry, z)
    coef_c = solve(2, offsets, *swap(lag))
    coef_got = lax.ppermute(coef_c, "blk", deal)
    coef_norm = lax.ppermute(coef_c, "blk", sibling)
    own_block = own(offsets, p, coef_c, z, q)
    return finish(n - 1, row_total, offsets, p, coef_got, (coef_a, coef_b, coef_norm), own_block, r_block, v)


def solution(mesh):
    return jax.shard_map(
        body,
        mesh=mesh,
        in_specs=(P("row", None), P("blk", None), P()),
        out_specs=(P(None, "row", "blk"), P(None, None, "blk")),
        check_vma=False,
    )
```

```python
import functools
import math

import jax
import jax.numpy as jnp
from jax import lax
from jax.experimental import pallas as pl
from jax.experimental.pallas import tpu as pltpu
from jax.sharding import PartitionSpec as P

F32 = jnp.float32
BF16 = jnp.bfloat16
W = 256
H = 128
LAGS = 96
VMEM_LIMIT = 24 * 1024 * 1024
FIRST_LIMIT = 50 * 1024 * 1024


def group_rows(m):
    return (16 * m, 16) if m < 4 else (64 + 8 * (m - 4), 8)


def lag_targets(o):
    t, s = [0], [0]
    first, second = [0], [1]
    rows = {}
    for step in range(4):
        count = 1 << step
        for m in range(count):
            start, _ = group_rows(m)
            place = {3: 0, 2: 8, 1: 12, 0: 14}[step]
            for n in range(count):
                lag = (o[step] + s[n] - t[m]) & (W - 1)
                rows[start + place + n] = lag + W * second[n]
        if step < 3:
            t, s = t + [x + o[step] for x in s], s + [x - o[step] for x in t]
            first, second = first + second, second + first
    rows[15] = 0
    rows[16 + 14] = W
    return rows, t, first


def split(x):
    hi = x.astype(BF16)
    return hi, (x - hi.astype(F32)).astype(BF16)


TN = (((0,), (0,)), ((), ()))
NT = (((1,), (1,)), ((), ()))


def skew(x):
    row = lax.broadcasted_iota(jnp.int32, (W, W), 0)
    for bit in (1, 2, 4):
        x = jnp.where((row & bit) != 0, pltpu.roll(x, W - bit, 1), x)
    tiles = [pltpu.roll(x[8 * t : 8 * t + 8], (W - 8 * t) % W, 1) for t in range(W // 8)]
    return jnp.concatenate(tiles, axis=0)


def build_onehot(o, table_ref):
    rows, _, _ = lag_targets(o)
    table_ref[...] = jnp.full((LAGS, 128), -1, jnp.int32)
    for r, target in rows.items():
        table_ref[r : r + 1, :] = jnp.full((1, 128), target, jnp.int32)
    table = jnp.concatenate([table_ref[...]] * 4, axis=1)
    return (table == lax.broadcasted_iota(jnp.int32, (LAGS, 2 * W), 1)).astype(F32).astype(BF16)


def lag_products(gram, o, onehot, out_ref):
    _, bases, first = lag_targets(o)
    diags = {}
    for kind in (0, 1):
        sheets = [skew(gram[kind * W : (kind + 1) * W, side * W : (side + 1) * W]) for side in (0, 1)]
        hi, lo = split(jnp.concatenate(sheets, axis=1))
        diags[kind] = lax.dot_general(onehot, lo, NT, preferred_element_type=F32) + lax.dot_general(
            onehot, hi, NT, preferred_element_type=F32
        )
    for m in range(8):
        start, count = group_rows(m)
        tile = diags[first[m]][start : start + count]
        if m > 0:
            tile = pltpu.roll(tile, (-bases[m]) & (W - 1), 1)
        out_ref[start : start + count, :] = tile


def gram_of(a, b):
    hi, lo = split(jnp.concatenate([a, b], axis=1))
    return (
        lax.dot_general(hi, lo, TN, preferred_element_type=F32)
        + lax.dot_general(lo, hi, TN, preferred_element_type=F32)
        + lax.dot_general(hi, hi, TN, preferred_element_type=F32)
    )


def angle(g, upper_sq, lower_sq):
    twice = 2.0 * g
    diff = upper_sq - lower_sq
    scale = jnp.maximum(jnp.abs(twice), jnp.abs(diff))
    live = scale > 0.0
    safe = jnp.where(live, scale, 1.0)
    x = jnp.where(live, diff / safe, 1.0)
    y = jnp.where(live, twice / safe, 0.0)
    r = jnp.sqrt(x * x + y * y)
    big = jnp.sqrt(0.5 * (1.0 + jnp.abs(x) / r))
    small = 0.5 * jnp.abs(y) / (r * big)
    wide = x < 0.0
    c = jnp.where(wide, small, big)
    s = jnp.where(wide, big, small)
    s = jnp.where(y < 0.0, -s, s)
    cross = twice * c * s
    return c, s, c * c * upper_sq + cross + s * s * lower_sq, s * s * upper_sq - cross + c * c * lower_sq


def angles(lags, o, coef_ref):
    row = lax.broadcasted_iota(jnp.int32, (8, W), 0)
    a = jnp.ones((8, W), F32)
    b = jnp.ones((8, W), F32)
    upper_sq = lags[15:16]
    lower_sq = lags[30:31]
    tiles = [lags[16 * m + 8 : 16 * m + 16] for m in range(4)]
    last = [lags[group_rows(m)[0] : group_rows(m)[0] + 8] for m in range(8)]
    for step in range(4):
        count = 1 << step
        if step == 3:
            parts, place = last, 0
        else:
            parts, place = tiles[:count], (6, 4, 0)[step]
        acc = None
        for m in range(count):
            term = a[m : m + 1] * parts[m]
            acc = term if acc is None else acc + term
        view = pltpu.roll(b, place, 0) if place else b
        acc = jnp.where((row >= place) & (row < place + count), acc * view, 0.0)
        g = jnp.sum(acc, axis=0, keepdims=True)
        c, s, upper_sq, lower_sq = angle(g, upper_sq, lower_sq)
        coef_ref[step : step + 1, :] = c
        coef_ref[4 + step : 5 + step, :] = s
        if step < 3:
            shift_a, shift_b = pltpu.roll(a, count, 0), pltpu.roll(b, count, 0)
            a, b = jnp.where(row < count, c * a, s * shift_b), jnp.where(row < count, c * b, -s * shift_a)
            turn = (o[step] - o[step + 1]) & (W - 1)
            b = pltpu.roll(b, turn, 1)
            lower_sq = pltpu.roll(jnp.broadcast_to(lower_sq, (8, W)), turn, 1)[0:1]
    coef_ref[8:9, :] = upper_sq
    coef_ref[9:10, :] = pltpu.roll(jnp.broadcast_to(lower_sq, (8, W)), o[3] & (W - 1), 1)[0:1]


def halves(x):
    return [x[:, :H], x[:, H:]]


def turn_halves(x, amount):
    short = amount & (H - 1)
    lane = lax.broadcasted_iota(jnp.int32, (1, H), 1)
    cross = (lane < short) != ((amount & H) != 0)
    a, b = pltpu.roll(x[0], short, 1), pltpu.roll(x[1], short, 1)
    return [jnp.where(cross, b, a), jnp.where(cross, a, b)]


def rotate(upper, lower, coef, o):
    upper, lower = list(upper), turn_halves(lower, (-o[0]) & (W - 1))
    for step in range(4):
        for h in (0, 1):
            c = coef[step : step + 1, h * H : (h + 1) * H]
            s = coef[4 + step : 5 + step, h * H : (h + 1) * H]
            upper[h], lower[h] = c * upper[h] + s * lower[h], c * lower[h] - s * upper[h]
        turn = (o[step] - o[step + 1]) if step < 3 else o[3]
        lower = turn_halves(lower, turn & (W - 1))
    return upper, lower


SMEM = pl.BlockSpec(memory_space=pltpu.SMEM)
VMEM = pl.BlockSpec(memory_space=pltpu.VMEM)
ANY = pl.BlockSpec(memory_space=pl.ANY)
LAG_SHAPE = jax.ShapeDtypeStruct((LAGS, W), F32)
COEF_SHAPE = jax.ShapeDtypeStruct((16, W), F32)
ONEHOT_SHAPE = jax.ShapeDtypeStruct((LAGS, 2 * W), BF16)
TABLE = pltpu.VMEM((LAGS, 128), jnp.int32)


def tile_rows(rows, most=512):
    r = most
    while rows % r:
        r //= 2
    return r


def block(rows):
    return jax.ShapeDtypeStruct((rows, W), F32)


def call(kernel, name, in_specs, out_specs, out_shape, scratch=(), us=1, limit=VMEM_LIMIT):
    return pl.pallas_call(
        kernel,
        name=name,
        in_specs=in_specs,
        out_specs=out_specs,
        out_shape=out_shape,
        scratch_shapes=list(scratch),
        compiler_params=pltpu.CompilerParams(vmem_limit_bytes=limit),
        cost_estimate=pl.CostEstimate(flops=us * 10**9, bytes_accessed=us * 3 * 10**6, transcendentals=0),
    )


def offsets_of(o_ref, round_index):
    return [o_ref[round_index, j] for j in range(4)]


def pick(flag, a, b):
    return jnp.where(flag, a, b), jnp.where(flag, b, a)


def pick_halves(flag, a, b):
    pairs = [pick(flag, x, y) for x, y in zip(a, b)]
    return [x for x, _ in pairs], [y for _, y in pairs]


def read(ref, rows):
    return [ref[rows, :H], ref[rows, H:]]


def write(ref, rows, x):
    ref[rows, :H] = x[0]
    ref[rows, H:] = x[1]


def first_kernel(
    o_hbm, rows_hbm, cols_hbm, upper_ref, lower_ref, lag_ref, rows_ref, cols_ref, table_ref, norm_ref, o_ref, sem
):
    count, feat = cols_ref.shape
    total = rows_ref.shape[0]
    r = tile_rows(total)
    tiles = total // r
    half = count // 2
    fetch_cols = [
        pltpu.make_async_copy(cols_hbm.at[pl.ds(k * half, half)], cols_ref.at[pl.ds(k * half, half)], sem.at[k])
        for k in range(2)
    ]
    fetch_rows = [
        pltpu.make_async_copy(rows_hbm.at[pl.ds(t * r, r)], rows_ref.at[pl.ds(t * r, r)], sem.at[2 + t])
        for t in range(tiles)
    ]
    fetch_o = pltpu.make_async_copy(o_hbm, o_ref, sem.at[15])
    for copy in [fetch_o] + fetch_cols + fetch_rows:
        copy.start()
    fetch_o.wait()
    o = offsets_of(o_ref, 0)
    onehot = build_onehot(o, table_ref)
    for copy in fetch_cols:
        copy.wait()
    for t in range(tiles):
        fetch_rows[t].wait()
        if t == 0:
            for k in range(0, count, H):
                wide = cols_ref[k : k + H].astype(F32)
                sums = jnp.sum(wide * wide, axis=1, keepdims=True)
                norm_ref[:, k : k + H] = jnp.transpose(jnp.broadcast_to(sums, (H, H)))[0:8]
        part = slice(t * r, (t + 1) * r)
        rows = rows_ref[part]
        cross = lax.dot_general(rows, cols_ref[...], NT, preferred_element_type=F32)
        wide = rows.astype(F32)
        row_norm = jnp.sum(wide * wide, axis=1, keepdims=True)
        kernel = jnp.exp(
            -(0.25 / math.sqrt(feat)) * (row_norm + norm_ref[0:1] - 2.0 * cross - 2.0 * feat)
        )
        upper_ref[part] = kernel[:, :W]
        lower_ref[part] = kernel[:, W:]
    lag_products(gram_of(upper_ref[...], lower_ref[...]), o, onehot, lag_ref)


def first(offsets, row_feats, col_feats):
    rows, feat = row_feats.shape
    return call(
        first_kernel,
        "first",
        [ANY, ANY, ANY],
        (VMEM, VMEM, VMEM),
        (block(rows), block(rows), LAG_SHAPE),
        [
            pltpu.VMEM(row_feats.shape, BF16),
            pltpu.VMEM(col_feats.shape, BF16),
            TABLE,
            pltpu.VMEM((8, 2 * W), F32),
            pltpu.SMEM((3, 4), jnp.int32),
            pltpu.SemaphoreType.DMA((16,)),
        ],
        us=10,
        limit=FIRST_LIMIT,
    )(offsets, row_feats, col_feats)


def table_kernel(round_index, o_ref, after_ref, out_ref, table_ref):
    out_ref[...] = build_onehot(offsets_of(o_ref, round_index), table_ref)


def table(round_index, offsets, after):
    return call(
        functools.partial(table_kernel, round_index), "table%d" % round_index, [SMEM, ANY], VMEM, ONEHOT_SHAPE, [TABLE]
    )(offsets, after)


def by_parts(total, go):
    part = total // 2
    r = tile_rows(part, 384)
    for k in range(2):

        @pl.loop(0, part // r)
        def _(i):
            start = pl.multiple_of(i * r, r)
            go(pl.ds(pl.multiple_of(k * part + i * r, r), r), k, pl.ds(start, r))


def turn_first_kernel(o_ref, p_ref, mine_ref, other_ref, a_ref, b_ref, xa, xb, ya, yb, coef_ref):
    p = p_ref[0]
    o = offsets_of(o_ref, 0)
    angles(mine_ref[...] + other_ref[...], o, coef_ref)
    coef = coef_ref[...]
    keep = ((p & 1) == 1) | (p == 0)

    def go(rows, k, rows_part):
        upper, lower = rotate(read(a_ref, rows), read(b_ref, rows), coef, o)
        x, y = pick_halves(keep, upper, lower)
        write((xa, xb)[k], rows_part, x)
        write((ya, yb)[k], rows_part, y)

    by_parts(a_ref.shape[0], go)


def turn_first(offsets, p, mine, other, a, b):
    rows = a.shape[0]
    part = block(rows // 2)
    return call(
        turn_first_kernel,
        "turn0",
        [SMEM, SMEM] + [VMEM] * 4,
        (VMEM,) * 5,
        (part, part, part, part, COEF_SHAPE),
        us=5,
    )(offsets, p, mine, other, a, b)


def pairs_start_kernel(p_ref, a_ref, b_ref, gram_ref):
    upper, lower = pick((p_ref[0] & 1) == 0, a_ref[...], b_ref[...])
    gram_ref[...] = gram_of(upper, lower)


def pairs_start(p, a, b):
    return call(
        pairs_start_kernel, "pairs0", [SMEM, VMEM, VMEM], VMEM, jax.ShapeDtypeStruct((2 * W, 2 * W), F32), us=3
    )(p, a, b)


def pairs_kernel(o_ref, p_ref, hot_ref, gram_ref, a_ref, b_ref, lag_ref):
    upper, lower = pick((p_ref[0] & 1) == 0, a_ref[...], b_ref[...])
    lag_products(gram_ref[...] + gram_of(upper, lower), offsets_of(o_ref, 1), hot_ref[...], lag_ref)


def pairs(offsets, p, hot, gram, a, b):
    return call(
        pairs_kernel, "pairs1", [SMEM, SMEM] + [VMEM] * 4, VMEM, LAG_SHAPE, us=4
    )(offsets, p, hot, gram, a, b)


def turn_second_kernel(o_ref, p_ref, coef_ref, rxa, rxb, sya, syb, za, zb, v_ref):
    p = p_ref[0]
    core = p & 1
    o = offsets_of(o_ref, 1)
    coef = coef_ref[...]

    def go(rows, k, rows_part):
        upper, lower = pick_halves(core == 0, read((rxa, rxb)[k], rows_part), read((sya, syb)[k], rows_part))
        upper, lower = rotate(upper, lower, coef, o)
        z, v = pick_halves((core == 0) & (p != 0), upper, lower)
        write((za, zb)[k], rows_part, z)
        write(v_ref, rows, v)

    by_parts(v_ref.shape[0], go)


def turn_second(offsets, p, coef, rxa, rxb, sya, syb):
    rows = rxa.shape[0] * 2
    part = block(rows // 2)
    return call(
        turn_second_kernel,
        "turn1",
        [SMEM, SMEM] + [VMEM] * 5,
        (VMEM,) * 3,
        (part, part, block(rows)),
        us=40,
    )(offsets, p, coef, rxa, rxb, sya, syb)


def side_kernel(last, o_ref, p_ref, hot_ref, coef_ref, sxa, sxb, rya, ryb, za, zb, q_ref, lag_ref):
    p = p_ref[0]
    core = p & 1
    o = offsets_of(o_ref, 1)
    coef = coef_ref[...]
    near_end = (p == 1) | (p == last - 1)
    part = za.shape[0]

    def go(rows, k, rows_part):
        upper, lower = pick_halves(
            (core == 0) != near_end, read((sxa, sxb)[k], rows_part), read((rya, ryb)[k], rows_part)
        )
        upper, lower = rotate(upper, lower, coef, o)
        wanted, _ = pick_halves((core == 1) | (p == last - 1), upper, lower)
        write(q_ref, rows, wanted)

    by_parts(q_ref.shape[0], go)
    z = jnp.concatenate([za[...], zb[...]], axis=0)
    upper, lower = pick(core == 0, z, q_ref[...])
    lag_products(gram_of(upper, lower), offsets_of(o_ref, 2), hot_ref[...], lag_ref)


def side(last, offsets, p, hot, coef, sxa, sxb, rya, ryb, za, zb):
    return call(
        functools.partial(side_kernel, last),
        "side",
        [SMEM, SMEM] + [VMEM] * 8,
        (VMEM, VMEM),
        (block(2 * za.shape[0]), LAG_SHAPE),
        us=8,
    )(offsets, p, hot, coef, sxa, sxb, rya, ryb, za, zb)


def solve_kernel(round_index, o_ref, mine_ref, other_ref, coef_ref):
    angles(mine_ref[...] + other_ref[...], offsets_of(o_ref, round_index), coef_ref)


def solve(round_index, offsets, mine, other):
    return call(
        functools.partial(solve_kernel, round_index),
        "solve%d" % round_index,
        [SMEM] + [VMEM] * 2,
        VMEM,
        COEF_SHAPE,
        us=2,
    )(offsets, mine, other)


def own_kernel(o_ref, p_ref, coef_ref, za, zb, q_ref, out_ref):
    p = p_ref[0]
    core = p & 1
    o = offsets_of(o_ref, 2)
    coef = coef_ref[...]

    def go(rows, k, rows_part):
        upper, lower = pick_halves(core == 0, read((za, zb)[k], rows_part), read(q_ref, rows))
        upper, lower = rotate(upper, lower, coef, o)
        wanted, _ = pick_halves((core == 1) & (p != 1), upper, lower)
        write(out_ref, rows, [x * x for x in wanted])

    by_parts(q_ref.shape[0], go)


def own(offsets, p, coef, za, zb, q):
    return call(own_kernel, "own", [SMEM, SMEM] + [VMEM] * 4, VMEM, block(q.shape[0]), us=40)(
        offsets, p, coef, za, zb, q
    )


def finish_kernel(
    last, row_total, o_ref, p_ref, coef_ref, a_ref, b_ref, c_ref, own_ref, ra, rb, v_ref, out_hbm, norm_ref, e_ref, sem
):
    p = p_ref[0]
    core = p & 1
    o = offsets_of(o_ref, 2)
    keep = pltpu.make_async_copy(own_ref, out_hbm.at[1 - core], sem.at[0])
    keep.start()
    coef = coef_ref[...]
    for k, ref in enumerate((a_ref, b_ref, c_ref)):
        norm_ref[k] = ref[8:10, :] / row_total
    part = ra.shape[0]
    r = tile_rows(part, 384)
    tiles = part // r
    sends = []
    for t in range(2 * tiles):
        rows = pl.ds(t * r, r)
        swap = (p == 0) | (p == last)
        upper, lower = pick_halves((core == 0) != swap, read((ra, rb)[t // tiles], pl.ds(t % tiles * r, r)), read(v_ref, rows))
        upper, lower = rotate(upper, lower, coef, o)
        wanted, _ = pick_halves((core == 0) | (p == last), upper, lower)
        write(e_ref, rows, [x * x for x in wanted])
        copy = pltpu.make_async_copy(e_ref.at[rows], out_hbm.at[core, rows], sem.at[1 + t])
        copy.start()
        sends.append(copy)
    for copy in [keep] + sends:
        copy.wait()


def finish(last, row_total, offsets, p, coef, coefs, own_block, ra, rb, v):
    rows = v.shape[0]
    return call(
        functools.partial(finish_kernel, last, row_total),
        "finish",
        [SMEM, SMEM] + [VMEM] * 8,
        (ANY, VMEM),
        (jax.ShapeDtypeStruct((2, rows, W), F32), jax.ShapeDtypeStruct((3, 2, W), F32)),
        [pltpu.VMEM((rows, W), F32), pltpu.SemaphoreType.DMA((16,))],
        us=5,
    )(offsets, p, coef, *coefs, own_block, ra, rb, v)


def body(row_feats, col_feats, offsets):
    n = lax.axis_size("blk")
    chips = n // 2
    p = lax.axis_index("blk").astype(jnp.int32).reshape(1)
    row_total = row_feats.shape[0] * lax.axis_size("row")
    across = [(0, 1), (1, 0)]
    sibling = [(i, i ^ 1) for i in range(n)]
    meet = [(2 * j + 1, 2 * j + 2) for j in range(chips - 1)] + [(2 * j, 2 * j - 1) for j in range(1, chips)]
    meet += [(0, 0), (n - 1, n - 1)]
    lend = [(2 * j, 2 * j + 3) for j in range(chips - 1)] + [(2 * j + 1, 2 * j - 2) for j in range(1, chips)]
    lend += [(1, 1), (n - 2, n - 2)]
    deal = [(2 * j, 2 * j + 2) for j in range(chips - 1)] + [(2 * j + 1, 2 * j - 1) for j in range(1, chips)]
    deal += [(1, 0), (n - 2, n - 1)]
    tell = [(2 * j, 2 * j - 2) for j in range(1, chips)] + [(2 * j + 1, 2 * j + 3) for j in range(chips - 1)]
    tell += [(0, 1), (n - 1, n - 2)]

    upper, lower, lag = first(offsets, row_feats, col_feats)
    lag_other = lax.ppermute(lag, "row", across)
    xa, xb, ya, yb, coef_a = turn_first(offsets, p, lag, lag_other, upper, lower)
    hot = table(1, offsets, coef_a)
    rxa = lax.ppermute(xa, "blk", meet)
    rxb = lax.ppermute(xb, "blk", meet)
    sya = lax.ppermute(ya, "blk", sibling)
    syb = lax.ppermute(yb, "blk", sibling)
    sxa = lax.ppermute(xa, "blk", sibling)
    sxb = lax.ppermute(xb, "blk", sibling)
    gram = pairs_start(p, rxa, sya)
    ya, gram = lax.optimization_barrier((ya, gram))
    rya = lax.ppermute(ya, "blk", lend)
    lag = pairs(offsets, p, hot, gram, rxb, syb)
    lag_other = lax.ppermute(lag, "row", across)
    hot = table(2, offsets, lag)
    yb, hot = lax.optimization_barrier((yb, hot))
    ryb = lax.ppermute(yb, "blk", lend)
    coef_b = solve(1, offsets, lag, lag_other)
    coef_side = lax.ppermute(coef_b, "blk", tell)
    rxa, rya, sxa, sxb = lax.optimization_barrier((rxa, rya, sxa, sxb))
    za, zb, v = turn_second(offsets, p, coef_b, rxa, rxb, sya, syb)
    za, zb, coef_side = lax.optimization_barrier((za, zb, coef_side))
    ra = lax.ppermute(za, "blk", deal)
    q, lag = side(n - 1, offsets, p, hot, coef_side, sxa, sxb, rya, ryb, za, zb)
    lag_other = lax.ppermute(lag, "row", across)
    later, _ = lax.optimization_barrier((zb, lag))
    rb = lax.ppermute(later, "blk", deal)
    coef_c = solve(2, offsets, lag, lag_other)
    coef_got = lax.ppermute(coef_c, "blk", deal)
    coef_norm = lax.ppermute(coef_c, "blk", sibling)
    coef_own, ra = lax.optimization_barrier((coef_c, ra))
    own_block = own(offsets, p, coef_own, za, zb, q)
    return finish(n - 1, row_total, offsets, p, coef_got, (coef_a, coef_b, coef_norm), own_block, ra, rb, v)


def solution(mesh):
    return jax.shard_map(
        body,
        mesh=mesh,
        in_specs=(P("row", None), P("blk", None), P()),
        out_specs=(P(None, "row", "blk"), P(None, None, "blk")),
        check_vma=False,
    )
```

```python
import functools
import math

import jax
import jax.numpy as jnp
from jax import lax
from jax.experimental import pallas as pl
from jax.experimental.pallas import tpu as pltpu
from jax.sharding import PartitionSpec as P

F32 = jnp.float32
BF16 = jnp.bfloat16
W = 256
H = 128
LAGS = 56
WIDE = 96
VMEM_LIMIT = 24 * 1024 * 1024
FIRST_LIMIT = 50 * 1024 * 1024


def group_rows(m):
    return (16 * m, 16) if m < 4 else (64 + 8 * (m - 4), 8)


def lag_plan():
    unit = [tuple(int(i == j) for j in range(4)) for i in range(4)]
    zero = (0, 0, 0, 0)

    def plus(a, b, sign=1):
        return tuple(x + sign * y for x, y in zip(a, b))

    t, s = [zero], [zero]
    first, second = [0], [1]
    wide = {15: (0, 0, zero), 30: (1, 1, zero)}
    for step in range(4):
        count = 1 << step
        for m in range(count):
            start, _ = group_rows(m)
            place = {3: 0, 2: 8, 1: 12, 0: 14}[step]
            for n in range(count):
                lag = plus(plus(unit[step], s[n]), t[m], -1)
                wide[start + place + n] = (first[m], second[n], lag)
        if step < 3:
            t, s = t + [plus(x, unit[step]) for x in s], s + [plus(x, unit[step], -1) for x in t]
            first, second = first + second, second + first
    table = sorted(set(wide.values()))
    return table, {r: table.index(key) for r, key in wide.items()}, t


TABLE_ROWS, USES, BASES = lag_plan()
UPPER_ROWS = sum(1 for row in TABLE_ROWS if row[0] == 0)


def shift_of(coefs, o):
    total = 0
    for k, value in zip(coefs, o):
        total = total + k * value if k else total
    return total & (W - 1)


def split(x):
    hi = x.astype(BF16)
    return hi, (x - hi.astype(F32)).astype(BF16)


TN = (((0,), (0,)), ((), ()))
NT = (((1,), (1,)), ((), ()))


def skew(x):
    row = lax.broadcasted_iota(jnp.int32, (W, W), 0)
    for bit in (1, 2, 4):
        x = jnp.where((row & bit) != 0, pltpu.roll(x, W - bit, 1), x)
    tiles = [pltpu.roll(x[8 * t : 8 * t + 8], (W - 8 * t) % W, 1) for t in range(W // 8)]
    return jnp.concatenate(tiles, axis=0)


def build_onehot(o, table_ref):
    table_ref[...] = jnp.full((LAGS, H), -1, jnp.int32)
    for r, (_, side, lag) in enumerate(TABLE_ROWS):
        table_ref[r : r + 1, :] = jnp.full((1, H), shift_of(lag, o) + W * side, jnp.int32)
    table = jnp.concatenate([table_ref[...]] * 4, axis=1)
    return (table == lax.broadcasted_iota(jnp.int32, (LAGS, 2 * W), 1)).astype(F32).astype(BF16)


def lag_products(gram, onehot, out_ref):
    diags = []
    for kind in (0, 1):
        sheets = [skew(gram[kind * W : (kind + 1) * W, side * W : (side + 1) * W]) for side in (0, 1)]
        hi, lo = split(jnp.concatenate(sheets, axis=1))
        diags.append(
            lax.dot_general(onehot, lo, NT, preferred_element_type=F32)
            + lax.dot_general(onehot, hi, NT, preferred_element_type=F32)
        )
    row = lax.broadcasted_iota(jnp.int32, (LAGS, W), 0)
    out_ref[...] = jnp.where(row < UPPER_ROWS, diags[0], diags[1])


def gram_of(a, b):
    hi, lo = split(jnp.concatenate([a, b], axis=1))
    return (
        lax.dot_general(hi, lo, TN, preferred_element_type=F32)
        + lax.dot_general(lo, hi, TN, preferred_element_type=F32)
        + lax.dot_general(hi, hi, TN, preferred_element_type=F32)
    )


def angle(g, upper_sq, lower_sq):
    twice = 2.0 * g
    diff = upper_sq - lower_sq
    scale = jnp.maximum(jnp.abs(twice), jnp.abs(diff))
    live = scale > 0.0
    safe = jnp.where(live, scale, 1.0)
    x = jnp.where(live, diff / safe, 1.0)
    y = jnp.where(live, twice / safe, 0.0)
    r = jnp.sqrt(x * x + y * y)
    big = jnp.sqrt(0.5 * (1.0 + jnp.abs(x) / r))
    small = 0.5 * jnp.abs(y) / (r * big)
    wide = x < 0.0
    c = jnp.where(wide, small, big)
    s = jnp.where(wide, big, small)
    s = jnp.where(y < 0.0, -s, s)
    cross = twice * c * s
    return c, s, c * c * upper_sq + cross + s * s * lower_sq, s * s * upper_sq - cross + c * c * lower_sq


def angles(lags, o, coef_ref, sum_ref, wide_ref):
    sum_ref[...] = lags
    for r, place in USES.items():
        wide_ref[r : r + 1, :] = sum_ref[place : place + 1, :]
    tiles, last = [], []
    for m in range(8):
        start, count = group_rows(m)
        tile = wide_ref[start : start + count, :]
        if m > 0:
            tile = pltpu.roll(tile, (-shift_of(BASES[m], o)) & (W - 1), 1)
        last.append(tile[0:8])
        if m < 4:
            tiles.append(tile[8:16])
    row = lax.broadcasted_iota(jnp.int32, (8, W), 0)
    a = jnp.ones((8, W), F32)
    b = jnp.ones((8, W), F32)
    upper_sq = tiles[0][7:8]
    lower_sq = tiles[1][6:7]
    for step in range(4):
        count = 1 << step
        if step == 3:
            parts, place = last, 0
        else:
            parts, place = tiles[:count], (6, 4, 0)[step]
        acc = None
        for m in range(count):
            term = a[m : m + 1] * parts[m]
            acc = term if acc is None else acc + term
        view = pltpu.roll(b, place, 0) if place else b
        acc = jnp.where((row >= place) & (row < place + count), acc * view, 0.0)
        g = jnp.sum(acc, axis=0, keepdims=True)
        c, s, upper_sq, lower_sq = angle(g, upper_sq, lower_sq)
        coef_ref[step : step + 1, :] = c
        coef_ref[4 + step : 5 + step, :] = s
        if step < 3:
            shift_a, shift_b = pltpu.roll(a, count, 0), pltpu.roll(b, count, 0)
            a, b = jnp.where(row < count, c * a, s * shift_b), jnp.where(row < count, c * b, -s * shift_a)
            turn = (o[step] - o[step + 1]) & (W - 1)
            b = pltpu.roll(b, turn, 1)
            lower_sq = pltpu.roll(jnp.broadcast_to(lower_sq, (8, W)), turn, 1)[0:1]
    coef_ref[8:9, :] = upper_sq
    coef_ref[9:10, :] = pltpu.roll(jnp.broadcast_to(lower_sq, (8, W)), o[3] & (W - 1), 1)[0:1]


def halves(x):
    return [x[:, :H], x[:, H:]]


def turn_halves(x, amount):
    short = amount & (H - 1)
    lane = lax.broadcasted_iota(jnp.int32, (1, H), 1)
    cross = (lane < short) != ((amount & H) != 0)
    a, b = pltpu.roll(x[0], short, 1), pltpu.roll(x[1], short, 1)
    return [jnp.where(cross, b, a), jnp.where(cross, a, b)]


def rotate(upper, lower, coef, o):
    upper, lower = list(upper), turn_halves(lower, (-o[0]) & (W - 1))
    for step in range(4):
        for h in (0, 1):
            c = coef[step : step + 1, h * H : (h + 1) * H]
            s = coef[4 + step : 5 + step, h * H : (h + 1) * H]
            upper[h], lower[h] = c * upper[h] + s * lower[h], c * lower[h] - s * upper[h]
        turn = (o[step] - o[step + 1]) if step < 3 else o[3]
        lower = turn_halves(lower, turn & (W - 1))
    return upper, lower


SMEM = pl.BlockSpec(memory_space=pltpu.SMEM)
VMEM = pl.BlockSpec(memory_space=pltpu.VMEM)
ANY = pl.BlockSpec(memory_space=pl.ANY)
LAG_SHAPE = jax.ShapeDtypeStruct((LAGS, W), F32)
COEF_SHAPE = jax.ShapeDtypeStruct((16, W), F32)
ONEHOT_SHAPE = jax.ShapeDtypeStruct((LAGS, 2 * W), BF16)
TABLE = pltpu.VMEM((LAGS, H), jnp.int32)
LAG_SCRATCH = [pltpu.VMEM((LAGS, W), F32), pltpu.VMEM((WIDE, W), F32)]


def tile_rows(rows, most=512):
    r = most
    while rows % r:
        r //= 2
    return r


def block(rows):
    return jax.ShapeDtypeStruct((rows, W), F32)


def call(kernel, name, in_specs, out_specs, out_shape, scratch=(), us=1, limit=VMEM_LIMIT):
    return pl.pallas_call(
        kernel,
        name=name,
        in_specs=in_specs,
        out_specs=out_specs,
        out_shape=out_shape,
        scratch_shapes=list(scratch),
        compiler_params=pltpu.CompilerParams(vmem_limit_bytes=limit),
        cost_estimate=pl.CostEstimate(flops=us * 10**9, bytes_accessed=us * 3 * 10**6, transcendentals=0),
    )


def offsets_of(o_ref, round_index):
    return [o_ref[round_index, j] for j in range(4)]


def pick(flag, a, b):
    return jnp.where(flag, a, b), jnp.where(flag, b, a)


def pick_halves(flag, a, b):
    pairs = [pick(flag, x, y) for x, y in zip(a, b)]
    return [x for x, _ in pairs], [y for _, y in pairs]


def read(ref, rows):
    return [ref[rows, :H], ref[rows, H:]]


def write(ref, rows, x):
    ref[rows, :H] = x[0]
    ref[rows, H:] = x[1]


def first_kernel(
    o_hbm, rows_hbm, cols_hbm, upper_ref, lower_ref, lag_ref, rows_ref, cols_ref, table_ref, norm_ref, o_ref, sem
):
    count, feat = cols_ref.shape
    total = rows_ref.shape[0]
    r = tile_rows(total)
    tiles = total // r
    half = count // 2
    fetch_cols = [
        pltpu.make_async_copy(cols_hbm.at[pl.ds(k * half, half)], cols_ref.at[pl.ds(k * half, half)], sem.at[k])
        for k in range(2)
    ]
    fetch_rows = [
        pltpu.make_async_copy(rows_hbm.at[pl.ds(t * r, r)], rows_ref.at[pl.ds(t * r, r)], sem.at[2 + t])
        for t in range(tiles)
    ]
    fetch_o = pltpu.make_async_copy(o_hbm, o_ref, sem.at[15])
    for copy in [fetch_o] + fetch_cols + fetch_rows:
        copy.start()
    fetch_o.wait()
    o = offsets_of(o_ref, 0)
    onehot = build_onehot(o, table_ref)
    for copy in fetch_cols:
        copy.wait()
    for t in range(tiles):
        fetch_rows[t].wait()
        if t == 0:
            for k in range(0, count, H):
                wide = cols_ref[k : k + H].astype(F32)
                sums = jnp.sum(wide * wide, axis=1, keepdims=True)
                norm_ref[:, k : k + H] = jnp.transpose(jnp.broadcast_to(sums, (H, H)))[0:8]
        part = slice(t * r, (t + 1) * r)
        rows = rows_ref[part]
        cross = lax.dot_general(rows, cols_ref[...], NT, preferred_element_type=F32)
        wide = rows.astype(F32)
        row_norm = jnp.sum(wide * wide, axis=1, keepdims=True)
        kernel = jnp.exp(
            -(0.25 / math.sqrt(feat)) * (row_norm + norm_ref[0:1] - 2.0 * cross - 2.0 * feat)
        )
        upper_ref[part] = kernel[:, :W]
        lower_ref[part] = kernel[:, W:]
    lag_products(gram_of(upper_ref[...], lower_ref[...]), onehot, lag_ref)


def first(offsets, row_feats, col_feats):
    rows, feat = row_feats.shape
    return call(
        first_kernel,
        "first",
        [ANY, ANY, ANY],
        (VMEM, VMEM, VMEM),
        (block(rows), block(rows), LAG_SHAPE),
        [
            pltpu.VMEM(row_feats.shape, BF16),
            pltpu.VMEM(col_feats.shape, BF16),
            TABLE,
            pltpu.VMEM((8, 2 * W), F32),
            pltpu.SMEM((3, 4), jnp.int32),
            pltpu.SemaphoreType.DMA((16,)),
        ],
        us=10,
        limit=FIRST_LIMIT,
    )(offsets, row_feats, col_feats)


def table_kernel(round_index, o_ref, after_ref, out_ref, table_ref):
    out_ref[...] = build_onehot(offsets_of(o_ref, round_index), table_ref)


def table(round_index, offsets, after):
    return call(
        functools.partial(table_kernel, round_index), "table%d" % round_index, [SMEM, ANY], VMEM, ONEHOT_SHAPE, [TABLE]
    )(offsets, after)


def by_parts(total, go):
    part = total // 2
    r = tile_rows(part, 384)
    for k in range(2):

        @pl.loop(0, part // r)
        def _(i):
            start = pl.multiple_of(i * r, r)
            go(pl.ds(pl.multiple_of(k * part + i * r, r), r), k, pl.ds(start, r))


def turn_first_kernel(o_ref, p_ref, mine_ref, other_ref, a_ref, b_ref, xa, xb, ya, yb, coef_ref, *lag_refs):
    p = p_ref[0]
    o = offsets_of(o_ref, 0)
    angles(mine_ref[...] + other_ref[...], o, coef_ref, *lag_refs)
    coef = coef_ref[...]
    keep = ((p & 1) == 1) | (p == 0)

    def go(rows, k, rows_part):
        upper, lower = rotate(read(a_ref, rows), read(b_ref, rows), coef, o)
        x, y = pick_halves(keep, upper, lower)
        write((xa, xb)[k], rows_part, x)
        write((ya, yb)[k], rows_part, y)

    by_parts(a_ref.shape[0], go)


def turn_first(offsets, p, mine, other, a, b):
    rows = a.shape[0]
    part = block(rows // 2)
    return call(
        turn_first_kernel,
        "turn0",
        [SMEM, SMEM] + [VMEM] * 4,
        (VMEM,) * 5,
        (part, part, part, part, COEF_SHAPE),
        LAG_SCRATCH,
        us=5,
    )(offsets, p, mine, other, a, b)


def pairs_start_kernel(p_ref, a_ref, b_ref, gram_ref):
    upper, lower = pick((p_ref[0] & 1) == 0, a_ref[...], b_ref[...])
    gram_ref[...] = gram_of(upper, lower)


def pairs_start(p, a, b):
    return call(
        pairs_start_kernel, "pairs0", [SMEM, VMEM, VMEM], VMEM, jax.ShapeDtypeStruct((2 * W, 2 * W), F32), us=3
    )(p, a, b)


def pairs_kernel(p_ref, hot_ref, gram_ref, a_ref, b_ref, lag_ref):
    upper, lower = pick((p_ref[0] & 1) == 0, a_ref[...], b_ref[...])
    lag_products(gram_ref[...] + gram_of(upper, lower), hot_ref[...], lag_ref)


def pairs(p, hot, gram, a, b):
    return call(
        pairs_kernel, "pairs1", [SMEM] + [VMEM] * 4, VMEM, LAG_SHAPE, us=4
    )(p, hot, gram, a, b)


def turn_second_kernel(o_ref, p_ref, coef_ref, rxa, rxb, sya, syb, za, zb, v_ref):
    p = p_ref[0]
    core = p & 1
    o = offsets_of(o_ref, 1)
    coef = coef_ref[...]

    def go(rows, k, rows_part):
        upper, lower = pick_halves(core == 0, read((rxa, rxb)[k], rows_part), read((sya, syb)[k], rows_part))
        upper, lower = rotate(upper, lower, coef, o)
        z, v = pick_halves((core == 0) & (p != 0), upper, lower)
        write((za, zb)[k], rows_part, z)
        write(v_ref, rows, v)

    by_parts(v_ref.shape[0], go)


def turn_second(offsets, p, coef, rxa, rxb, sya, syb):
    rows = rxa.shape[0] * 2
    part = block(rows // 2)
    return call(
        turn_second_kernel,
        "turn1",
        [SMEM, SMEM] + [VMEM] * 5,
        (VMEM,) * 3,
        (part, part, block(rows)),
        us=40,
    )(offsets, p, coef, rxa, rxb, sya, syb)


def side_kernel(last, o_ref, p_ref, hot_ref, coef_ref, sxa, sxb, rya, ryb, za, zb, q_ref, lag_ref):
    p = p_ref[0]
    core = p & 1
    o = offsets_of(o_ref, 1)
    coef = coef_ref[...]
    near_end = (p == 1) | (p == last - 1)
    part = za.shape[0]

    def go(rows, k, rows_part):
        upper, lower = pick_halves(
            (core == 0) != near_end, read((sxa, sxb)[k], rows_part), read((rya, ryb)[k], rows_part)
        )
        upper, lower = rotate(upper, lower, coef, o)
        wanted, _ = pick_halves((core == 1) | (p == last - 1), upper, lower)
        write(q_ref, rows, wanted)

    by_parts(q_ref.shape[0], go)
    z = jnp.concatenate([za[...], zb[...]], axis=0)
    upper, lower = pick(core == 0, z, q_ref[...])
    lag_products(gram_of(upper, lower), hot_ref[...], lag_ref)


def side(last, offsets, p, hot, coef, sxa, sxb, rya, ryb, za, zb):
    return call(
        functools.partial(side_kernel, last),
        "side",
        [SMEM, SMEM] + [VMEM] * 8,
        (VMEM, VMEM),
        (block(2 * za.shape[0]), LAG_SHAPE),
        us=8,
    )(offsets, p, hot, coef, sxa, sxb, rya, ryb, za, zb)


def solve_kernel(round_index, o_ref, mine_ref, other_ref, coef_ref, *lag_refs):
    angles(mine_ref[...] + other_ref[...], offsets_of(o_ref, round_index), coef_ref, *lag_refs)


def solve(round_index, offsets, mine, other):
    return call(
        functools.partial(solve_kernel, round_index),
        "solve%d" % round_index,
        [SMEM] + [VMEM] * 2,
        VMEM,
        COEF_SHAPE,
        LAG_SCRATCH,
        us=2,
    )(offsets, mine, other)


def own_kernel(o_ref, p_ref, coef_ref, za, zb, q_ref, out_ref):
    p = p_ref[0]
    core = p & 1
    o = offsets_of(o_ref, 2)
    coef = coef_ref[...]

    def go(rows, k, rows_part):
        upper, lower = pick_halves(core == 0, read((za, zb)[k], rows_part), read(q_ref, rows))
        upper, lower = rotate(upper, lower, coef, o)
        wanted, _ = pick_halves((core == 1) & (p != 1), upper, lower)
        write(out_ref, rows, [x * x for x in wanted])

    by_parts(q_ref.shape[0], go)


def own(offsets, p, coef, za, zb, q):
    return call(own_kernel, "own", [SMEM, SMEM] + [VMEM] * 4, VMEM, block(q.shape[0]), us=40)(
        offsets, p, coef, za, zb, q
    )


def finish_kernel(
    last, row_total, o_ref, p_ref, coef_ref, a_ref, b_ref, c_ref, own_ref, ra, rb, v_ref, out_hbm, norm_ref, e_ref, sem
):
    p = p_ref[0]
    core = p & 1
    o = offsets_of(o_ref, 2)
    keep = pltpu.make_async_copy(own_ref, out_hbm.at[1 - core], sem.at[0])
    keep.start()
    coef = coef_ref[...]
    for k, ref in enumerate((a_ref, b_ref, c_ref)):
        norm_ref[k] = ref[8:10, :] / row_total
    part = ra.shape[0]
    r = tile_rows(part, 384)
    tiles = part // r
    sends = []
    for t in range(2 * tiles):
        rows = pl.ds(t * r, r)
        swap = (p == 0) | (p == last)
        upper, lower = pick_halves((core == 0) != swap, read((ra, rb)[t // tiles], pl.ds(t % tiles * r, r)), read(v_ref, rows))
        upper, lower = rotate(upper, lower, coef, o)
        wanted, _ = pick_halves((core == 0) | (p == last), upper, lower)
        write(e_ref, rows, [x * x for x in wanted])
        copy = pltpu.make_async_copy(e_ref.at[rows], out_hbm.at[core, rows], sem.at[1 + t])
        copy.start()
        sends.append(copy)
    for copy in [keep] + sends:
        copy.wait()


def finish(last, row_total, offsets, p, coef, coefs, own_block, ra, rb, v):
    rows = v.shape[0]
    return call(
        functools.partial(finish_kernel, last, row_total),
        "finish",
        [SMEM, SMEM] + [VMEM] * 8,
        (ANY, VMEM),
        (jax.ShapeDtypeStruct((2, rows, W), F32), jax.ShapeDtypeStruct((3, 2, W), F32)),
        [pltpu.VMEM((rows, W), F32), pltpu.SemaphoreType.DMA((16,))],
        us=5,
    )(offsets, p, coef, *coefs, own_block, ra, rb, v)


def body(row_feats, col_feats, offsets):
    n = lax.axis_size("blk")
    chips = n // 2
    p = lax.axis_index("blk").astype(jnp.int32).reshape(1)
    row_total = row_feats.shape[0] * lax.axis_size("row")
    across = [(0, 1), (1, 0)]
    sibling = [(i, i ^ 1) for i in range(n)]
    meet = [(2 * j + 1, 2 * j + 2) for j in range(chips - 1)] + [(2 * j, 2 * j - 1) for j in range(1, chips)]
    meet += [(0, 0), (n - 1, n - 1)]
    lend = [(2 * j, 2 * j + 3) for j in range(chips - 1)] + [(2 * j + 1, 2 * j - 2) for j in range(1, chips)]
    lend += [(1, 1), (n - 2, n - 2)]
    deal = [(2 * j, 2 * j + 2) for j in range(chips - 1)] + [(2 * j + 1, 2 * j - 1) for j in range(1, chips)]
    deal += [(1, 0), (n - 2, n - 1)]
    tell = [(2 * j, 2 * j - 2) for j in range(1, chips)] + [(2 * j + 1, 2 * j + 3) for j in range(chips - 1)]
    tell += [(0, 1), (n - 1, n - 2)]

    upper, lower, lag = first(offsets, row_feats, col_feats)
    lag_other = lax.ppermute(lag, "row", across)
    xa, xb, ya, yb, coef_a = turn_first(offsets, p, lag, lag_other, upper, lower)
    hot = table(1, offsets, coef_a)
    rxa = lax.ppermute(xa, "blk", meet)
    rxb = lax.ppermute(xb, "blk", meet)
    sya = lax.ppermute(ya, "blk", sibling)
    syb = lax.ppermute(yb, "blk", sibling)
    sxa = lax.ppermute(xa, "blk", sibling)
    sxb = lax.ppermute(xb, "blk", sibling)
    gram = pairs_start(p, rxa, sya)
    ya, gram = lax.optimization_barrier((ya, gram))
    rya = lax.ppermute(ya, "blk", lend)
    lag = pairs(p, hot, gram, rxb, syb)
    lag_other = lax.ppermute(lag, "row", across)
    hot = table(2, offsets, lag)
    yb, hot = lax.optimization_barrier((yb, hot))
    ryb = lax.ppermute(yb, "blk", lend)
    coef_b = solve(1, offsets, lag, lag_other)
    coef_side = lax.ppermute(coef_b, "blk", tell)
    rxa, rya, sxa, sxb = lax.optimization_barrier((rxa, rya, sxa, sxb))
    za, zb, v = turn_second(offsets, p, coef_b, rxa, rxb, sya, syb)
    za, zb, coef_side = lax.optimization_barrier((za, zb, coef_side))
    ra = lax.ppermute(za, "blk", deal)
    q, lag = side(n - 1, offsets, p, hot, coef_side, sxa, sxb, rya, ryb, za, zb)
    lag_other = lax.ppermute(lag, "row", across)
    later, _ = lax.optimization_barrier((zb, lag))
    rb = lax.ppermute(later, "blk", deal)
    coef_c = solve(2, offsets, lag, lag_other)
    coef_got = lax.ppermute(coef_c, "blk", deal)
    coef_norm = lax.ppermute(coef_c, "blk", sibling)
    coef_own, ra = lax.optimization_barrier((coef_c, ra))
    own_block = own(offsets, p, coef_own, za, zb, q)
    return finish(n - 1, row_total, offsets, p, coef_got, (coef_a, coef_b, coef_norm), own_block, ra, rb, v)


def solution(mesh):
    return jax.shard_map(
        body,
        mesh=mesh,
        in_specs=(P("row", None), P("blk", None), P()),
        out_specs=(P(None, "row", "blk"), P(None, None, "blk")),
        check_vma=False,
    )
```

```python
import functools
import math

import jax
import jax.numpy as jnp
from jax import lax
from jax.experimental import pallas as pl
from jax.experimental.pallas import tpu as pltpu
from jax.sharding import PartitionSpec as P

F32 = jnp.float32
BF16 = jnp.bfloat16
W = 256
H = 128
LAGS = 56
WIDE = 96
VMEM_LIMIT = 24 * 1024 * 1024
FIRST_LIMIT = 50 * 1024 * 1024


def group_rows(m):
    return (16 * m, 16) if m < 4 else (64 + 8 * (m - 4), 8)


def lag_plan():
    unit = [tuple(int(i == j) for j in range(4)) for i in range(4)]
    zero = (0, 0, 0, 0)

    def plus(a, b, sign=1):
        return tuple(x + sign * y for x, y in zip(a, b))

    t, s = [zero], [zero]
    first, second = [0], [1]
    wide = {15: (0, 0, zero), 30: (1, 1, zero)}
    for step in range(4):
        count = 1 << step
        for m in range(count):
            start, _ = group_rows(m)
            place = {3: 0, 2: 8, 1: 12, 0: 14}[step]
            for n in range(count):
                lag = plus(plus(unit[step], s[n]), t[m], -1)
                wide[start + place + n] = (first[m], second[n], lag)
        if step < 3:
            t, s = t + [plus(x, unit[step]) for x in s], s + [plus(x, unit[step], -1) for x in t]
            first, second = first + second, second + first
    table = sorted(set(wide.values()))
    return table, {r: table.index(key) for r, key in wide.items()}, t


TABLE_ROWS, USES, BASES = lag_plan()
UPPER_ROWS = sum(1 for row in TABLE_ROWS if row[0] == 0)


def shift_of(coefs, o):
    total = 0
    for k, value in zip(coefs, o):
        total = total + k * value if k else total
    return total & (W - 1)


def split(x):
    hi = x.astype(BF16)
    return hi, (x - hi.astype(F32)).astype(BF16)


TN = (((0,), (0,)), ((), ()))
NT = (((1,), (1,)), ((), ()))


def skew(x):
    row = lax.broadcasted_iota(jnp.int32, (W, W), 0)
    for bit in (1, 2, 4):
        x = jnp.where((row & bit) != 0, pltpu.roll(x, W - bit, 1), x)
    tiles = [pltpu.roll(x[8 * t : 8 * t + 8], (W - 8 * t) % W, 1) for t in range(W // 8)]
    return jnp.concatenate(tiles, axis=0)


def build_onehot(o, table_ref):
    table_ref[...] = jnp.full((LAGS, H), -1, jnp.int32)
    for r, (_, side, lag) in enumerate(TABLE_ROWS):
        table_ref[r : r + 1, :] = jnp.full((1, H), shift_of(lag, o) + W * side, jnp.int32)
    table = jnp.concatenate([table_ref[...]] * 4, axis=1)
    return (table == lax.broadcasted_iota(jnp.int32, (LAGS, 2 * W), 1)).astype(F32).astype(BF16)


def lag_products(gram, onehot, out_ref):
    diags = []
    for kind in (0, 1):
        sheets = [skew(gram[kind * W : (kind + 1) * W, side * W : (side + 1) * W]) for side in (0, 1)]
        hi, lo = split(jnp.concatenate(sheets, axis=1))
        diags.append(
            lax.dot_general(onehot, lo, NT, preferred_element_type=F32)
            + lax.dot_general(onehot, hi, NT, preferred_element_type=F32)
        )
    row = lax.broadcasted_iota(jnp.int32, (LAGS, W), 0)
    out_ref[...] = jnp.where(row < UPPER_ROWS, diags[0], diags[1])


def gram_of(a, b):
    hi, lo = split(jnp.concatenate([a, b], axis=1))
    return (
        lax.dot_general(hi, lo, TN, preferred_element_type=F32)
        + lax.dot_general(lo, hi, TN, preferred_element_type=F32)
        + lax.dot_general(hi, hi, TN, preferred_element_type=F32)
    )


def gram_whole(a, b):
    hi, lo = split(jnp.concatenate([a, b], axis=1))
    parts = lax.dot_general(hi, jnp.concatenate([hi, lo], axis=1), TN, preferred_element_type=F32)
    mixed = parts[:, 2 * W :]
    return parts[:, : 2 * W] + (mixed + jnp.transpose(mixed))


def angle(g, upper_sq, lower_sq):
    twice = 2.0 * g
    diff = upper_sq - lower_sq
    scale = jnp.maximum(jnp.abs(twice), jnp.abs(diff))
    live = scale > 0.0
    safe = jnp.where(live, scale, 1.0)
    x = jnp.where(live, diff / safe, 1.0)
    y = jnp.where(live, twice / safe, 0.0)
    r = jnp.sqrt(x * x + y * y)
    big = jnp.sqrt(0.5 * (1.0 + jnp.abs(x) / r))
    small = 0.5 * jnp.abs(y) / (r * big)
    wide = x < 0.0
    c = jnp.where(wide, small, big)
    s = jnp.where(wide, big, small)
    s = jnp.where(y < 0.0, -s, s)
    cross = twice * c * s
    return c, s, c * c * upper_sq + cross + s * s * lower_sq, s * s * upper_sq - cross + c * c * lower_sq


def angles(lags, o, coef_ref, sum_ref, wide_ref):
    sum_ref[...] = lags
    for r, place in USES.items():
        wide_ref[r : r + 1, :] = sum_ref[place : place + 1, :]
    tiles, last = [], []
    for m in range(8):
        start, count = group_rows(m)
        tile = wide_ref[start : start + count, :]
        if m > 0:
            tile = pltpu.roll(tile, (-shift_of(BASES[m], o)) & (W - 1), 1)
        last.append(tile[0:8])
        if m < 4:
            tiles.append(tile[8:16])
    row = lax.broadcasted_iota(jnp.int32, (8, W), 0)
    a = jnp.ones((8, W), F32)
    b = jnp.ones((8, W), F32)
    upper_sq = tiles[0][7:8]
    lower_sq = tiles[1][6:7]
    for step in range(4):
        count = 1 << step
        if step == 3:
            parts, place = last, 0
        else:
            parts, place = tiles[:count], (6, 4, 0)[step]
        acc = None
        for m in range(count):
            term = a[m : m + 1] * parts[m]
            acc = term if acc is None else acc + term
        view = pltpu.roll(b, place, 0) if place else b
        acc = jnp.where((row >= place) & (row < place + count), acc * view, 0.0)
        g = jnp.sum(acc, axis=0, keepdims=True)
        c, s, upper_sq, lower_sq = angle(g, upper_sq, lower_sq)
        coef_ref[step : step + 1, :] = c
        coef_ref[4 + step : 5 + step, :] = s
        if step < 3:
            shift_a, shift_b = pltpu.roll(a, count, 0), pltpu.roll(b, count, 0)
            a, b = jnp.where(row < count, c * a, s * shift_b), jnp.where(row < count, c * b, -s * shift_a)
            turn = (o[step] - o[step + 1]) & (W - 1)
            b = pltpu.roll(b, turn, 1)
            lower_sq = pltpu.roll(jnp.broadcast_to(lower_sq, (8, W)), turn, 1)[0:1]
    coef_ref[8:9, :] = upper_sq
    coef_ref[9:10, :] = pltpu.roll(jnp.broadcast_to(lower_sq, (8, W)), o[3] & (W - 1), 1)[0:1]


def halves(x):
    return [x[:, :H], x[:, H:]]


def turn_halves(x, amount):
    short = amount & (H - 1)
    lane = lax.broadcasted_iota(jnp.int32, (1, H), 1)
    cross = (lane < short) != ((amount & H) != 0)
    a, b = pltpu.roll(x[0], short, 1), pltpu.roll(x[1], short, 1)
    return [jnp.where(cross, b, a), jnp.where(cross, a, b)]


def rotate(upper, lower, coef, o):
    upper, lower = list(upper), turn_halves(lower, (-o[0]) & (W - 1))
    for step in range(4):
        for h in (0, 1):
            c = coef[step : step + 1, h * H : (h + 1) * H]
            s = coef[4 + step : 5 + step, h * H : (h + 1) * H]
            upper[h], lower[h] = c * upper[h] + s * lower[h], c * lower[h] - s * upper[h]
        turn = (o[step] - o[step + 1]) if step < 3 else o[3]
        lower = turn_halves(lower, turn & (W - 1))
    return upper, lower


SMEM = pl.BlockSpec(memory_space=pltpu.SMEM)
VMEM = pl.BlockSpec(memory_space=pltpu.VMEM)
ANY = pl.BlockSpec(memory_space=pl.ANY)
LAG_SHAPE = jax.ShapeDtypeStruct((LAGS, W), F32)
COEF_SHAPE = jax.ShapeDtypeStruct((16, W), F32)
ONEHOT_SHAPE = jax.ShapeDtypeStruct((LAGS, 2 * W), BF16)
TABLE = pltpu.VMEM((LAGS, H), jnp.int32)
LAG_SCRATCH = [pltpu.VMEM((LAGS, W), F32), pltpu.VMEM((WIDE, W), F32)]


def tile_rows(rows, most=512):
    r = most
    while rows % r:
        r //= 2
    return r


def block(rows):
    return jax.ShapeDtypeStruct((rows, W), F32)


def call(kernel, name, in_specs, out_specs, out_shape, scratch=(), us=1, limit=VMEM_LIMIT):
    return pl.pallas_call(
        kernel,
        name=name,
        in_specs=in_specs,
        out_specs=out_specs,
        out_shape=out_shape,
        scratch_shapes=list(scratch),
        compiler_params=pltpu.CompilerParams(vmem_limit_bytes=limit),
        cost_estimate=pl.CostEstimate(flops=us * 10**9, bytes_accessed=us * 3 * 10**6, transcendentals=0),
    )


def offsets_of(o_ref, round_index):
    return [o_ref[round_index, j] for j in range(4)]


def pick(flag, a, b):
    return jnp.where(flag, a, b), jnp.where(flag, b, a)


def pick_halves(flag, a, b):
    pairs = [pick(flag, x, y) for x, y in zip(a, b)]
    return [x for x, _ in pairs], [y for _, y in pairs]


def read(ref, rows):
    return [ref[rows, :H], ref[rows, H:]]


def write(ref, rows, x):
    ref[rows, :H] = x[0]
    ref[rows, H:] = x[1]


def first_kernel(
    o_hbm, rows_hbm, cols_hbm, upper_ref, lower_ref, lag_ref, rows_ref, cols_ref, table_ref, norm_ref, o_ref, sem
):
    count, feat = cols_ref.shape
    total = rows_ref.shape[0]
    r = tile_rows(total)
    tiles = total // r
    half = count // 2
    fetch_cols = [
        pltpu.make_async_copy(cols_hbm.at[pl.ds(k * half, half)], cols_ref.at[pl.ds(k * half, half)], sem.at[k])
        for k in range(2)
    ]
    fetch_rows = [
        pltpu.make_async_copy(rows_hbm.at[pl.ds(t * r, r)], rows_ref.at[pl.ds(t * r, r)], sem.at[2 + t])
        for t in range(tiles)
    ]
    fetch_o = pltpu.make_async_copy(o_hbm, o_ref, sem.at[15])
    for copy in [fetch_o] + fetch_cols + fetch_rows:
        copy.start()
    fetch_o.wait()
    o = offsets_of(o_ref, 0)
    onehot = build_onehot(o, table_ref)
    for copy in fetch_cols:
        copy.wait()
    for t in range(tiles):
        fetch_rows[t].wait()
        if t == 0:
            for k in range(0, count, H):
                wide = cols_ref[k : k + H].astype(F32)
                sums = jnp.sum(wide * wide, axis=1, keepdims=True)
                norm_ref[:, k : k + H] = jnp.transpose(jnp.broadcast_to(sums, (H, H)))[0:8]
        part = slice(t * r, (t + 1) * r)
        rows = rows_ref[part]
        cross = lax.dot_general(rows, cols_ref[...], NT, preferred_element_type=F32)
        wide = rows.astype(F32)
        row_norm = jnp.sum(wide * wide, axis=1, keepdims=True)
        kernel = jnp.exp(
            -(0.25 / math.sqrt(feat)) * (row_norm + norm_ref[0:1] - 2.0 * cross - 2.0 * feat)
        )
        upper_ref[part] = kernel[:, :W]
        lower_ref[part] = kernel[:, W:]
    lag_products(gram_whole(upper_ref[...], lower_ref[...]), onehot, lag_ref)


def first(offsets, row_feats, col_feats):
    rows, feat = row_feats.shape
    return call(
        first_kernel,
        "first",
        [ANY, ANY, ANY],
        (VMEM, VMEM, VMEM),
        (block(rows), block(rows), LAG_SHAPE),
        [
            pltpu.VMEM(row_feats.shape, BF16),
            pltpu.VMEM(col_feats.shape, BF16),
            TABLE,
            pltpu.VMEM((8, 2 * W), F32),
            pltpu.SMEM((3, 4), jnp.int32),
            pltpu.SemaphoreType.DMA((16,)),
        ],
        us=10,
        limit=FIRST_LIMIT,
    )(offsets, row_feats, col_feats)


def table_kernel(round_index, o_ref, after_ref, out_ref, table_ref):
    out_ref[...] = build_onehot(offsets_of(o_ref, round_index), table_ref)


def table(round_index, offsets, after):
    return call(
        functools.partial(table_kernel, round_index), "table%d" % round_index, [SMEM, ANY], VMEM, ONEHOT_SHAPE, [TABLE]
    )(offsets, after)


def by_parts(total, go):
    part = total // 2
    r = tile_rows(part, 384)
    for k in range(2):

        @pl.loop(0, part // r)
        def _(i):
            start = pl.multiple_of(i * r, r)
            go(pl.ds(pl.multiple_of(k * part + i * r, r), r), k, pl.ds(start, r))


def turn_first_kernel(o_ref, p_ref, mine_ref, other_ref, a_ref, b_ref, xa, xb, ya, yb, coef_ref, *lag_refs):
    p = p_ref[0]
    o = offsets_of(o_ref, 0)
    angles(mine_ref[...] + other_ref[...], o, coef_ref, *lag_refs)
    coef = coef_ref[...]
    keep = ((p & 1) == 1) | (p == 0)

    def go(rows, k, rows_part):
        upper, lower = rotate(read(a_ref, rows), read(b_ref, rows), coef, o)
        x, y = pick_halves(keep, upper, lower)
        write((xa, xb)[k], rows_part, x)
        write((ya, yb)[k], rows_part, y)

    by_parts(a_ref.shape[0], go)


def turn_first(offsets, p, mine, other, a, b):
    rows = a.shape[0]
    part = block(rows // 2)
    return call(
        turn_first_kernel,
        "turn0",
        [SMEM, SMEM] + [VMEM] * 4,
        (VMEM,) * 5,
        (part, part, part, part, COEF_SHAPE),
        LAG_SCRATCH,
        us=5,
    )(offsets, p, mine, other, a, b)


def pairs_start_kernel(p_ref, a_ref, b_ref, gram_ref):
    upper, lower = pick((p_ref[0] & 1) == 0, a_ref[...], b_ref[...])
    gram_ref[...] = gram_of(upper, lower)


def pairs_start(p, a, b):
    return call(
        pairs_start_kernel, "pairs0", [SMEM, VMEM, VMEM], VMEM, jax.ShapeDtypeStruct((2 * W, 2 * W), F32), us=3
    )(p, a, b)


def pairs_kernel(p_ref, hot_ref, gram_ref, a_ref, b_ref, lag_ref):
    upper, lower = pick((p_ref[0] & 1) == 0, a_ref[...], b_ref[...])
    lag_products(gram_ref[...] + gram_of(upper, lower), hot_ref[...], lag_ref)


def pairs(p, hot, gram, a, b):
    return call(
        pairs_kernel, "pairs1", [SMEM] + [VMEM] * 4, VMEM, LAG_SHAPE, us=4
    )(p, hot, gram, a, b)


def turn_second_kernel(o_ref, p_ref, coef_ref, rxa, rxb, sya, syb, za, zb, v_ref):
    p = p_ref[0]
    core = p & 1
    o = offsets_of(o_ref, 1)
    coef = coef_ref[...]

    def go(rows, k, rows_part):
        upper, lower = pick_halves(core == 0, read((rxa, rxb)[k], rows_part), read((sya, syb)[k], rows_part))
        upper, lower = rotate(upper, lower, coef, o)
        z, v = pick_halves((core == 0) & (p != 0), upper, lower)
        write((za, zb)[k], rows_part, z)
        write(v_ref, rows, v)

    by_parts(v_ref.shape[0], go)


def turn_second(offsets, p, coef, rxa, rxb, sya, syb):
    rows = rxa.shape[0] * 2
    part = block(rows // 2)
    return call(
        turn_second_kernel,
        "turn1",
        [SMEM, SMEM] + [VMEM] * 5,
        (VMEM,) * 3,
        (part, part, block(rows)),
        us=40,
    )(offsets, p, coef, rxa, rxb, sya, syb)


def side_kernel(last, o_ref, p_ref, hot_ref, coef_ref, sxa, sxb, rya, ryb, za, zb, q_ref, lag_ref):
    p = p_ref[0]
    core = p & 1
    o = offsets_of(o_ref, 1)
    coef = coef_ref[...]
    near_end = (p == 1) | (p == last - 1)
    part = za.shape[0]
    r = tile_rows(part, 384)
    parts, pending = None, None
    for t in range(2 * part // r + 1):
        ready, pending = pending, None
        if t < 2 * part // r:
            k = t * r // part
            rows = slice(t * r - k * part, t * r - k * part + r)
            upper, lower = pick_halves(
                (core == 0) != near_end, read((sxa, sxb)[k], rows), read((rya, ryb)[k], rows)
            )
            upper, lower = rotate(upper, lower, coef, o)
            wanted, _ = pick_halves((core == 1) | (p == last - 1), upper, lower)
            write(q_ref, slice(t * r, (t + 1) * r), wanted)
            pending = (za, zb)[k][rows], jnp.concatenate(wanted, axis=1)
        if ready is not None:
            added = gram_of(*pick(core == 0, *ready))
            parts = added if parts is None else parts + added
    lag_products(parts, hot_ref[...], lag_ref)


def side(last, offsets, p, hot, coef, sxa, sxb, rya, ryb, za, zb):
    return call(
        functools.partial(side_kernel, last),
        "side",
        [SMEM, SMEM] + [VMEM] * 8,
        (VMEM, VMEM),
        (block(2 * za.shape[0]), LAG_SHAPE),
        us=8,
    )(offsets, p, hot, coef, sxa, sxb, rya, ryb, za, zb)


def solve_kernel(round_index, o_ref, mine_ref, other_ref, coef_ref, *lag_refs):
    angles(mine_ref[...] + other_ref[...], offsets_of(o_ref, round_index), coef_ref, *lag_refs)


def solve(round_index, offsets, mine, other):
    return call(
        functools.partial(solve_kernel, round_index),
        "solve%d" % round_index,
        [SMEM] + [VMEM] * 2,
        VMEM,
        COEF_SHAPE,
        LAG_SCRATCH,
        us=2,
    )(offsets, mine, other)


def own_kernel(o_ref, p_ref, coef_ref, za, zb, q_ref, out_ref):
    p = p_ref[0]
    core = p & 1
    o = offsets_of(o_ref, 2)
    coef = coef_ref[...]

    def go(rows, k, rows_part):
        upper, lower = pick_halves(core == 0, read((za, zb)[k], rows_part), read(q_ref, rows))
        upper, lower = rotate(upper, lower, coef, o)
        wanted, _ = pick_halves((core == 1) & (p != 1), upper, lower)
        write(out_ref, rows, [x * x for x in wanted])

    by_parts(q_ref.shape[0], go)


def own(offsets, p, coef, za, zb, q):
    return call(own_kernel, "own", [SMEM, SMEM] + [VMEM] * 4, VMEM, block(q.shape[0]), us=40)(
        offsets, p, coef, za, zb, q
    )


def finish_kernel(
    last, row_total, o_ref, p_ref, coef_ref, a_ref, b_ref, c_ref, own_ref, ra, rb, v_ref, out_hbm, norm_ref, e_ref, sem
):
    p = p_ref[0]
    core = p & 1
    o = offsets_of(o_ref, 2)
    keep = pltpu.make_async_copy(own_ref, out_hbm.at[1 - core], sem.at[0])
    keep.start()
    coef = coef_ref[...]
    for k, ref in enumerate((a_ref, b_ref, c_ref)):
        norm_ref[k] = ref[8:10, :] / row_total
    part = ra.shape[0]
    r = tile_rows(part, 384)
    tiles = part // r
    sends = []
    for t in range(2 * tiles):
        rows = pl.ds(t * r, r)
        swap = (p == 0) | (p == last)
        upper, lower = pick_halves((core == 0) != swap, read((ra, rb)[t // tiles], pl.ds(t % tiles * r, r)), read(v_ref, rows))
        upper, lower = rotate(upper, lower, coef, o)
        wanted, _ = pick_halves((core == 0) | (p == last), upper, lower)
        write(e_ref, rows, [x * x for x in wanted])
        copy = pltpu.make_async_copy(e_ref.at[rows], out_hbm.at[core, rows], sem.at[1 + t])
        copy.start()
        sends.append(copy)
    for copy in [keep] + sends:
        copy.wait()


def finish(last, row_total, offsets, p, coef, coefs, own_block, ra, rb, v):
    rows = v.shape[0]
    return call(
        functools.partial(finish_kernel, last, row_total),
        "finish",
        [SMEM, SMEM] + [VMEM] * 8,
        (ANY, VMEM),
        (jax.ShapeDtypeStruct((2, rows, W), F32), jax.ShapeDtypeStruct((3, 2, W), F32)),
        [pltpu.VMEM((rows, W), F32), pltpu.SemaphoreType.DMA((16,))],
        us=5,
    )(offsets, p, coef, *coefs, own_block, ra, rb, v)


def body(row_feats, col_feats, offsets):
    n = lax.axis_size("blk")
    chips = n // 2
    p = lax.axis_index("blk").astype(jnp.int32).reshape(1)
    row_total = row_feats.shape[0] * lax.axis_size("row")
    across = [(0, 1), (1, 0)]
    sibling = [(i, i ^ 1) for i in range(n)]
    meet = [(2 * j + 1, 2 * j + 2) for j in range(chips - 1)] + [(2 * j, 2 * j - 1) for j in range(1, chips)]
    meet += [(0, 0), (n - 1, n - 1)]
    lend = [(2 * j, 2 * j + 3) for j in range(chips - 1)] + [(2 * j + 1, 2 * j - 2) for j in range(1, chips)]
    lend += [(1, 1), (n - 2, n - 2)]
    deal = [(2 * j, 2 * j + 2) for j in range(chips - 1)] + [(2 * j + 1, 2 * j - 1) for j in range(1, chips)]
    deal += [(1, 0), (n - 2, n - 1)]
    tell = [(2 * j, 2 * j - 2) for j in range(1, chips)] + [(2 * j + 1, 2 * j + 3) for j in range(chips - 1)]
    tell += [(0, 1), (n - 1, n - 2)]

    upper, lower, lag = first(offsets, row_feats, col_feats)
    lag_other = lax.ppermute(lag, "row", across)
    xa, xb, ya, yb, coef_a = turn_first(offsets, p, lag, lag_other, upper, lower)
    hot = table(1, offsets, coef_a)
    rxa = lax.ppermute(xa, "blk", meet)
    rxb = lax.ppermute(xb, "blk", meet)
    sya = lax.ppermute(ya, "blk", sibling)
    syb = lax.ppermute(yb, "blk", sibling)
    sxa = lax.ppermute(xa, "blk", sibling)
    sxb = lax.ppermute(xb, "blk", sibling)
    gram = pairs_start(p, rxa, sya)
    ya, gram = lax.optimization_barrier((ya, gram))
    rya = lax.ppermute(ya, "blk", lend)
    lag = pairs(p, hot, gram, rxb, syb)
    lag_other = lax.ppermute(lag, "row", across)
    hot = table(2, offsets, lag)
    yb, hot = lax.optimization_barrier((yb, hot))
    ryb = lax.ppermute(yb, "blk", lend)
    coef_b = solve(1, offsets, lag, lag_other)
    coef_side = lax.ppermute(coef_b, "blk", tell)
    rxa, rya, sxa, sxb = lax.optimization_barrier((rxa, rya, sxa, sxb))
    za, zb, v = turn_second(offsets, p, coef_b, rxa, rxb, sya, syb)
    za, zb, coef_side = lax.optimization_barrier((za, zb, coef_side))
    ra = lax.ppermute(za, "blk", deal)
    q, lag = side(n - 1, offsets, p, hot, coef_side, sxa, sxb, rya, ryb, za, zb)
    lag_other = lax.ppermute(lag, "row", across)
    later, _ = lax.optimization_barrier((zb, lag))
    rb = lax.ppermute(later, "blk", deal)
    coef_c = solve(2, offsets, lag, lag_other)
    coef_got = lax.ppermute(coef_c, "blk", deal)
    coef_own, ra = lax.optimization_barrier((coef_c, ra))
    own_block = own(offsets, p, coef_own, za, zb, q)
    coef_c, own_block = lax.optimization_barrier((coef_c, own_block))
    coef_norm = lax.ppermute(coef_c, "blk", sibling)
    return finish(n - 1, row_total, offsets, p, coef_got, (coef_a, coef_b, coef_norm), own_block, ra, rb, v)


def solution(mesh):
    return jax.shard_map(
        body,
        mesh=mesh,
        in_specs=(P("row", None), P("blk", None), P()),
        out_specs=(P(None, "row", "blk"), P(None, None, "blk")),
        check_vma=False,
    )
```

```python
import functools
import math

import jax
import jax.numpy as jnp
from jax import lax
from jax.experimental import pallas as pl
from jax.experimental.pallas import tpu as pltpu
from jax.sharding import PartitionSpec as P

F32 = jnp.float32
BF16 = jnp.bfloat16
W = 256
H = 128
LAGS = 56
WIDE = 96
VMEM_LIMIT = 24 * 1024 * 1024
FIRST_LIMIT = 50 * 1024 * 1024


def group_rows(m):
    return (16 * m, 16) if m < 4 else (64 + 8 * (m - 4), 8)


def lag_plan():
    unit = [tuple(int(i == j) for j in range(4)) for i in range(4)]
    zero = (0, 0, 0, 0)

    def plus(a, b, sign=1):
        return tuple(x + sign * y for x, y in zip(a, b))

    t, s = [zero], [zero]
    first, second = [0], [1]
    wide = {15: (0, 0, zero), 30: (1, 1, zero)}
    for step in range(4):
        count = 1 << step
        for m in range(count):
            start, _ = group_rows(m)
            place = {3: 0, 2: 8, 1: 12, 0: 14}[step]
            for n in range(count):
                lag = plus(plus(unit[step], s[n]), t[m], -1)
                wide[start + place + n] = (first[m], second[n], lag)
        if step < 3:
            t, s = t + [plus(x, unit[step]) for x in s], s + [plus(x, unit[step], -1) for x in t]
            first, second = first + second, second + first
    table = sorted(set(wide.values()))
    return table, {r: table.index(key) for r, key in wide.items()}, t


TABLE_ROWS, USES, BASES = lag_plan()
UPPER_ROWS = sum(1 for row in TABLE_ROWS if row[0] == 0)


def shift_of(coefs, o):
    total = 0
    for k, value in zip(coefs, o):
        total = total + k * value if k else total
    return total & (W - 1)


def split(x):
    hi = x.astype(BF16)
    return hi, (x - hi.astype(F32)).astype(BF16)


TN = (((0,), (0,)), ((), ()))
NT = (((1,), (1,)), ((), ()))


def skew(x):
    row = lax.broadcasted_iota(jnp.int32, (W, W), 0)
    for bit in (1, 2, 4):
        x = jnp.where((row & bit) != 0, pltpu.roll(x, W - bit, 1), x)
    tiles = [pltpu.roll(x[8 * t : 8 * t + 8], (W - 8 * t) % W, 1) for t in range(W // 8)]
    return jnp.concatenate(tiles, axis=0)


def build_onehot(o, table_ref):
    table_ref[...] = jnp.full((LAGS, H), -1, jnp.int32)
    for r, (_, side, lag) in enumerate(TABLE_ROWS):
        table_ref[r : r + 1, :] = jnp.full((1, H), shift_of(lag, o) + W * side, jnp.int32)
    table = jnp.concatenate([table_ref[...]] * 4, axis=1)
    return (table == lax.broadcasted_iota(jnp.int32, (LAGS, 2 * W), 1)).astype(F32).astype(BF16)


def lag_products(gram, onehot, out_ref):
    diags = []
    for kind in (0, 1):
        sheets = [skew(gram[kind * W : (kind + 1) * W, side * W : (side + 1) * W]) for side in (0, 1)]
        hi, lo = split(jnp.concatenate(sheets, axis=1))
        diags.append(
            lax.dot_general(onehot, lo, NT, preferred_element_type=F32)
            + lax.dot_general(onehot, hi, NT, preferred_element_type=F32)
        )
    row = lax.broadcasted_iota(jnp.int32, (LAGS, W), 0)
    out_ref[...] = jnp.where(row < UPPER_ROWS, diags[0], diags[1])


def gram_of(a, b):
    hi, lo = split(jnp.concatenate([a, b], axis=1))
    return (
        lax.dot_general(hi, lo, TN, preferred_element_type=F32)
        + lax.dot_general(lo, hi, TN, preferred_element_type=F32)
        + lax.dot_general(hi, hi, TN, preferred_element_type=F32)
    )


def gram_whole(a, b):
    hi, lo = split(jnp.concatenate([a, b], axis=1))
    parts = lax.dot_general(hi, jnp.concatenate([hi, lo], axis=1), TN, preferred_element_type=F32)
    mixed = parts[:, 2 * W :]
    return parts[:, : 2 * W] + (mixed + jnp.transpose(mixed))


def angle(g, upper_sq, lower_sq):
    twice = 2.0 * g
    diff = upper_sq - lower_sq
    scale = jnp.maximum(jnp.abs(twice), jnp.abs(diff))
    live = scale > 0.0
    safe = jnp.where(live, scale, 1.0)
    x = jnp.where(live, diff / safe, 1.0)
    y = jnp.where(live, twice / safe, 0.0)
    r = jnp.sqrt(x * x + y * y)
    big = jnp.sqrt(0.5 * (1.0 + jnp.abs(x) / r))
    small = 0.5 * jnp.abs(y) / (r * big)
    wide = x < 0.0
    c = jnp.where(wide, small, big)
    s = jnp.where(wide, big, small)
    s = jnp.where(y < 0.0, -s, s)
    cross = twice * c * s
    return c, s, c * c * upper_sq + cross + s * s * lower_sq, s * s * upper_sq - cross + c * c * lower_sq


def angles(lags, o, coef_ref, sum_ref, wide_ref):
    sum_ref[...] = lags
    for r, place in USES.items():
        wide_ref[r : r + 1, :] = sum_ref[place : place + 1, :]
    tiles, last = [], []
    for m in range(8):
        start, count = group_rows(m)
        tile = wide_ref[start : start + count, :]
        if m > 0:
            tile = pltpu.roll(tile, (-shift_of(BASES[m], o)) & (W - 1), 1)
        last.append(tile[0:8])
        if m < 4:
            tiles.append(tile[8:16])
    row = lax.broadcasted_iota(jnp.int32, (8, W), 0)
    a = jnp.ones((8, W), F32)
    b = jnp.ones((8, W), F32)
    upper_sq = tiles[0][7:8]
    lower_sq = tiles[1][6:7]
    for step in range(4):
        count = 1 << step
        if step == 3:
            parts, place = last, 0
        else:
            parts, place = tiles[:count], (6, 4, 0)[step]
        acc = None
        for m in range(count):
            term = a[m : m + 1] * parts[m]
            acc = term if acc is None else acc + term
        view = pltpu.roll(b, place, 0) if place else b
        acc = jnp.where((row >= place) & (row < place + count), acc * view, 0.0)
        g = jnp.sum(acc, axis=0, keepdims=True)
        c, s, upper_sq, lower_sq = angle(g, upper_sq, lower_sq)
        coef_ref[step : step + 1, :] = c
        coef_ref[4 + step : 5 + step, :] = s
        if step < 3:
            shift_a, shift_b = pltpu.roll(a, count, 0), pltpu.roll(b, count, 0)
            a, b = jnp.where(row < count, c * a, s * shift_b), jnp.where(row < count, c * b, -s * shift_a)
            turn = (o[step] - o[step + 1]) & (W - 1)
            b = pltpu.roll(b, turn, 1)
            lower_sq = pltpu.roll(jnp.broadcast_to(lower_sq, (8, W)), turn, 1)[0:1]
    coef_ref[8:9, :] = upper_sq
    coef_ref[9:10, :] = pltpu.roll(jnp.broadcast_to(lower_sq, (8, W)), o[3] & (W - 1), 1)[0:1]


def halves(x):
    return [x[:, :H], x[:, H:]]


def turn_halves(x, amount):
    short = amount & (H - 1)
    lane = lax.broadcasted_iota(jnp.int32, (1, H), 1)
    cross = (lane < short) != ((amount & H) != 0)
    a, b = pltpu.roll(x[0], short, 1), pltpu.roll(x[1], short, 1)
    return [jnp.where(cross, b, a), jnp.where(cross, a, b)]


def rotate(upper, lower, coef, o):
    upper, lower = list(upper), turn_halves(lower, (-o[0]) & (W - 1))
    for step in range(4):
        for h in (0, 1):
            c = coef[step : step + 1, h * H : (h + 1) * H]
            s = coef[4 + step : 5 + step, h * H : (h + 1) * H]
            upper[h], lower[h] = c * upper[h] + s * lower[h], c * lower[h] - s * upper[h]
        turn = (o[step] - o[step + 1]) if step < 3 else o[3]
        lower = turn_halves(lower, turn & (W - 1))
    return upper, lower


SMEM = pl.BlockSpec(memory_space=pltpu.SMEM)
VMEM = pl.BlockSpec(memory_space=pltpu.VMEM)
ANY = pl.BlockSpec(memory_space=pl.ANY)
LAG_SHAPE = jax.ShapeDtypeStruct((LAGS, W), F32)
COEF_SHAPE = jax.ShapeDtypeStruct((16, W), F32)
ONEHOT_SHAPE = jax.ShapeDtypeStruct((LAGS, 2 * W), BF16)
TABLE = pltpu.VMEM((LAGS, H), jnp.int32)
LAG_SCRATCH = [pltpu.VMEM((LAGS, W), F32), pltpu.VMEM((WIDE, W), F32)]


def tile_rows(rows, most=512):
    r = most
    while rows % r:
        r //= 2
    return r


def block(rows):
    return jax.ShapeDtypeStruct((rows, W), F32)


def call(kernel, name, in_specs, out_specs, out_shape, scratch=(), us=1, limit=VMEM_LIMIT):
    return pl.pallas_call(
        kernel,
        name=name,
        in_specs=in_specs,
        out_specs=out_specs,
        out_shape=out_shape,
        scratch_shapes=list(scratch),
        compiler_params=pltpu.CompilerParams(vmem_limit_bytes=limit),
        cost_estimate=pl.CostEstimate(flops=us * 10**9, bytes_accessed=us * 3 * 10**6, transcendentals=0),
    )


def offsets_of(o_ref, round_index):
    return [o_ref[round_index, j] for j in range(4)]


def pick(flag, a, b):
    return jnp.where(flag, a, b), jnp.where(flag, b, a)


def pick_halves(flag, a, b):
    pairs = [pick(flag, x, y) for x, y in zip(a, b)]
    return [x for x, _ in pairs], [y for _, y in pairs]


def read(ref, rows):
    return [ref[rows, :H], ref[rows, H:]]


def write(ref, rows, x):
    ref[rows, :H] = x[0]
    ref[rows, H:] = x[1]


def first_kernel(
    o_hbm, rows_hbm, cols_hbm, upper_ref, lower_ref, lag_ref, rows_ref, cols_ref, table_ref, norm_ref, o_ref, sem
):
    count, feat = cols_ref.shape
    total = rows_ref.shape[0]
    r = tile_rows(total)
    tiles = total // r
    half = count // 2
    fetch_cols = [
        pltpu.make_async_copy(cols_hbm.at[pl.ds(k * half, half)], cols_ref.at[pl.ds(k * half, half)], sem.at[k])
        for k in range(2)
    ]
    fetch_rows = [
        pltpu.make_async_copy(rows_hbm.at[pl.ds(t * r, r)], rows_ref.at[pl.ds(t * r, r)], sem.at[2 + t])
        for t in range(tiles)
    ]
    fetch_o = pltpu.make_async_copy(o_hbm, o_ref, sem.at[15])
    for copy in [fetch_o] + fetch_cols + fetch_rows:
        copy.start()
    fetch_o.wait()
    o = offsets_of(o_ref, 0)
    onehot = build_onehot(o, table_ref)
    for copy in fetch_cols:
        copy.wait()
    for t in range(tiles):
        fetch_rows[t].wait()
        if t == 0:
            for k in range(0, count, H):
                wide = cols_ref[k : k + H].astype(F32)
                sums = jnp.sum(wide * wide, axis=1, keepdims=True)
                norm_ref[:, k : k + H] = jnp.transpose(jnp.broadcast_to(sums, (H, H)))[0:8]
        part = slice(t * r, (t + 1) * r)
        rows = rows_ref[part]
        cross = lax.dot_general(rows, cols_ref[...], NT, preferred_element_type=F32)
        wide = rows.astype(F32)
        row_norm = jnp.sum(wide * wide, axis=1, keepdims=True)
        kernel = jnp.exp(
            -(0.25 / math.sqrt(feat)) * (row_norm + norm_ref[0:1] - 2.0 * cross - 2.0 * feat)
        )
        upper_ref[part] = kernel[:, :W]
        lower_ref[part] = kernel[:, W:]
    lag_products(gram_whole(upper_ref[...], lower_ref[...]), onehot, lag_ref)


def first(offsets, row_feats, col_feats):
    rows, feat = row_feats.shape
    return call(
        first_kernel,
        "first",
        [ANY, ANY, ANY],
        (VMEM, VMEM, VMEM),
        (block(rows), block(rows), LAG_SHAPE),
        [
            pltpu.VMEM(row_feats.shape, BF16),
            pltpu.VMEM(col_feats.shape, BF16),
            TABLE,
            pltpu.VMEM((8, 2 * W), F32),
            pltpu.SMEM((3, 4), jnp.int32),
            pltpu.SemaphoreType.DMA((16,)),
        ],
        us=10,
        limit=FIRST_LIMIT,
    )(offsets, row_feats, col_feats)


def table_kernel(round_index, o_ref, after_ref, out_ref, table_ref):
    out_ref[...] = build_onehot(offsets_of(o_ref, round_index), table_ref)


def table(round_index, offsets, after):
    return call(
        functools.partial(table_kernel, round_index), "table%d" % round_index, [SMEM, ANY], VMEM, ONEHOT_SHAPE, [TABLE]
    )(offsets, after)


def by_parts(total, go):
    part = total // 2
    r = tile_rows(part, 384)
    for k in range(2):

        @pl.loop(0, part // r)
        def _(i):
            start = pl.multiple_of(i * r, r)
            go(pl.ds(pl.multiple_of(k * part + i * r, r), r), k, pl.ds(start, r))


def turn_first_kernel(o_ref, p_ref, mine_ref, other_ref, a_ref, b_ref, xa, xb, ya, yb, coef_ref, *lag_refs):
    p = p_ref[0]
    o = offsets_of(o_ref, 0)
    angles(mine_ref[...] + other_ref[...], o, coef_ref, *lag_refs)
    coef = coef_ref[...]
    keep = ((p & 1) == 1) | (p == 0)

    def go(rows, k, rows_part):
        upper, lower = rotate(read(a_ref, rows), read(b_ref, rows), coef, o)
        x, y = pick_halves(keep, upper, lower)
        write((xa, xb)[k], rows_part, x)
        write((ya, yb)[k], rows_part, y)

    by_parts(a_ref.shape[0], go)


def turn_first(offsets, p, mine, other, a, b):
    rows = a.shape[0]
    part = block(rows // 2)
    return call(
        turn_first_kernel,
        "turn0",
        [SMEM, SMEM] + [VMEM] * 4,
        (VMEM,) * 5,
        (part, part, part, part, COEF_SHAPE),
        LAG_SCRATCH,
        us=5,
    )(offsets, p, mine, other, a, b)


def pairs_start_kernel(p_ref, a_ref, b_ref, gram_ref):
    upper, lower = pick((p_ref[0] & 1) == 0, a_ref[...], b_ref[...])
    gram_ref[...] = gram_of(upper, lower)


def pairs_start(p, a, b):
    return call(
        pairs_start_kernel, "pairs0", [SMEM, VMEM, VMEM], VMEM, jax.ShapeDtypeStruct((2 * W, 2 * W), F32), us=3
    )(p, a, b)


def pairs_kernel(p_ref, hot_ref, gram_ref, a_ref, b_ref, lag_ref):
    upper, lower = pick((p_ref[0] & 1) == 0, a_ref[...], b_ref[...])
    lag_products(gram_ref[...] + gram_of(upper, lower), hot_ref[...], lag_ref)


def pairs(p, hot, gram, a, b):
    return call(
        pairs_kernel, "pairs1", [SMEM] + [VMEM] * 4, VMEM, LAG_SHAPE, us=4
    )(p, hot, gram, a, b)


def turn_second_kernel(o_ref, p_ref, coef_ref, rxa, rxb, sya, syb, za, zb, v_ref):
    p = p_ref[0]
    core = p & 1
    o = offsets_of(o_ref, 1)
    coef = coef_ref[...]

    def go(rows, k, rows_part):
        upper, lower = pick_halves(core == 0, read((rxa, rxb)[k], rows_part), read((sya, syb)[k], rows_part))
        upper, lower = rotate(upper, lower, coef, o)
        z, v = pick_halves((core == 0) & (p != 0), upper, lower)
        write((za, zb)[k], rows_part, z)
        write(v_ref, rows, v)

    by_parts(v_ref.shape[0], go)


def turn_second(offsets, p, coef, rxa, rxb, sya, syb):
    rows = rxa.shape[0] * 2
    part = block(rows // 2)
    return call(
        turn_second_kernel,
        "turn1",
        [SMEM, SMEM] + [VMEM] * 5,
        (VMEM,) * 3,
        (part, part, block(rows)),
        us=40,
    )(offsets, p, coef, rxa, rxb, sya, syb)


def side_kernel(last, o_ref, p_ref, hot_ref, coef_ref, sxa, sxb, rya, ryb, za, zb, q_ref, lag_ref):
    p = p_ref[0]
    core = p & 1
    o = offsets_of(o_ref, 1)
    coef = coef_ref[...]
    near_end = (p == 1) | (p == last - 1)
    part = za.shape[0]
    r = tile_rows(part, 384)
    parts, pending = None, None
    for t in range(2 * part // r + 1):
        ready, pending = pending, None
        if t < 2 * part // r:
            k = t * r // part
            rows = slice(t * r - k * part, t * r - k * part + r)
            upper, lower = pick_halves(
                (core == 0) != near_end, read((sxa, sxb)[k], rows), read((rya, ryb)[k], rows)
            )
            upper, lower = rotate(upper, lower, coef, o)
            wanted, _ = pick_halves((core == 1) | (p == last - 1), upper, lower)
            write(q_ref, slice(t * r, (t + 1) * r), wanted)
            pending = (za, zb)[k][rows], jnp.concatenate(wanted, axis=1)
        if ready is not None:
            added = gram_of(*pick(core == 0, *ready))
            parts = added if parts is None else parts + added
    lag_products(parts, hot_ref[...], lag_ref)


def side(last, offsets, p, hot, coef, sxa, sxb, rya, ryb, za, zb):
    return call(
        functools.partial(side_kernel, last),
        "side",
        [SMEM, SMEM] + [VMEM] * 8,
        (VMEM, VMEM),
        (block(2 * za.shape[0]), LAG_SHAPE),
        us=8,
    )(offsets, p, hot, coef, sxa, sxb, rya, ryb, za, zb)


def solve_kernel(round_index, o_ref, mine_ref, other_ref, coef_ref, *lag_refs):
    angles(mine_ref[...] + other_ref[...], offsets_of(o_ref, round_index), coef_ref, *lag_refs)


def solve(round_index, offsets, mine, other):
    return call(
        functools.partial(solve_kernel, round_index),
        "solve%d" % round_index,
        [SMEM] + [VMEM] * 2,
        VMEM,
        COEF_SHAPE,
        LAG_SCRATCH,
        us=2,
    )(offsets, mine, other)


def own_kernel(o_ref, p_ref, coef_ref, za, zb, q_ref, out_ref):
    p = p_ref[0]
    core = p & 1
    o = offsets_of(o_ref, 2)
    coef = coef_ref[...]

    def go(rows, k, rows_part):
        upper, lower = pick_halves(core == 0, read((za, zb)[k], rows_part), read(q_ref, rows))
        upper, lower = rotate(upper, lower, coef, o)
        wanted, _ = pick_halves((core == 1) & (p != 1), upper, lower)
        write(out_ref, rows, [x * x for x in wanted])

    by_parts(q_ref.shape[0], go)


def own(offsets, p, coef, za, zb, q):
    return call(own_kernel, "own", [SMEM, SMEM] + [VMEM] * 4, VMEM, block(q.shape[0]), us=40)(
        offsets, p, coef, za, zb, q
    )


def finish_kernel(
    last, row_total, o_ref, p_ref, coef_ref, a_ref, b_ref, c_ref, own_ref, ra, rb, v_ref, out_hbm, norm_ref, e_ref, sem
):
    p = p_ref[0]
    core = p & 1
    o = offsets_of(o_ref, 2)
    keep = pltpu.make_async_copy(own_ref, out_hbm.at[1 - core], sem.at[0])
    keep.start()
    coef = coef_ref[...]
    for k, ref in enumerate((a_ref, b_ref, c_ref)):
        norm_ref[k] = ref[8:10, :] / row_total
    part = ra.shape[0]
    r = tile_rows(part, 384)
    tiles = part // r
    sends = []
    for t in range(2 * tiles):
        rows = pl.ds(t * r, r)
        swap = (p == 0) | (p == last)
        upper, lower = pick_halves((core == 0) != swap, read((ra, rb)[t // tiles], pl.ds(t % tiles * r, r)), read(v_ref, rows))
        upper, lower = rotate(upper, lower, coef, o)
        wanted, _ = pick_halves((core == 0) | (p == last), upper, lower)
        write(e_ref, rows, [x * x for x in wanted])
        copy = pltpu.make_async_copy(e_ref.at[rows], out_hbm.at[core, rows], sem.at[1 + t])
        copy.start()
        sends.append(copy)
    for copy in [keep] + sends:
        copy.wait()


def finish(last, row_total, offsets, p, coef, coefs, own_block, ra, rb, v):
    rows = v.shape[0]
    return call(
        functools.partial(finish_kernel, last, row_total),
        "finish",
        [SMEM, SMEM] + [VMEM] * 8,
        (ANY, VMEM),
        (jax.ShapeDtypeStruct((2, rows, W), F32), jax.ShapeDtypeStruct((3, 2, W), F32)),
        [pltpu.VMEM((rows, W), F32), pltpu.SemaphoreType.DMA((16,))],
        us=5,
    )(offsets, p, coef, *coefs, own_block, ra, rb, v)


def body(row_feats, col_feats, offsets):
    n = lax.axis_size("blk")
    chips = n // 2
    p = lax.axis_index("blk").astype(jnp.int32).reshape(1)
    row_total = row_feats.shape[0] * lax.axis_size("row")
    across = [(0, 1), (1, 0)]
    sibling = [(i, i ^ 1) for i in range(n)]
    meet = [(2 * j + 1, 2 * j + 2) for j in range(chips - 1)] + [(2 * j, 2 * j - 1) for j in range(1, chips)]
    meet += [(0, 0), (n - 1, n - 1)]
    lend = [(2 * j, 2 * j + 3) for j in range(chips - 1)] + [(2 * j + 1, 2 * j - 2) for j in range(1, chips)]
    lend += [(1, 1), (n - 2, n - 2)]
    deal = [(2 * j, 2 * j + 2) for j in range(chips - 1)] + [(2 * j + 1, 2 * j - 1) for j in range(1, chips)]
    deal += [(1, 0), (n - 2, n - 1)]
    tell = [(2 * j, 2 * j - 2) for j in range(1, chips)] + [(2 * j + 1, 2 * j + 3) for j in range(chips - 1)]
    tell += [(0, 1), (n - 1, n - 2)]

    upper, lower, lag = first(offsets, row_feats, col_feats)
    lag_other = lax.ppermute(lag, "row", across)
    xa, xb, ya, yb, coef_a = turn_first(offsets, p, lag, lag_other, upper, lower)
    hot = table(1, offsets, coef_a)
    rxa = lax.ppermute(xa, "blk", meet)
    rxb = lax.ppermute(xb, "blk", meet)
    sya = lax.ppermute(ya, "blk", sibling)
    syb = lax.ppermute(yb, "blk", sibling)
    sxa = lax.ppermute(xa, "blk", sibling)
    sxb = lax.ppermute(xb, "blk", sibling)
    gram = pairs_start(p, rxa, sya)
    ya, gram = lax.optimization_barrier((ya, gram))
    rya = lax.ppermute(ya, "blk", lend)
    lag = pairs(p, hot, gram, rxb, syb)
    lag_other = lax.ppermute(lag, "row", across)
    hot = table(2, offsets, lag)
    yb, hot = lax.optimization_barrier((yb, hot))
    ryb = lax.ppermute(yb, "blk", lend)
    coef_b = solve(1, offsets, lag, lag_other)
    rxa, rya, sxa, sxb = lax.optimization_barrier((rxa, rya, sxa, sxb))
    za, zb, v = turn_second(offsets, p, coef_b, rxa, rxb, sya, syb)
    ra = lax.ppermute(za, "blk", deal)
    told, za = lax.optimization_barrier((coef_b, za))
    coef_side = lax.ppermute(told, "blk", tell)
    q, lag = side(n - 1, offsets, p, hot, coef_side, sxa, sxb, rya, ryb, za, zb)
    lag_other = lax.ppermute(lag, "row", across)
    later, _ = lax.optimization_barrier((zb, lag))
    rb = lax.ppermute(later, "blk", deal)
    coef_c = solve(2, offsets, lag, lag_other)
    coef_got = lax.ppermute(coef_c, "blk", deal)
    coef_own, ra = lax.optimization_barrier((coef_c, ra))
    own_block = own(offsets, p, coef_own, za, zb, q)
    coef_c, own_block = lax.optimization_barrier((coef_c, own_block))
    coef_norm = lax.ppermute(coef_c, "blk", sibling)
    return finish(n - 1, row_total, offsets, p, coef_got, (coef_a, coef_b, coef_norm), own_block, ra, rb, v)


def solution(mesh):
    return jax.shard_map(
        body,
        mesh=mesh,
        in_specs=(P("row", None), P("blk", None), P()),
        out_specs=(P(None, "row", "blk"), P(None, None, "blk")),
        check_vma=False,
    )
```

```python
import functools
import math

import jax
import jax.numpy as jnp
from jax import lax
from jax.experimental import pallas as pl
from jax.experimental.pallas import tpu as pltpu
from jax.sharding import PartitionSpec as P

F32 = jnp.float32
BF16 = jnp.bfloat16
W = 256
H = 128
LAGS = 56
WIDE = 96
VMEM_LIMIT = 24 * 1024 * 1024
FIRST_LIMIT = 50 * 1024 * 1024


def group_rows(m):
    return (16 * m, 16) if m < 4 else (64 + 8 * (m - 4), 8)


def lag_plan():
    unit = [tuple(int(i == j) for j in range(4)) for i in range(4)]
    zero = (0, 0, 0, 0)

    def plus(a, b, sign=1):
        return tuple(x + sign * y for x, y in zip(a, b))

    t, s = [zero], [zero]
    first, second = [0], [1]
    wide = {15: (0, 0, zero), 30: (1, 1, zero)}
    for step in range(4):
        count = 1 << step
        for m in range(count):
            start, _ = group_rows(m)
            place = {3: 0, 2: 8, 1: 12, 0: 14}[step]
            for n in range(count):
                lag = plus(plus(unit[step], s[n]), t[m], -1)
                wide[start + place + n] = (first[m], second[n], lag)
        if step < 3:
            t, s = t + [plus(x, unit[step]) for x in s], s + [plus(x, unit[step], -1) for x in t]
            first, second = first + second, second + first
    table = sorted(set(wide.values()))
    return table, {r: table.index(key) for r, key in wide.items()}, t


TABLE_ROWS, USES, BASES = lag_plan()
UPPER_ROWS = sum(1 for row in TABLE_ROWS if row[0] == 0)


def shift_of(coefs, o):
    total = 0
    for k, value in zip(coefs, o):
        total = total + k * value if k else total
    return total & (W - 1)


def split(x):
    hi = x.astype(BF16)
    return hi, (x - hi.astype(F32)).astype(BF16)


TN = (((0,), (0,)), ((), ()))
NT = (((1,), (1,)), ((), ()))


def skew(x):
    row = lax.broadcasted_iota(jnp.int32, (W, W), 0)
    for bit in (1, 2, 4):
        x = jnp.where((row & bit) != 0, pltpu.roll(x, W - bit, 1), x)
    tiles = [pltpu.roll(x[8 * t : 8 * t + 8], (W - 8 * t) % W, 1) for t in range(W // 8)]
    return jnp.concatenate(tiles, axis=0)


def build_onehot(o, table_ref):
    table_ref[...] = jnp.full((LAGS, H), -1, jnp.int32)
    for r, (_, side, lag) in enumerate(TABLE_ROWS):
        table_ref[r : r + 1, :] = jnp.full((1, H), shift_of(lag, o) + W * side, jnp.int32)
    table = jnp.concatenate([table_ref[...]] * 4, axis=1)
    return (table == lax.broadcasted_iota(jnp.int32, (LAGS, 2 * W), 1)).astype(F32).astype(BF16)


def lag_products(gram, onehot, out_ref):
    diags = []
    for kind in (0, 1):
        sheets = [skew(gram[kind * W : (kind + 1) * W, side * W : (side + 1) * W]) for side in (0, 1)]
        hi, lo = split(jnp.concatenate(sheets, axis=1))
        diags.append(
            lax.dot_general(onehot, lo, NT, preferred_element_type=F32)
            + lax.dot_general(onehot, hi, NT, preferred_element_type=F32)
        )
    row = lax.broadcasted_iota(jnp.int32, (LAGS, W), 0)
    out_ref[...] = jnp.where(row < UPPER_ROWS, diags[0], diags[1])


def gram_of(a, b):
    hi, lo = split(jnp.concatenate([a, b], axis=1))
    return (
        lax.dot_general(hi, lo, TN, preferred_element_type=F32)
        + lax.dot_general(lo, hi, TN, preferred_element_type=F32)
        + lax.dot_general(hi, hi, TN, preferred_element_type=F32)
    )


def gram_whole(a, b):
    hi, lo = split(jnp.concatenate([a, b], axis=1))
    parts = lax.dot_general(hi, jnp.concatenate([hi, lo], axis=1), TN, preferred_element_type=F32)
    mixed = parts[:, 2 * W :]
    return parts[:, : 2 * W] + (mixed + jnp.transpose(mixed))


def angle(g, upper_sq, lower_sq):
    twice = 2.0 * g
    diff = upper_sq - lower_sq
    scale = jnp.maximum(jnp.abs(twice), jnp.abs(diff))
    live = scale > 0.0
    safe = jnp.where(live, scale, 1.0)
    x = jnp.where(live, diff / safe, 1.0)
    y = jnp.where(live, twice / safe, 0.0)
    r = jnp.sqrt(x * x + y * y)
    big = jnp.sqrt(0.5 * (1.0 + jnp.abs(x) / r))
    small = 0.5 * jnp.abs(y) / (r * big)
    wide = x < 0.0
    c = jnp.where(wide, small, big)
    s = jnp.where(wide, big, small)
    s = jnp.where(y < 0.0, -s, s)
    cross = twice * c * s
    return c, s, c * c * upper_sq + cross + s * s * lower_sq, s * s * upper_sq - cross + c * c * lower_sq


def angles(lags, o, coef_ref, sum_ref, wide_ref):
    sum_ref[...] = lags
    for r, place in USES.items():
        wide_ref[r : r + 1, :] = sum_ref[place : place + 1, :]
    tiles, last = [], []
    for m in range(8):
        start, count = group_rows(m)
        tile = wide_ref[start : start + count, :]
        if m > 0:
            tile = pltpu.roll(tile, (-shift_of(BASES[m], o)) & (W - 1), 1)
        last.append(tile[0:8])
        if m < 4:
            tiles.append(tile[8:16])
    row = lax.broadcasted_iota(jnp.int32, (8, W), 0)
    a = jnp.ones((8, W), F32)
    b = jnp.ones((8, W), F32)
    upper_sq = tiles[0][7:8]
    lower_sq = tiles[1][6:7]
    for step in range(4):
        count = 1 << step
        if step == 3:
            parts, place = last, 0
        else:
            parts, place = tiles[:count], (6, 4, 0)[step]
        acc = None
        for m in range(count):
            term = a[m : m + 1] * parts[m]
            acc = term if acc is None else acc + term
        view = pltpu.roll(b, place, 0) if place else b
        acc = jnp.where((row >= place) & (row < place + count), acc * view, 0.0)
        g = jnp.sum(acc, axis=0, keepdims=True)
        c, s, upper_sq, lower_sq = angle(g, upper_sq, lower_sq)
        coef_ref[step : step + 1, :] = c
        coef_ref[4 + step : 5 + step, :] = s
        if step < 3:
            shift_a, shift_b = pltpu.roll(a, count, 0), pltpu.roll(b, count, 0)
            a, b = jnp.where(row < count, c * a, s * shift_b), jnp.where(row < count, c * b, -s * shift_a)
            turn = (o[step] - o[step + 1]) & (W - 1)
            b = pltpu.roll(b, turn, 1)
            lower_sq = pltpu.roll(jnp.broadcast_to(lower_sq, (8, W)), turn, 1)[0:1]
    coef_ref[8:9, :] = upper_sq
    coef_ref[9:10, :] = pltpu.roll(jnp.broadcast_to(lower_sq, (8, W)), o[3] & (W - 1), 1)[0:1]


def halves(x):
    return [x[:, :H], x[:, H:]]


def turn_halves(x, amount):
    short = amount & (H - 1)
    lane = lax.broadcasted_iota(jnp.int32, (1, H), 1)
    cross = (lane < short) != ((amount & H) != 0)
    a, b = pltpu.roll(x[0], short, 1), pltpu.roll(x[1], short, 1)
    return [jnp.where(cross, b, a), jnp.where(cross, a, b)]


def rotate(upper, lower, coef, o):
    upper, lower = list(upper), turn_halves(lower, (-o[0]) & (W - 1))
    for step in range(4):
        for h in (0, 1):
            c = coef[step : step + 1, h * H : (h + 1) * H]
            s = coef[4 + step : 5 + step, h * H : (h + 1) * H]
            upper[h], lower[h] = c * upper[h] + s * lower[h], c * lower[h] - s * upper[h]
        turn = (o[step] - o[step + 1]) if step < 3 else o[3]
        lower = turn_halves(lower, turn & (W - 1))
    return upper, lower


SMEM = pl.BlockSpec(memory_space=pltpu.SMEM)
VMEM = pl.BlockSpec(memory_space=pltpu.VMEM)
ANY = pl.BlockSpec(memory_space=pl.ANY)
LAG_SHAPE = jax.ShapeDtypeStruct((LAGS, W), F32)
COEF_SHAPE = jax.ShapeDtypeStruct((16, W), F32)
ONEHOT_SHAPE = jax.ShapeDtypeStruct((LAGS, 2 * W), BF16)
TABLE = pltpu.VMEM((LAGS, H), jnp.int32)
LAG_SCRATCH = [pltpu.VMEM((LAGS, W), F32), pltpu.VMEM((WIDE, W), F32)]


def tile_rows(rows, most=512):
    r = most
    while rows % r:
        r //= 2
    return r


def block(rows):
    return jax.ShapeDtypeStruct((rows, W), F32)


def call(kernel, name, in_specs, out_specs, out_shape, scratch=(), us=1, limit=VMEM_LIMIT):
    return pl.pallas_call(
        kernel,
        name=name,
        in_specs=in_specs,
        out_specs=out_specs,
        out_shape=out_shape,
        scratch_shapes=list(scratch),
        compiler_params=pltpu.CompilerParams(vmem_limit_bytes=limit),
        cost_estimate=pl.CostEstimate(flops=us * 10**9, bytes_accessed=us * 3 * 10**6, transcendentals=0),
    )


def offsets_of(o_ref, round_index):
    return [o_ref[round_index, j] for j in range(4)]


def pick(flag, a, b):
    return jnp.where(flag, a, b), jnp.where(flag, b, a)


def pick_halves(flag, a, b):
    pairs = [pick(flag, x, y) for x, y in zip(a, b)]
    return [x for x, _ in pairs], [y for _, y in pairs]


def read(ref, rows):
    return [ref[rows, :H], ref[rows, H:]]


def write(ref, rows, x):
    ref[rows, :H] = x[0]
    ref[rows, H:] = x[1]


def first_kernel(
    o_hbm, rows_hbm, cols_hbm, upper_ref, lower_ref, lag_ref, rows_ref, cols_ref, turned_ref, table_ref, norm_ref, o_ref, sem
):
    count, feat = cols_ref.shape
    total = rows_ref.shape[0]
    r = tile_rows(total)
    tiles = total // r
    half = count // 2
    fetch_cols = [
        pltpu.make_async_copy(cols_hbm.at[pl.ds(k * half, half)], cols_ref.at[pl.ds(k * half, half)], sem.at[k])
        for k in range(2)
    ]
    fetch_rows = [
        pltpu.make_async_copy(rows_hbm.at[pl.ds(t * r, r)], rows_ref.at[pl.ds(t * r, r)], sem.at[2 + t])
        for t in range(tiles)
    ]
    fetch_o = pltpu.make_async_copy(o_hbm, o_ref, sem.at[15])
    for copy in [fetch_o] + fetch_cols + fetch_rows:
        copy.start()
    fetch_o.wait()
    o = offsets_of(o_ref, 0)
    onehot = build_onehot(o, table_ref)
    for copy in fetch_cols:
        copy.wait()
    turned_ref[...] = jnp.transpose(cols_ref[...])
    for t in range(tiles):
        fetch_rows[t].wait()
        if t == 0:
            for k in range(0, count, H):
                wide = cols_ref[k : k + H].astype(F32)
                sums = jnp.sum(wide * wide, axis=1, keepdims=True)
                norm_ref[:, k : k + H] = jnp.transpose(jnp.broadcast_to(sums, (H, H)))[0:8]
        part = slice(t * r, (t + 1) * r)
        rows = rows_ref[part]
        cross = jnp.dot(rows, turned_ref[...], preferred_element_type=F32)
        wide = rows.astype(F32)
        row_norm = jnp.sum(wide * wide, axis=1, keepdims=True)
        kernel = jnp.exp(
            -(0.25 / math.sqrt(feat)) * (row_norm + norm_ref[0:1] - 2.0 * cross - 2.0 * feat)
        )
        upper_ref[part] = kernel[:, :W]
        lower_ref[part] = kernel[:, W:]
    lag_products(gram_whole(upper_ref[...], lower_ref[...]), onehot, lag_ref)


def first(offsets, row_feats, col_feats):
    rows, feat = row_feats.shape
    return call(
        first_kernel,
        "first",
        [ANY, ANY, ANY],
        (VMEM, VMEM, VMEM),
        (block(rows), block(rows), LAG_SHAPE),
        [
            pltpu.VMEM(row_feats.shape, BF16),
            pltpu.VMEM(col_feats.shape, BF16),
            pltpu.VMEM(col_feats.shape[::-1], BF16),
            TABLE,
            pltpu.VMEM((8, 2 * W), F32),
            pltpu.SMEM((3, 4), jnp.int32),
            pltpu.SemaphoreType.DMA((16,)),
        ],
        us=10,
        limit=FIRST_LIMIT,
    )(offsets, row_feats, col_feats)


def table_kernel(round_index, o_ref, after_ref, out_ref, table_ref):
    out_ref[...] = build_onehot(offsets_of(o_ref, round_index), table_ref)


def table(round_index, offsets, after):
    return call(
        functools.partial(table_kernel, round_index), "table%d" % round_index, [SMEM, ANY], VMEM, ONEHOT_SHAPE, [TABLE]
    )(offsets, after)


def by_parts(total, go):
    part = total // 2
    r = tile_rows(part, 384)
    for k in range(2):

        @pl.loop(0, part // r)
        def _(i):
            start = pl.multiple_of(i * r, r)
            go(pl.ds(pl.multiple_of(k * part + i * r, r), r), k, pl.ds(start, r))


def turn_first_kernel(o_ref, p_ref, mine_ref, other_ref, a_ref, b_ref, xa, xb, ya, yb, coef_ref, *lag_refs):
    p = p_ref[0]
    o = offsets_of(o_ref, 0)
    angles(mine_ref[...] + other_ref[...], o, coef_ref, *lag_refs)
    coef = coef_ref[...]
    keep = ((p & 1) == 1) | (p == 0)

    def go(rows, k, rows_part):
        upper, lower = rotate(read(a_ref, rows), read(b_ref, rows), coef, o)
        x, y = pick_halves(keep, upper, lower)
        write((xa, xb)[k], rows_part, x)
        write((ya, yb)[k], rows_part, y)

    by_parts(a_ref.shape[0], go)


def turn_first(offsets, p, mine, other, a, b):
    rows = a.shape[0]
    part = block(rows // 2)
    return call(
        turn_first_kernel,
        "turn0",
        [SMEM, SMEM] + [VMEM] * 4,
        (VMEM,) * 5,
        (part, part, part, part, COEF_SHAPE),
        LAG_SCRATCH,
        us=5,
    )(offsets, p, mine, other, a, b)


def pairs_start_kernel(p_ref, a_ref, b_ref, gram_ref):
    upper, lower = pick((p_ref[0] & 1) == 0, a_ref[...], b_ref[...])
    gram_ref[...] = gram_of(upper, lower)


def pairs_start(p, a, b):
    return call(
        pairs_start_kernel, "pairs0", [SMEM, VMEM, VMEM], VMEM, jax.ShapeDtypeStruct((2 * W, 2 * W), F32), us=3
    )(p, a, b)


def pairs_kernel(p_ref, hot_ref, gram_ref, a_ref, b_ref, lag_ref):
    upper, lower = pick((p_ref[0] & 1) == 0, a_ref[...], b_ref[...])
    lag_products(gram_ref[...] + gram_of(upper, lower), hot_ref[...], lag_ref)


def pairs(p, hot, gram, a, b):
    return call(
        pairs_kernel, "pairs1", [SMEM] + [VMEM] * 4, VMEM, LAG_SHAPE, us=4
    )(p, hot, gram, a, b)


def turn_second_kernel(o_ref, p_ref, coef_ref, rxa, rxb, sya, syb, za, zb, v_ref):
    p = p_ref[0]
    core = p & 1
    o = offsets_of(o_ref, 1)
    coef = coef_ref[...]

    def go(rows, k, rows_part):
        upper, lower = pick_halves(core == 0, read((rxa, rxb)[k], rows_part), read((sya, syb)[k], rows_part))
        upper, lower = rotate(upper, lower, coef, o)
        z, v = pick_halves((core == 0) & (p != 0), upper, lower)
        write((za, zb)[k], rows_part, z)
        write(v_ref, rows, v)

    by_parts(v_ref.shape[0], go)


def turn_second(offsets, p, coef, rxa, rxb, sya, syb):
    rows = rxa.shape[0] * 2
    part = block(rows // 2)
    return call(
        turn_second_kernel,
        "turn1",
        [SMEM, SMEM] + [VMEM] * 5,
        (VMEM,) * 3,
        (part, part, block(rows)),
        us=40,
    )(offsets, p, coef, rxa, rxb, sya, syb)


def side_kernel(last, o_ref, p_ref, hot_ref, coef_ref, sxa, sxb, rya, ryb, za, zb, q_ref, lag_ref):
    p = p_ref[0]
    core = p & 1
    o = offsets_of(o_ref, 1)
    coef = coef_ref[...]
    near_end = (p == 1) | (p == last - 1)
    part = za.shape[0]
    r = tile_rows(part, 384)
    parts, pending = None, None
    for t in range(2 * part // r + 1):
        ready, pending = pending, None
        if t < 2 * part // r:
            k = t * r // part
            rows = slice(t * r - k * part, t * r - k * part + r)
            upper, lower = pick_halves(
                (core == 0) != near_end, read((sxa, sxb)[k], rows), read((rya, ryb)[k], rows)
            )
            upper, lower = rotate(upper, lower, coef, o)
            wanted, _ = pick_halves((core == 1) | (p == last - 1), upper, lower)
            write(q_ref, slice(t * r, (t + 1) * r), wanted)
            pending = (za, zb)[k][rows], jnp.concatenate(wanted, axis=1)
        if ready is not None:
            added = gram_of(*pick(core == 0, *ready))
            parts = added if parts is None else parts + added
    lag_products(parts, hot_ref[...], lag_ref)


def side(last, offsets, p, hot, coef, sxa, sxb, rya, ryb, za, zb):
    return call(
        functools.partial(side_kernel, last),
        "side",
        [SMEM, SMEM] + [VMEM] * 8,
        (VMEM, VMEM),
        (block(2 * za.shape[0]), LAG_SHAPE),
        us=8,
    )(offsets, p, hot, coef, sxa, sxb, rya, ryb, za, zb)


def solve_kernel(round_index, o_ref, mine_ref, other_ref, coef_ref, *lag_refs):
    angles(mine_ref[...] + other_ref[...], offsets_of(o_ref, round_index), coef_ref, *lag_refs)


def solve(round_index, offsets, mine, other):
    return call(
        functools.partial(solve_kernel, round_index),
        "solve%d" % round_index,
        [SMEM] + [VMEM] * 2,
        VMEM,
        COEF_SHAPE,
        LAG_SCRATCH,
        us=2,
    )(offsets, mine, other)


def own_kernel(o_ref, p_ref, coef_ref, za, zb, q_ref, out_ref):
    p = p_ref[0]
    core = p & 1
    o = offsets_of(o_ref, 2)
    coef = coef_ref[...]

    def go(rows, k, rows_part):
        upper, lower = pick_halves(core == 0, read((za, zb)[k], rows_part), read(q_ref, rows))
        upper, lower = rotate(upper, lower, coef, o)
        wanted, _ = pick_halves((core == 1) & (p != 1), upper, lower)
        write(out_ref, rows, [x * x for x in wanted])

    by_parts(q_ref.shape[0], go)


def own(offsets, p, coef, za, zb, q):
    return call(own_kernel, "own", [SMEM, SMEM] + [VMEM] * 4, VMEM, block(q.shape[0]), us=40)(
        offsets, p, coef, za, zb, q
    )


def finish_kernel(
    last, row_total, o_ref, p_ref, coef_ref, a_ref, b_ref, c_ref, own_ref, ra, rb, v_ref, out_hbm, norm_ref, e_ref, sem
):
    p = p_ref[0]
    core = p & 1
    o = offsets_of(o_ref, 2)
    keep = pltpu.make_async_copy(own_ref, out_hbm.at[1 - core], sem.at[0])
    keep.start()
    coef = coef_ref[...]
    for k, ref in enumerate((a_ref, b_ref, c_ref)):
        norm_ref[k] = ref[8:10, :] / row_total
    part = ra.shape[0]
    r = tile_rows(part, 384)
    tiles = part // r
    sends = []
    for t in range(2 * tiles):
        rows = pl.ds(t * r, r)
        swap = (p == 0) | (p == last)
        upper, lower = pick_halves((core == 0) != swap, read((ra, rb)[t // tiles], pl.ds(t % tiles * r, r)), read(v_ref, rows))
        upper, lower = rotate(upper, lower, coef, o)
        wanted, _ = pick_halves((core == 0) | (p == last), upper, lower)
        write(e_ref, rows, [x * x for x in wanted])
        copy = pltpu.make_async_copy(e_ref.at[rows], out_hbm.at[core, rows], sem.at[1 + t])
        copy.start()
        sends.append(copy)
    for copy in [keep] + sends:
        copy.wait()


def finish(last, row_total, offsets, p, coef, coefs, own_block, ra, rb, v):
    rows = v.shape[0]
    return call(
        functools.partial(finish_kernel, last, row_total),
        "finish",
        [SMEM, SMEM] + [VMEM] * 8,
        (ANY, VMEM),
        (jax.ShapeDtypeStruct((2, rows, W), F32), jax.ShapeDtypeStruct((3, 2, W), F32)),
        [pltpu.VMEM((rows, W), F32), pltpu.SemaphoreType.DMA((16,))],
        us=5,
    )(offsets, p, coef, *coefs, own_block, ra, rb, v)


def body(row_feats, col_feats, offsets):
    n = lax.axis_size("blk")
    chips = n // 2
    p = lax.axis_index("blk").astype(jnp.int32).reshape(1)
    row_total = row_feats.shape[0] * lax.axis_size("row")
    across = [(0, 1), (1, 0)]
    sibling = [(i, i ^ 1) for i in range(n)]
    meet = [(2 * j + 1, 2 * j + 2) for j in range(chips - 1)] + [(2 * j, 2 * j - 1) for j in range(1, chips)]
    meet += [(0, 0), (n - 1, n - 1)]
    lend = [(2 * j, 2 * j + 3) for j in range(chips - 1)] + [(2 * j + 1, 2 * j - 2) for j in range(1, chips)]
    lend += [(1, 1), (n - 2, n - 2)]
    deal = [(2 * j, 2 * j + 2) for j in range(chips - 1)] + [(2 * j + 1, 2 * j - 1) for j in range(1, chips)]
    deal += [(1, 0), (n - 2, n - 1)]
    tell = [(2 * j, 2 * j - 2) for j in range(1, chips)] + [(2 * j + 1, 2 * j + 3) for j in range(chips - 1)]
    tell += [(0, 1), (n - 1, n - 2)]

    upper, lower, lag = first(offsets, row_feats, col_feats)
    lag_other = lax.ppermute(lag, "row", across)
    xa, xb, ya, yb, coef_a = turn_first(offsets, p, lag, lag_other, upper, lower)
    hot = table(1, offsets, coef_a)
    rxa = lax.ppermute(xa, "blk", meet)
    rxb = lax.ppermute(xb, "blk", meet)
    sya = lax.ppermute(ya, "blk", sibling)
    syb = lax.ppermute(yb, "blk", sibling)
    sxa = lax.ppermute(xa, "blk", sibling)
    sxb = lax.ppermute(xb, "blk", sibling)
    gram = pairs_start(p, rxa, sya)
    ya, gram = lax.optimization_barrier((ya, gram))
    rya = lax.ppermute(ya, "blk", lend)
    lag = pairs(p, hot, gram, rxb, syb)
    lag_other = lax.ppermute(lag, "row", across)
    hot = table(2, offsets, lag)
    yb, hot = lax.optimization_barrier((yb, hot))
    ryb = lax.ppermute(yb, "blk", lend)
    coef_b = solve(1, offsets, lag, lag_other)
    coef_side = lax.ppermute(coef_b, "blk", tell)
    rxa, rya, sxa, sxb = lax.optimization_barrier((rxa, rya, sxa, sxb))
    za, zb, v = turn_second(offsets, p, coef_b, rxa, rxb, sya, syb)
    za, zb, coef_side = lax.optimization_barrier((za, zb, coef_side))
    ra = lax.ppermute(za, "blk", deal)
    q, lag = side(n - 1, offsets, p, hot, coef_side, sxa, sxb, rya, ryb, za, zb)
    lag_other = lax.ppermute(lag, "row", across)
    later, _ = lax.optimization_barrier((zb, lag))
    rb = lax.ppermute(later, "blk", deal)
    coef_c = solve(2, offsets, lag, lag_other)
    coef_got = lax.ppermute(coef_c, "blk", deal)
    coef_own, ra = lax.optimization_barrier((coef_c, ra))
    own_block = own(offsets, p, coef_own, za, zb, q)
    coef_c, own_block = lax.optimization_barrier((coef_c, own_block))
    coef_norm = lax.ppermute(coef_c, "blk", sibling)
    return finish(n - 1, row_total, offsets, p, coef_got, (coef_a, coef_b, coef_norm), own_block, ra, rb, v)


def solution(mesh):
    return jax.shard_map(
        body,
        mesh=mesh,
        in_specs=(P("row", None), P("blk", None), P()),
        out_specs=(P(None, "row", "blk"), P(None, None, "blk")),
        check_vma=False,
    )
```
